128 devices in a mesh: dp: 16 (over z, x_lo, core), tensor: 8 (over x_hi, y).
Axes of the slice: x: 4 (x_hi: 2, x_lo: 2; x = x_hi * 2 + x_lo), y: 4, z: 4, core: 2. Of those that a mesh axis runs over, the one named last changes fastest.
Arguments:
- layer_input: bfloat16 [5120, 2048], P('dp'), may hold values from -4.5 to 4.5
- doc_lengths: int32 [4], replicated, may hold values from 1 to 4800, as said below
- expert_ids: int32 [5120, 4], P('dp'), may hold values from 0 to 15, all different within a row; in each aligned block of 320 rows (0 to 319, 320 to 639, ...) at most 110 rows name the same one
- attn_gain: float32 [2048], replicated, may hold values from 0.1 to 1.9
- qkv_weight: bfloat16 [2048, 3, 16, 128], P(None, None, 'tensor'), may hold values from -0.125 to 0.125
- qkv_bias: bfloat16 [3, 16, 128], P(None, 'tensor'), may hold values from -3 to 3
- out_weight: bfloat16 [16, 128, 2048], P('tensor'), may hold values from -0.5 to 0.5
- ffn_gain: float32 [2048], replicated, may hold values from 0.1 to 1.9
- router_weight: bfloat16 [2048, 16], replicated, may hold values from -0.0625 to 0.0625
- shared_gate: bfloat16 [2048], replicated, may hold values from -0.125 to 0.125
- shared_in: bfloat16 [2048, 2, 5632], P(None, None, 'tensor'), may hold values from -0.125 to 0.125
- shared_out: bfloat16 [5632, 2048], P('tensor'), may hold values from -0.3125 to 0.3125
- expert_in: bfloat16 [16, 2048, 2, 1408], P('dp', None, None, 'tensor'), may hold values from -0.125 to 0.125
- expert_out: bfloat16 [16, 1408, 2048], P('dp', 'tensor'), may hold values from -1.25 to 1.25
- cotangent: bfloat16 [5120, 2048], P('dp'), may hold values from -6 to 6
Outputs:
- layer_output: bfloat16 [5120, 2048], P('dp')
- input_grad: float32 [5120, 2048], P('dp')
- qkv_grad: float32 [2048, 3, 16, 128], P('dp', None, 'tensor')
- bias_grad: float32 [3, 16, 128], P(None, 'tensor', 'dp')
- outproj_grad: float32 [16, 128, 2048], P('tensor', None, 'dp')
- attn_gain_grad: float32 [2048], P('dp')
- ffn_gain_grad: float32 [2048], P('dp')
- router_grad: float32 [2048, 16], P('dp')
- shared_gate_grad: float32 [2048], P('dp')
- shared_in_grad: float32 [2048, 2, 5632], P('dp', None, 'tensor')
- shared_out_grad: float32 [5632, 2048], P('tensor', 'dp')
- expert_in_grad: float32 [16, 2048, 2, 1408], P('dp', None, None, 'tensor')
- expert_out_grad: float32 [16, 1408, 2048], P('dp', 'tensor')
- rms_stats: float32 [5], replicated
The draws below stay inside these ranges and needn't reach their ends.
Inputs may be any that keep to these rules, and one draw needn't show every extreme that they name: `doc_lengths`: positive lengths that add up to 5120; one of the two middle documents has exactly 4800 tokens, beginning within the first 320 tokens and ending within the last 320. `expert_ids`: the tokens of one group name each expert at most 110 times; some group names some expert exactly 110 times.
All inputs are finite; a program needn't handle non-finite values.
Results may differ from the reference program's by a relative error of at most 0.02.
Values may be sent and summed in bfloat16 or wider, within the bound.
A program may use at most 256 MiB of HBM per device.

```python
import math
import jax
import jax.numpy as jnp
import numpy as np
from jax import lax

D = 2048
H = 16
HD = 128
EFF = 1408
SFF = 5632
TOP = 4
DBLOCK = 256
TOK_DEV = 320
TOKENS = 5120
EXPERTS = 16
CAP = 110
N_DP = 16


def draw_doc_lengths(key, part):
    key = jax.random.fold_in(key, 11)
    subkeys = jax.random.split(key, 4)
    before = jax.random.randint(subkeys[0], (), 2, TOK_DEV - 1)
    trailing = TOK_DEV - before
    where_long = jax.random.randint(subkeys[1], (), 0, 2)
    cut_trailing = jax.random.randint(subkeys[2], (), 1, trailing)
    cut_before = jax.random.randint(subkeys[3], (), 1, before)
    longest = TOKENS - TOK_DEV
    layout_one = jnp.stack([before, jnp.asarray(longest, jnp.int32), cut_trailing, trailing - cut_trailing])
    layout_two = jnp.stack([cut_before, before - cut_before, jnp.asarray(longest, jnp.int32), trailing])
    return jnp.where(where_long == 0, layout_one, layout_two).astype(jnp.int32)


def draw_layer_input(key, part):
    key = jax.random.fold_in(key, 23)
    row_place = jnp.arange(TOKENS, dtype=jnp.float32)[:, None] / (TOKENS - 1)
    row_scale = 0.5 + row_place
    normal_part = jax.random.normal(key, (TOKENS, D), jnp.float32)
    base = jnp.clip(normal_part, -3.0, 3.0)
    return (base * row_scale).astype(jnp.bfloat16)


def shard_levels(own_key, shape, cuts, least, top_value):
    def one(dim, shards_of):
        draws = jax.random.uniform(jax.random.fold_in(jax.random.fold_in(own_key, 6), dim), (shards_of,), jnp.float32, least / len(cuts), top_value / len(cuts))
        return jnp.repeat(jnp.exp(draws), shape[dim] // shards_of).reshape((-1,) + (1,) * (len(shape) - dim - 1))

    gain = one(*cuts[0])
    for cut in cuts[1:]:
        gain = gain * one(*cut)
    return gain


def deal_out(stream_key, own, number, rows, count, top, reach, skew):
    sequence = jax.random.permutation(stream_key, count)
    crowded, ordinary = load_shares(count, rows * top, reach, skew, True), load_shares(count, rows * top, reach, skew, False)
    places = jnp.arange(count)

    def named(sizes, turn):
        used = int((sizes > 0).sum())
        fixed = max(1, used // 4)
        passed = fixed + (places - fixed + turn * (used - fixed)) % max(1, count - fixed)
        return jnp.zeros((count,), jnp.int32).at[sequence[jnp.where(places < fixed, places, passed)]].set(jnp.asarray(sizes, jnp.int32))

    sizes = jnp.where(number % 4 == 0, named(crowded, number // 4), named(ordinary, number - number // 4 - 1))
    mixed = jax.random.permutation(jax.random.fold_in(own, 3), count)
    donor, receiver = mixed[0:count // 2 * 2:2], mixed[1:count // 2 * 2:2]
    room = jnp.minimum(sizes[donor] - 1, reach - sizes[receiver]) // 2
    room = jnp.where((donor == sequence[0]) | (receiver == sequence[0]) | (sizes[receiver] == 0), 0, jnp.maximum(room, 0))
    passed = jax.random.randint(jax.random.fold_in(own, 4), (count // 2,), 0, 1 << 20) % (room + 1)
    sizes = sizes.at[donor].add(-passed).at[receiver].add(passed)
    items = jnp.searchsorted(jnp.cumsum(sizes), jnp.arange(rows * top), side="right").astype(jnp.int32)
    listing = items.reshape(top, rows).T
    listing = listing[jax.random.permutation(jax.random.fold_in(own, 1), rows)]
    turn = jax.random.randint(jax.random.fold_in(own, 2), (rows, 1), 0, top)
    return jnp.take_along_axis(listing, (jnp.arange(top)[None, :] + turn) % top, axis=1)


def load_shares(number_of, total, most, slope, full):
    loads = [(1 << 20) // math.isqrt(grade ** slope) + 1 for grade in range(1, number_of + 1)]
    largest = most if full else min(most, max(-(-total // number_of), total * loads[0] // sum(loads)))
    least = 1 if total - largest >= number_of - 1 else 0
    holding, rest = [largest] + [least] * (number_of - 1), total - largest - least * (number_of - 1)
    while rest > 0:
        movable = [i for i in range(1, number_of) if holding[i] < largest] or [i for i in range(1, number_of) if holding[i] < most]
        pool, remaining = sum([loads[i] for i in movable]), rest
        for i in movable:
            extra = min(most - holding[i], max(1, remaining * loads[i] // pool), rest)
            holding[i] = holding[i] + extra
            rest = rest - extra
    return np.array(holding)


def gaussian(key, dims, deviation, reach, cuts=(), kind=jnp.bfloat16):
    drawn = jax.random.normal(key, dims, jnp.float32) * deviation
    if len(cuts) > 0:
        drawn = shard_levels(key, dims, cuts, -0.22, 0.18) * drawn
    return jnp.clip(drawn, min=-reach, max=reach).astype(kind)


def setup_inputs(seed: int = 0) -> dict:
    keys = jax.random.split(jax.random.key(seed), 16)
    layer_input = draw_layer_input(jax.random.fold_in(keys[15], 71), 0)
    doc_lengths = draw_doc_lengths(jax.random.fold_in(keys[15], 71), 0)
    expert_ids_keys = jax.random.split(jax.random.fold_in(keys[2], 1), TOKENS // TOK_DEV)
    expert_ids_turns = jax.random.permutation(jax.random.fold_in(keys[2], 3), TOKENS // TOK_DEV)
    expert_ids = jax.vmap(lambda own, number: deal_out(jax.random.fold_in(keys[2], 2), own, number, TOK_DEV, EXPERTS, TOP, CAP, 0))(expert_ids_keys, expert_ids_turns).reshape((TOKENS, TOP))
    attn_gain = jnp.clip(1.0 + 0.18 * jax.random.normal(keys[3], (D,), jnp.float32), 0.1, 1.9)
    qkv_weight = gaussian(keys[4], (D, 3, H, HD), D ** -0.5, 0.125, ((2, 8),))
    qkv_bias = gaussian(keys[5], (3, H, HD), 0.5, 3.0, ((1, 8),))
    out_weight = gaussian(keys[6], (H, HD, D), (H * HD // 16) ** -0.5, 0.5, ((0, 8),))
    ffn_gain = jnp.clip(1.0 + 0.18 * jax.random.normal(keys[7], (D,), jnp.float32), 0.1, 1.9)
    router_weight = gaussian(keys[8], (D, EXPERTS), (4 * D) ** -0.5, 0.0625)
    shared_gate = gaussian(keys[9], (D,), D ** -0.5, 0.125)
    shared_in = gaussian(keys[10], (D, 2, SFF), D ** -0.5, 0.125, ((2, 8),))
    shared_out = gaussian(keys[11], (SFF, D), (SFF // 16) ** -0.5, 0.3125, ((0, 8),))
    expert_in = gaussian(keys[12], (EXPERTS, D, 2, EFF), D ** -0.5, 0.125, ((0, 16), (3, 8)))
    expert_out = gaussian(keys[13], (EXPERTS, EFF, D), (max(EFF // 64, 1)) ** -0.5, 1.25, ((0, 16), (1, 8)))
    cotangent = gaussian(keys[14], (TOKENS, D), 1.0, 6.0, ((0, 16),))
    return {"layer_input": layer_input, "doc_lengths": doc_lengths, "expert_ids": expert_ids, "attn_gain": attn_gain, "qkv_weight": qkv_weight, "qkv_bias": qkv_bias, "out_weight": out_weight, "ffn_gain": ffn_gain, "router_weight": router_weight, "shared_gate": shared_gate, "shared_in": shared_in, "shared_out": shared_out, "expert_in": expert_in, "expert_out": expert_out, "cotangent": cotangent}


EPSILON = 1e-06
THETA = 1000000.0
NEG_FILL = -1e+30
PRECISE = lax.Precision.HIGHEST

@jax.custom_vjp
def low(v):
    return lax.optimization_barrier(v.astype(jnp.bfloat16)).astype(jnp.float32)

@jax.custom_vjp
def low_back(v):
    return v

def low_keep(v):
    return (low(v), None)

def low_pass(kept, grad):
    return (grad,)

def back_keep(v):
    return (v, None)

def back_low(kept, grad):
    return (low(grad),)
low.defvjp(low_keep, low_pass)
low_back.defvjp(back_keep, back_low)

def doc_layout(lengths, token_index):
    doc_ends = jnp.cumsum(lengths).astype(jnp.int32)
    starts = (doc_ends - lengths).astype(jnp.int32)
    seq_ids = lax.optimization_barrier(jnp.sum((token_index[:, None] >= doc_ends[None, :]).astype(jnp.int32), axis=1)).astype(jnp.int32)
    member = seq_ids[:, None] == jnp.arange(lengths.shape[0], dtype=jnp.int32)[None, :]
    begins = lax.optimization_barrier(jnp.sum(jnp.where(member, starts[None, :], 0), axis=1)).astype(jnp.int32)
    offsets = (token_index - begins).astype(jnp.int32)
    return (seq_ids, offsets, offsets // DBLOCK)

def rope_tables(offsets, head_dim):
    half_dim = head_dim // 2
    frequencies = jnp.exp(jnp.arange(half_dim, dtype=jnp.float32) * (-2.0 * math.log(THETA) / head_dim))
    angles = offsets.astype(jnp.float32)[:, None] * frequencies[None, :]
    return (jnp.cos(angles)[:, None, :], jnp.sin(angles)[:, None, :])

def rotate(vectors, cosine, sine_table):
    half_dim = vectors.shape[-1] // 2
    front_half = vectors[..., :half_dim]
    back_half = vectors[..., half_dim:]
    return jnp.concatenate([front_half * cosine - back_half * sine_table, back_half * cosine + front_half * sine_table], axis=-1)

def softmax_rows(logits):
    row_peak = lax.optimization_barrier(jnp.max(logits, axis=-1, keepdims=True))
    exp_terms = jnp.exp(logits - row_peak)
    return exp_terms / lax.optimization_barrier(jnp.sum(exp_terms, axis=-1, keepdims=True))

def attend_block(pieces, keys_all, values_all, seq_all, blk_all):
    query_block, seq_query, blk_query = pieces
    raw_scores = jnp.einsum('qhe,khe->hqk', query_block, keys_all, precision=PRECISE) * HD ** (-0.5)
    scores = low_back(raw_scores)
    allowed = (seq_query[:, None] == seq_all[None, :]) & (blk_all[None, :] <= blk_query[:, None])
    masked = jnp.where(allowed[None], scores, NEG_FILL)
    row_peak = lax.optimization_barrier(jnp.max(masked, axis=2, keepdims=True))
    exp_terms = jnp.where(allowed[None], jnp.exp(masked - row_peak), 0.0)
    attn_probs = low(exp_terms / lax.optimization_barrier(jnp.sum(exp_terms, axis=2, keepdims=True)))
    return jnp.einsum('hqk,khe->qhe', attn_probs, values_all, precision=PRECISE)

def route_slots(expert_ids):
    grouped = expert_ids.reshape(N_DP, TOK_DEV * TOP)
    onehot = (grouped[:, :, None] == jnp.arange(EXPERTS, dtype=jnp.int32)[None, None, :]).astype(jnp.int32)
    rank_in = jnp.cumsum(onehot, axis=1).astype(jnp.int32) - onehot
    slot_in = lax.optimization_barrier(jnp.sum(rank_in * onehot, axis=2)).astype(jnp.int32)
    device = jnp.arange(N_DP, dtype=jnp.int32)[:, None]
    places = (grouped * (N_DP * CAP) + device * CAP + slot_in).reshape(-1).astype(jnp.int32)
    token_of = (device * TOK_DEV + jnp.arange(TOK_DEV * TOP, dtype=jnp.int32)[None, :] // TOP).reshape(-1).astype(jnp.int32)
    owner_row = jnp.zeros((EXPERTS * N_DP * CAP,), jnp.int32).at[places].set(token_of)
    filled = jnp.zeros((EXPERTS * N_DP * CAP,), jnp.float32).at[places].set(1.0)
    return (places, owner_row, filled)

def reference(layer_input, doc_lengths, expert_ids, attn_gain, qkv_weight, qkv_bias, out_weight, ffn_gain, router_weight, shared_gate, shared_in, shared_out, expert_in, expert_out, cotangent):
    every_index = jnp.arange(TOKENS, dtype=jnp.int32)
    seq_all, pos_all, blk_all = doc_layout(doc_lengths, every_index)
    cosine, sine_table = rope_tables(pos_all, HD)
    places, owner_row, filled = route_slots(expert_ids)
    route_hot = (expert_ids[:, :, None] == jnp.arange(EXPERTS, dtype=jnp.int32)[None, None, :]).astype(jnp.float32)
    q_block = min(512, TOKENS)
    n_blocks = TOKENS // q_block

    def forward(residual, gain_one, w_qkv, b_qkv, w_out, gain_two, w_router, w_sgate, w_sin, w_sout, w_ein, w_eout):
        inv_first = lax.rsqrt(lax.optimization_barrier(jnp.mean(residual * residual, axis=1, keepdims=True)) + EPSILON)
        normed_one = low(residual * inv_first * gain_one)
        projected = low_back(jnp.einsum('td,dshe->tshe', normed_one, w_qkv, precision=PRECISE) + b_qkv[None])
        queries = low(rotate(projected[:, 0], cosine, sine_table))
        keys_all = low(rotate(projected[:, 1], cosine, sine_table))
        values_all = low(projected[:, 2])

        def block_fn(pieces):
            return attend_block(pieces, keys_all, values_all, seq_all, blk_all)
        head_blocks = lax.map(jax.checkpoint(block_fn), (queries.reshape(n_blocks, q_block, H, HD), seq_all.reshape(n_blocks, q_block), blk_all.reshape(n_blocks, q_block)))
        heads_out = low(low_back(head_blocks.reshape(TOKENS, H, HD)))
        attn_out = low_back(jnp.einsum('the,hed->td', heads_out, w_out, precision=PRECISE))
        middle = residual + attn_out
        inv_second = lax.rsqrt(lax.optimization_barrier(jnp.mean(middle * middle, axis=1, keepdims=True)) + EPSILON)
        normed_two = low(middle * inv_second * gain_two)
        router_probs = softmax_rows(jnp.dot(normed_two, w_router, precision=PRECISE))
        route_gates = lax.optimization_barrier(jnp.sum(route_hot * router_probs[:, None, :], axis=2))
        gate_value = jax.nn.sigmoid(jnp.dot(normed_two, w_sgate, precision=PRECISE))
        shared_gu = low_back(jnp.einsum('td,dsf->tsf', normed_two, w_sin, precision=PRECISE))
        shared_hidden = low(jax.nn.silu(shared_gu[:, 0]) * shared_gu[:, 1])
        shared_res = low_back(jnp.dot(shared_hidden, w_sout, precision=PRECISE))
        exp_rows = normed_two[owner_row] * filled[:, None]

        def expert_block(pieces):
            block_rows, w_in, w_down = pieces
            expert_gu = low_back(jnp.einsum('rd,dsf->rsf', block_rows, w_in, precision=PRECISE))
            expert_hidden = low(jax.nn.silu(expert_gu[:, 0]) * expert_gu[:, 1])
            return low_back(jnp.dot(expert_hidden, w_down, precision=PRECISE))
        expert_res = lax.map(jax.checkpoint(expert_block), (exp_rows.reshape(EXPERTS, N_DP * CAP, D), w_ein, w_eout))
        route_out = expert_res.reshape(-1, D)[places].reshape(TOKENS, TOP, D)
        routed = lax.optimization_barrier(jnp.sum(route_gates[:, :, None] * route_out, axis=1))
        moe_out = routed + gate_value[:, None] * shared_res
        output = middle + moe_out
        return (output, (attn_out, middle, moe_out))
    primals = (layer_input.astype(jnp.float32), attn_gain, qkv_weight.astype(jnp.float32), qkv_bias.astype(jnp.float32), out_weight.astype(jnp.float32), ffn_gain, router_weight.astype(jnp.float32), shared_gate.astype(jnp.float32), shared_in.astype(jnp.float32), shared_out.astype(jnp.float32), expert_in.astype(jnp.float32), expert_out.astype(jnp.float32))
    output, pullback, extras = jax.vjp(forward, *primals, has_aux=True)
    gradient = pullback(cotangent.astype(jnp.float32))
    attn_out, middle, moe_out = extras
    residual = primals[0]
    rms_stats = jnp.sqrt(jnp.stack([jnp.mean(residual * residual), jnp.mean(attn_out * attn_out), jnp.mean(middle * middle), jnp.mean(moe_out * moe_out), jnp.mean(output * output)]))
    return (output.astype(jnp.bfloat16), gradient[0], gradient[2], gradient[3], gradient[4], gradient[1], gradient[5], gradient[6], gradient[7], gradient[8], gradient[9], gradient[10], gradient[11], rms_stats)
```

```python
import math

import jax
import jax.numpy as jnp
from jax import lax
from jax.experimental import pallas as pl
from jax.experimental.pallas import tpu as pltpu
from jax.sharding import PartitionSpec as P

DBLOCK = 256
EPSILON = 1e-06
THETA = 1000000.0
NEG_FILL = -1e30
MESH = pl.DeviceIdType.MESH
f32 = jnp.float32
bf16 = jnp.bfloat16
N_DP = 16
N_T = 8
SLOTS = 112

HBM = pl.BlockSpec(memory_space=pl.ANY)
VMEM = pl.BlockSpec(memory_space=pltpu.VMEM)


def greet(peers):
    barrier = pltpu.get_barrier_semaphore()
    for peer in peers:
        pl.semaphore_signal(barrier, inc=1, device_id=peer, device_id_type=MESH)
    pl.semaphore_wait(barrier, len(peers))


def remote(src, dst, send, recv, device):
    return pltpu.make_async_remote_copy(
        src_ref=src,
        dst_ref=dst,
        send_sem=send,
        recv_sem=recv,
        device_id=device,
        device_id_type=MESH,
    )


def dma(*shape):
    return pltpu.SemaphoreType.DMA(shape)


def comm_params(number, limit=None):
    return pltpu.CompilerParams(
        collective_id=number, has_side_effects=True, vmem_limit_bytes=limit
    )


def gather_keys(kv, q):
    def kernel(kv_ref, q_ref, all_ref, pair_ref, send, recv, qsend, qrecv, local):
        me = lax.axis_index("dp")
        core = lax.rem(me, 2)
        greet([{"dp": me ^ k} for k in range(1, N_DP)])
        swap = remote(
            q_ref.at[1 - core], pair_ref.at[core], qsend, qrecv, {"dp": me ^ 1}
        )
        swap.start()
        copies = []
        for k in (2, 4, 12, 6, 14, 8, 10, 3, 5, 13, 7, 15, 9, 11, 1):
            peer = me ^ k
            head = core if k % 2 == 0 else 1 - core
            copies.append(
                remote(kv_ref.at[head], all_ref.at[me], send.at[k], recv.at[k], {"dp": peer})
            )
            copies[-1].start()
        own = pltpu.make_async_copy(kv_ref.at[core], all_ref.at[me], local.at[0])
        own.start()
        own_q = pltpu.make_async_copy(q_ref.at[core], pair_ref.at[core], local.at[1])
        own_q.start()
        swap.wait()
        for copy in copies:
            copy.wait()
        own.wait()
        own_q.wait()

    return pl.pallas_call(
        kernel,
        out_shape=(
            jax.ShapeDtypeStruct((N_DP,) + kv.shape[1:], kv.dtype),
            jax.ShapeDtypeStruct(q.shape, q.dtype),
        ),
        in_specs=[HBM, HBM],
        out_specs=(HBM, HBM),
        scratch_shapes=[dma(N_DP), dma(N_DP), pltpu.SemaphoreType.DMA, pltpu.SemaphoreType.DMA, dma(2)],
        compiler_params=comm_params(1),
        name="gather_keys",
    )(kv, q)


def swap_cores(x, number):
    def kernel(x_ref, out_ref, send, recv, local):
        me = lax.axis_index("dp")
        core = lax.rem(me, 2)
        greet([{"dp": me ^ 1}])
        swap = remote(x_ref.at[1 - core], out_ref.at[core], send, recv, {"dp": me ^ 1})
        swap.start()
        own = pltpu.make_async_copy(x_ref.at[core], out_ref.at[core], local)
        own.start()
        swap.wait()
        own.wait()

    return pl.pallas_call(
        kernel,
        out_shape=jax.ShapeDtypeStruct(x.shape, x.dtype),
        in_specs=[HBM],
        out_specs=HBM,
        scratch_shapes=[pltpu.SemaphoreType.DMA, pltpu.SemaphoreType.DMA, pltpu.SemaphoreType.DMA],
        compiler_params=comm_params(number),
        name="swap_cores",
    )(x)


ORDER = (2, 4, 12, 6, 14, 8, 10, 3, 5, 13, 7, 15, 9, 11, 1)


def rows_out(x, number):
    def kernel(x_ref, out_ref, send, recv, local):
        me = lax.axis_index("dp")
        parity = lax.rem(lax.axis_index("tensor"), 2)
        core = lax.rem(me, 2)
        greet([{"dp": me ^ k} for k in range(1, N_DP)])

        def copy(k):
            return remote(
                x_ref.at[me ^ k], out_ref.at[me // 2], send.at[k], recv.at[k], {"dp": me ^ k}
            )

        @pl.when(core == parity)
        def _():
            for k in ORDER:
                copy(k).start()
            own = pltpu.make_async_copy(x_ref.at[me], out_ref.at[me // 2], local)
            own.start()
            own.wait()
            for k in ORDER:
                copy(k).wait_send()
                if k % 2 == 0:
                    copy(k).wait_recv()

        @pl.when(core != parity)
        def _():
            for k in ORDER:
                if k % 2 == 1:
                    copy(k).wait_recv()

    return pl.pallas_call(
        kernel,
        out_shape=jax.ShapeDtypeStruct((8,) + x.shape[1:], x.dtype),
        in_specs=[HBM],
        out_specs=HBM,
        scratch_shapes=[dma(N_DP), dma(N_DP), pltpu.SemaphoreType.DMA],
        compiler_params=comm_params(number),
        name="rows_out",
    )(x)


def rows_back(xs, number):
    count = len(xs)

    def kernel(*refs):
        x_refs, out_refs = refs[:count], refs[count : 2 * count]
        send, recv, local = refs[2 * count :]
        me = lax.axis_index("dp")
        parity = lax.rem(lax.axis_index("tensor"), 2)
        core = lax.rem(me, 2)
        greet([{"dp": me ^ k} for k in range(1, N_DP)])

        def copy(i, k):
            peer = me ^ k
            return remote(
                x_refs[i].at[peer // 2],
                out_refs[i].at[me],
                send.at[i, k],
                recv.at[i, k],
                {"dp": peer},
            )

        def own(i):
            return pltpu.make_async_copy(x_refs[i].at[me // 2], out_refs[i].at[me], local.at[i])

        @pl.when(core == parity)
        def _():
            for i in range(count):
                for k in ORDER:
                    if k % 2 == 0:
                        copy(i, k).start()
                own(i).start()
            for i in range(count):
                own(i).wait()
                for k in ORDER:
                    if k % 2 == 0:
                        copy(i, k).wait_send()
                    copy(i, k).wait_recv()

        @pl.when(core != parity)
        def _():
            for i in range(count):
                for k in ORDER:
                    if k % 2 == 1:
                        copy(i, k).start()
            for i in range(count):
                for k in ORDER:
                    if k % 2 == 1:
                        copy(i, k).wait_send()

    return pl.pallas_call(
        kernel,
        out_shape=tuple(jax.ShapeDtypeStruct((N_DP,) + x.shape[1:], x.dtype) for x in xs),
        in_specs=[HBM] * count,
        out_specs=(HBM,) * count,
        scratch_shapes=[dma(count, N_DP), dma(count, N_DP), dma(count)],
        compiler_params=comm_params(number),
        name="rows_back",
    )(*xs)


def scatter_keys(dkv, dq, number):
    def kernel(x_ref, q_ref, out_ref, pair_ref, send, recv, qsend, qrecv, local):
        me = lax.axis_index("dp")
        core = lax.rem(me, 2)
        greet([{"dp": me ^ k} for k in range(1, N_DP)])
        copies = []
        for k in ORDER:
            peer = me ^ k
            copies.append(
                remote(x_ref.at[peer], out_ref.at[me], send.at[k], recv.at[k], {"dp": peer})
            )
            copies[-1].start()
        swap = remote(
            q_ref.at[1 - core], pair_ref.at[core], qsend, qrecv, {"dp": me ^ 1}
        )
        swap.start()
        own = pltpu.make_async_copy(x_ref.at[me], out_ref.at[me], local.at[0])
        own.start()
        own_q = pltpu.make_async_copy(q_ref.at[core], pair_ref.at[core], local.at[1])
        own_q.start()
        swap.wait()
        for copy in copies:
            copy.wait()
        own.wait()
        own_q.wait()

    return pl.pallas_call(
        kernel,
        out_shape=(
            jax.ShapeDtypeStruct(dkv.shape, dkv.dtype),
            jax.ShapeDtypeStruct(dq.shape, dq.dtype),
        ),
        in_specs=[HBM, HBM],
        out_specs=(HBM, HBM),
        scratch_shapes=[dma(N_DP), dma(N_DP), pltpu.SemaphoreType.DMA, pltpu.SemaphoreType.DMA, dma(2)],
        compiler_params=comm_params(number),
        name="scatter_keys",
    )(dkv, dq)


def join(finish, partials, slices, gains, n_gather, plain_shapes, number, name):
    n_part, n_slice, n_gain = len(partials), len(slices), len(gains)
    rows, width = partials[0].shape[1:]
    n_in = n_part + n_slice + n_gain
    n_plain = len(plain_shapes)

    def kernel(*refs):
        part_refs = refs[:n_part]
        slice_refs = refs[n_part : n_part + n_slice]
        gain_refs = refs[n_part + n_slice : n_in]
        full_refs = refs[n_in : n_in + n_gather]
        plain_refs = refs[n_in + n_gather : n_in + n_gather + n_plain]
        got, mine, send, recv, asend, arecv, local = refs[n_in + n_gather + n_plain :]
        me = lax.axis_index("tensor")
        greet([{"tensor": me ^ k} for k in range(1, N_T)])
        steps = (1, 3, 2, 4, 5, 7, 6)
        arriving = []
        for i in range(n_part):
            arriving.append([])
            for k in steps:
                copy = remote(
                    part_refs[i].at[me ^ k],
                    got.at[i, k],
                    send.at[i, k],
                    recv.at[i, k],
                    {"tensor": me ^ k},
                )
                copy.start()
                arriving[i].append(copy)
        leaving = []

        def total(i):
            value = part_refs[i][me].astype(f32)
            for k, copy in zip(steps, arriving[i]):
                copy.wait_recv()
                value = value + got[i, k].astype(f32)
            return value

        def gather(i, value):
            mine[i] = value.astype(bf16)
            for k in steps:
                copy = remote(
                    mine.at[i],
                    full_refs[i].at[me],
                    asend.at[i, k],
                    arecv.at[i, k],
                    {"tensor": me ^ k},
                )
                copy.start()
                leaving.append(copy)
            own = pltpu.make_async_copy(mine.at[i], full_refs[i].at[me], local.at[i])
            own.start()
            leaving.append(own)

        own_slices = [ref[me] if ref.ndim == 3 else ref[...] for ref in slice_refs]
        finish(total, gather, own_slices, [ref[...] for ref in gain_refs], plain_refs)
        for copies in arriving:
            for copy in copies:
                copy.wait_send()
        for copy in leaving:
            copy.wait()

    return pl.pallas_call(
        kernel,
        out_shape=tuple(jax.ShapeDtypeStruct((N_T, rows, width), bf16) for _ in range(n_gather))
        + tuple(jax.ShapeDtypeStruct(s, f32) for s in plain_shapes),
        in_specs=[VMEM] * n_in,
        out_specs=(HBM,) * n_gather + (VMEM,) * n_plain,
        scratch_shapes=[
            pltpu.VMEM((n_part, N_T, rows, width), bf16),
            pltpu.VMEM((n_gather, rows, width), bf16),
            dma(n_part, N_T),
            dma(n_part, N_T),
            dma(n_gather, N_T),
            dma(n_gather, N_T),
            dma(n_gather),
        ],
        compiler_params=comm_params(number, 48 * 1024 * 1024),
        name=name,
    )(*partials, *slices, *gains)


def sum_small(pack, number):
    rows = pack.shape[1]

    def kernel(x_ref, one_ref, both_ref, got, mine, more, send, recv, tsend, trecv):
        me = lax.axis_index("dp")
        t = lax.axis_index("tensor")
        greet([{"dp": me ^ k} for k in range(1, N_DP)] + [{"tensor": t ^ k} for k in range(1, N_T)])
        copies = []
        for k in range(1, N_DP):
            copies.append(
                remote(x_ref.at[me ^ k], got.at[k], send.at[k], recv.at[k], {"dp": me ^ k})
            )
            copies[-1].start()
        value = x_ref[me]
        for k in range(1, N_DP):
            copies[k - 1].wait_recv()
            value = value + got[k]
        one_ref[...] = value
        mine[...] = value
        others = []
        for k in range(1, N_T):
            others.append(remote(mine, more.at[k], tsend.at[k], trecv.at[k], {"tensor": t ^ k}))
            others[-1].start()
        for k in range(1, N_T):
            others[k - 1].wait_recv()
            value = value + more[k]
        both_ref[...] = value
        for copy in copies + others:
            copy.wait_send()

    return pl.pallas_call(
        kernel,
        out_shape=(jax.ShapeDtypeStruct((rows, 128), f32),) * 2,
        in_specs=[VMEM],
        out_specs=(VMEM, VMEM),
        scratch_shapes=[
            pltpu.VMEM((N_DP, rows, 128), f32),
            pltpu.VMEM((rows, 128), f32),
            pltpu.VMEM((N_T, rows, 128), f32),
            dma(N_DP),
            dma(N_DP),
            dma(N_T),
            dma(N_T),
        ],
        compiler_params=comm_params(number),
        name="sum_small",
    )(pack)


def doc_layout(lengths, token_index):
    doc_ends = jnp.cumsum(lengths)
    starts = doc_ends - lengths
    seq_ids = jnp.sum((token_index[:, None] >= doc_ends[None, :]).astype(jnp.int32), axis=1)
    member = seq_ids[:, None] == jnp.arange(lengths.shape[0], dtype=jnp.int32)[None, :]
    begins = jnp.sum(jnp.where(member, starts[None, :], 0), axis=1)
    offsets = token_index - begins
    return (seq_ids, offsets, offsets // DBLOCK)


def rope_tables(offsets, head_dim):
    half_dim = head_dim // 2
    frequencies = jnp.exp(
        jnp.arange(half_dim, dtype=f32) * (-2.0 * math.log(THETA) / head_dim)
    )
    angles = offsets.astype(f32)[:, None] * frequencies[None, :]
    return (jnp.cos(angles)[:, None, :], jnp.sin(angles)[:, None, :])


def rotate(vectors, cosine, sine):
    half_dim = vectors.shape[-1] // 2
    front, back = vectors[..., :half_dim], vectors[..., half_dim:]
    return jnp.concatenate([front * cosine - back * sine, back * cosine + front * sine], axis=-1)


def silu_back(gate_part, up_part, d_hidden):
    sigmoid_gate = jax.nn.sigmoid(gate_part)
    d_gate = d_hidden * up_part * sigmoid_gate * (1.0 + gate_part * (1.0 - sigmoid_gate))
    d_up = d_hidden * gate_part * sigmoid_gate
    return d_gate, d_up


def dot(pattern, a, b):
    return jnp.einsum(pattern, a, b, preferred_element_type=f32)


def attn_finish(total, gather, slices, gains, plain):
    resid = slices[0].astype(f32)
    attn_out = total(0)
    middle = resid + attn_out
    inv = lax.rsqrt(jnp.mean(middle * middle, axis=1, keepdims=True) + EPSILON)
    gather(0, middle * inv * gains[0])
    plain[0][...] = middle
    plain[1][0:1] = jnp.sum(resid * resid, axis=0, keepdims=True)
    plain[1][1:2] = jnp.sum(attn_out * attn_out, axis=0, keepdims=True)
    plain[1][2:3] = jnp.sum(middle * middle, axis=0, keepdims=True)


def ffn_finish(total, gather, slices, gains, plain):
    upstream, middle = slices[0].astype(f32), slices[1]
    inv = lax.rsqrt(jnp.mean(middle * middle, axis=1, keepdims=True) + EPSILON)
    d_normed = total(0)
    scaled = d_normed * gains[0]
    d_middle = (
        upstream
        + inv * scaled
        - middle * (inv * inv * inv) * jnp.mean(scaled * middle, axis=1, keepdims=True)
    )
    gather(0, d_middle)
    plain[0][...] = d_middle
    plain[1][0:1] = jnp.sum(d_normed * middle * inv, axis=0, keepdims=True)
    moe_out = total(1)
    output = middle + moe_out
    gather(1, output)
    plain[1][1:2] = jnp.sum(moe_out * moe_out, axis=0, keepdims=True)
    plain[1][2:3] = jnp.sum(output * output, axis=0, keepdims=True)


def input_finish(total, gather, slices, gains, plain):
    resid, d_middle = slices[0].astype(f32), slices[1]
    inv = lax.rsqrt(jnp.mean(resid * resid, axis=1, keepdims=True) + EPSILON)
    d_normed = total(0)
    scaled = d_normed * gains[0]
    gather(
        0,
        d_middle
        + inv * scaled
        - resid * (inv * inv * inv) * jnp.mean(scaled * resid, axis=1, keepdims=True),
    )
    plain[0][0:1] = jnp.sum(d_normed * resid * inv, axis=0, keepdims=True)


def on_device(
    layer_input,
    doc_lengths,
    expert_ids,
    attn_gain,
    qkv_weight,
    qkv_bias,
    out_weight,
    ffn_gain,
    router_weight,
    shared_gate,
    shared_in,
    shared_out,
    expert_in,
    expert_out,
    cotangent,
):
    tok, width = layer_input.shape
    dp, tn = lax.axis_index("dp"), lax.axis_index("tensor")
    core = lax.rem(dp, 2)
    parity = lax.rem(tn, 2)
    experts = router_weight.shape[1]
    head_dim = qkv_weight.shape[3]
    stream = tok * N_DP
    part_rows = tok // N_T
    score_scale = head_dim ** (-0.5)
    eff = expert_out.shape[1]

    pairs = [(i, i ^ 1) for i in range(N_T)]
    other_in = lax.ppermute(expert_in[0], "tensor", pairs)
    other_out = lax.ppermute(expert_out[0], "tensor", pairs)

    hot = jnp.sum(
        (expert_ids[:, :, None] == jnp.arange(experts, dtype=jnp.int32)[None, None, :]).astype(f32),
        axis=1,
    )
    before = (jnp.arange(tok)[:, None] > jnp.arange(tok)[None, :]).astype(bf16)
    rank = dot("ts,se->te", before, hot.astype(bf16))
    place = jnp.where(hot > 0, rank, -1.0).astype(jnp.int32).T
    places = (
        place[:, None, :] == jnp.arange(SLOTS, dtype=jnp.int32)[None, :, None]
    ).astype(bf16)
    places_flat = places.reshape(experts * SLOTS, tok)

    up_send = dot("rt,td->rd", places_flat, cotangent).astype(bf16)
    up_rows = rows_out(up_send.reshape(experts, SLOTS, width), 2).reshape(-1, width)

    local_index = dp * tok + jnp.arange(tok, dtype=jnp.int32)
    pair_index = (dp // 2) * (2 * tok) + jnp.arange(2 * tok, dtype=jnp.int32)
    every_index = jnp.arange(stream, dtype=jnp.int32)
    _, pos_local, _ = doc_layout(doc_lengths, local_index)
    seq_pair, _, blk_pair = doc_layout(doc_lengths, pair_index)
    seq_all, _, blk_all = doc_layout(doc_lengths, every_index)
    allowed = (seq_pair[:, None] == seq_all[None, :]) & (blk_all[None, :] <= blk_pair[:, None])
    cosine, sine = rope_tables(pos_local, head_dim)
    residual = layer_input.astype(f32)
    inv_first = lax.rsqrt(jnp.mean(residual * residual, axis=1, keepdims=True) + EPSILON)
    normed_one = (residual * inv_first * attn_gain).astype(bf16)
    projected = dot("td,dshe->tshe", normed_one, qkv_weight) + qkv_bias.astype(f32)[None]
    q_own = rotate(projected[:, 0], cosine, sine).astype(bf16).transpose(1, 0, 2)
    k_own = rotate(projected[:, 1], cosine, sine).astype(bf16).transpose(1, 0, 2)
    v_own = projected[:, 2].astype(bf16).transpose(1, 0, 2)
    kv_own = jnp.concatenate([k_own, v_own], axis=1)
    kv_all, queries = gather_keys(kv_own, q_own)
    queries = queries.reshape(2 * tok, head_dim)
    keys = kv_all[:, :tok].reshape(stream, head_dim)
    values = kv_all[:, tok:].reshape(stream, head_dim)

    raw_scores = dot("qe,ke->qk", queries, keys) * score_scale
    masked = jnp.where(allowed, raw_scores, NEG_FILL)
    row_peak = jnp.max(masked, axis=1, keepdims=True)
    exp_terms = jnp.where(allowed, jnp.exp(masked - row_peak), 0.0)
    attn_probs = exp_terms / jnp.sum(exp_terms, axis=1, keepdims=True)
    probs_low = attn_probs.astype(bf16)
    pair_out = dot("qk,ke->qe", probs_low, values).astype(bf16)
    heads_out = swap_cores(pair_out.reshape(2, tok, head_dim), 3)
    attn_part = dot("hqe,hed->qd", heads_out, out_weight).astype(bf16)
    normed_two, middle, stats_one = join(
        attn_finish,
        [attn_part.reshape(N_T, part_rows, width)],
        [layer_input.reshape(N_T, part_rows, width)],
        [ffn_gain.reshape(1, width)],
        1,
        [(part_rows, width), (8, width)],
        4,
        "join_attn",
    )
    normed_two = normed_two.reshape(tok, width)

    row_send = dot("rt,td->rd", places_flat, normed_two).astype(bf16)
    exp_rows = rows_out(row_send.reshape(experts, SLOTS, width), 5).reshape(-1, width)

    gate_value = jax.nn.sigmoid(dot("td,d->t", normed_two, shared_gate))
    shared_gu = dot("td,dsf->tsf", normed_two, shared_in)
    shared_hidden = (jax.nn.silu(shared_gu[:, 0]) * shared_gu[:, 1]).astype(bf16)
    shared_part = dot("tf,fd->td", shared_hidden, shared_out)
    upstream = cotangent.astype(f32)
    d_shared = (gate_value[:, None] * upstream).astype(bf16)
    gate_partial = jnp.sum(upstream * shared_part, axis=1) * gate_value * (1.0 - gate_value)
    d_shared_hidden = dot("td,fd->tf", d_shared, shared_out)
    d_gate, d_up = silu_back(shared_gu[:, 0], shared_gu[:, 1], d_shared_hidden)
    d_shared_gu = jnp.stack([d_gate, d_up], axis=1).astype(bf16)
    shared_out_part = dot("tf,td->fd", shared_hidden, d_shared).astype(bf16)
    shared_in_part = dot("td,tsf->dsf", normed_two, d_shared_gu).astype(bf16)
    shared_d_normed = (
        dot("tsf,dsf->td", d_shared_gu, shared_in)
        + gate_partial[:, None] * shared_gate.astype(f32)[None, :]
    )
    gate_vec_part = dot("t,td->d", gate_partial, normed_two.astype(f32))

    w_in = jnp.concatenate([expert_in[0], other_in], axis=2)
    w_out = jnp.concatenate([expert_out[0], other_out], axis=0)
    row_logits = dot("rd,de->re", exp_rows, router_weight)
    row_probs = jax.nn.softmax(row_logits, axis=1)
    own_expert = (jnp.arange(experts, dtype=jnp.int32) == dp).astype(f32)[None, :]
    row_gate = jnp.sum(row_probs * own_expert, axis=1, keepdims=True)
    expert_gu = dot("rd,dsf->rsf", exp_rows, w_in)
    expert_hidden = (jax.nn.silu(expert_gu[:, 0]) * expert_gu[:, 1]).astype(bf16)
    expert_part = (row_gate * dot("rf,fd->rd", expert_hidden, w_out)).astype(bf16)
    raw_hidden = dot("rd,fd->rf", up_rows, w_out)
    d_gate_row = jnp.sum(expert_hidden.astype(f32) * raw_hidden, axis=1, keepdims=True)
    d_row_logits = (d_gate_row * row_gate * (own_expert - row_probs)).astype(bf16)
    d_gate, d_up = silu_back(expert_gu[:, 0], expert_gu[:, 1], row_gate * raw_hidden)
    d_expert_gu = jnp.stack([d_gate, d_up], axis=1).astype(bf16)
    d_rows = (
        dot("rsf,dsf->rd", d_expert_gu, w_in) + dot("re,de->rd", d_row_logits, router_weight)
    ).astype(bf16)
    router_part = dot("re,rd->ed", d_row_logits, exp_rows)
    gated_hidden = (expert_hidden.astype(f32) * row_gate).astype(bf16)
    send_in = dot("rd,rsf->dsf", exp_rows, d_expert_gu[:, :, eff:]).astype(bf16)
    send_out = dot("rf,rd->fd", gated_hidden[:, eff:], up_rows).astype(bf16)
    got_in = lax.ppermute(send_in, "tensor", pairs)
    got_out = lax.ppermute(send_out, "tensor", pairs)
    expert_in_grad = (
        dot("rd,rsf->dsf", exp_rows, d_expert_gu[:, :, :eff]) + got_in.astype(f32)
    )[None]
    expert_out_grad = (
        dot("rf,rd->fd", gated_hidden[:, :eff], up_rows) + got_out.astype(f32)
    )[None]

    back_grads, back_out = rows_back(
        [d_rows.reshape(8, SLOTS, width), expert_part.reshape(8, SLOTS, width)], 6
    )

    def combine(operands):
        flat, one, two = operands
        return (
            dot("rt,rd->td", flat, one.reshape(-1, width)),
            dot("rt,rd->td", flat, two.reshape(-1, width)),
        )

    d_routed, routed = lax.cond(
        core == parity,
        combine,
        lambda operands: (jnp.zeros((tok, width), f32),) * 2,
        (places_flat, back_grads, back_out),
    )
    d_normed_part = (shared_d_normed + d_routed).astype(bf16)
    moe_part = (gate_value[:, None] * shared_part + routed).astype(bf16)
    d_attn, output, d_middle, stats_two = join(
        ffn_finish,
        [d_normed_part.reshape(N_T, part_rows, width), moe_part.reshape(N_T, part_rows, width)],
        [cotangent.reshape(N_T, part_rows, width), middle],
        [ffn_gain.reshape(1, width)],
        2,
        [(part_rows, width), (8, width)],
        7,
        "join_ffn",
    )
    d_attn = d_attn.reshape(tok, width)

    outproj_part = dot("hqe,qd->hed", heads_out, d_attn).astype(bf16)
    d_heads = dot("qd,hed->hqe", d_attn, out_weight).astype(bf16)
    d_heads = swap_cores(d_heads, 8).reshape(2 * tok, head_dim)
    d_values = dot("qk,qe->ke", probs_low, d_heads)
    d_probs = dot("qe,ke->qk", d_heads, values)
    d_scores = (
        attn_probs * (d_probs - jnp.sum(attn_probs * d_probs, axis=1, keepdims=True))
    ).astype(bf16)
    d_queries = dot("qk,ke->qe", d_scores, keys) * score_scale
    d_keys = dot("qk,qe->ke", d_scores, queries) * score_scale
    dkv = jnp.concatenate(
        [d_keys.reshape(N_DP, tok, head_dim), d_values.reshape(N_DP, tok, head_dim)], axis=1
    ).astype(bf16)
    got_kv, d_queries = scatter_keys(
        dkv, d_queries.astype(bf16).reshape(2, tok, head_dim), 9
    )
    d_kv = jnp.sum(got_kv.astype(f32).reshape(8, 2, 2, tok, head_dim), axis=0)
    d_q = rotate(d_queries.astype(f32).transpose(1, 0, 2), cosine, -sine)
    d_k = rotate(d_kv[:, 0].transpose(1, 0, 2), cosine, -sine)
    d_v = d_kv[:, 1].transpose(1, 0, 2)
    d_proj = jnp.stack([d_q, d_k, d_v], axis=1).astype(bf16)
    d_normed_one = dot("tshe,dshe->td", d_proj, qkv_weight).astype(bf16)
    qkv_part = dot("td,tshe->dshe", normed_one, d_proj).astype(bf16)
    bias_part = jnp.sum(d_proj.astype(f32), axis=0)
    input_grad, stats_three = join(
        input_finish,
        [d_normed_one.reshape(N_T, part_rows, width)],
        [layer_input.reshape(N_T, part_rows, width), d_middle],
        [attn_gain.reshape(1, width)],
        1,
        [(8, width)],
        10,
        "join_input",
    )
    input_grad = input_grad.reshape(tok, width).astype(f32)

    def slices(row):
        return row.reshape(-1, N_DP, 128).transpose(1, 0, 2)

    five = jnp.concatenate([jnp.sum(stats_one[:3], axis=1), jnp.sum(stats_two[1:3], axis=1)])
    pack = jnp.concatenate(
        [
            slices(router_part),
            slices(gate_vec_part),
            slices(stats_two[0]),
            slices(stats_three[0]),
            jnp.broadcast_to(jnp.pad(five, (0, 123))[None, None], (N_DP, 1, 128)),
            jnp.pad(
                bias_part.reshape(6, N_DP, 8).transpose(1, 0, 2).reshape(N_DP, 1, 48),
                ((0, 0), (0, 3), (0, 80)),
            ),
        ],
        axis=1,
    )
    over_dp, over_both = sum_small(pack, 11)
    bias_grad = over_dp[20, :48].reshape(3, 2, 8)
    router_grad = over_both[:16].T
    rms_stats = jnp.sqrt(over_both[19, :5] / (stream * width))

    def scattered(part, dim):
        return lax.psum_scatter(part, "dp", scatter_dimension=dim, tiled=True).astype(f32)

    return (
        output.reshape(tok, width),
        input_grad,
        scattered(qkv_part, 0),
        bias_grad,
        scattered(outproj_part, 2),
        over_both[18],
        over_both[17],
        router_grad,
        over_both[16],
        scattered(shared_in_part, 0),
        scattered(shared_out_part, 1),
        expert_in_grad,
        expert_out_grad,
        rms_stats,
    )


def solution(mesh):
    in_specs = (
        P("dp", None),
        P(),
        P("dp", None),
        P(),
        P(None, None, "tensor", None),
        P(None, "tensor", None),
        P("tensor", None, None),
        P(),
        P(),
        P(),
        P(None, None, "tensor"),
        P("tensor", None),
        P("dp", None, None, "tensor"),
        P("dp", "tensor", None),
        P("dp", None),
    )
    out_specs = (
        P("dp", None),
        P("dp", None),
        P("dp", None, "tensor", None),
        P(None, "tensor", "dp"),
        P("tensor", None, "dp"),
        P("dp"),
        P("dp"),
        P("dp", None),
        P("dp"),
        P("dp", None, "tensor"),
        P("tensor", "dp"),
        P("dp", None, None, "tensor"),
        P("dp", "tensor", None),
        P(),
    )
    return jax.shard_map(
        on_device, mesh=mesh, in_specs=in_specs, out_specs=out_specs, check_vma=False
    )
```

```python
import math

import jax
import jax.numpy as jnp
from jax import lax
from jax.experimental import pallas as pl
from jax.experimental.pallas import tpu as pltpu
from jax.sharding import PartitionSpec as P

DBLOCK = 256
EPSILON = 1e-06
THETA = 1000000.0
NEG_FILL = -1e30
MESH = pl.DeviceIdType.MESH
f32 = jnp.float32
bf16 = jnp.bfloat16
N_DP = 16
N_T = 8
SLOTS = 112
LIMIT = 48 * 1024 * 1024
CODE = 1 << 16

HBM = pl.BlockSpec(memory_space=pl.ANY)
VMEM = pl.BlockSpec(memory_space=pltpu.VMEM)


def greet(peers, more=None):
    barrier = pltpu.get_barrier_semaphore()
    for peer in peers:
        pl.semaphore_signal(barrier, inc=1, device_id=peer, device_id_type=MESH)
    count = len(peers)
    if more is not None:
        count = count + more.greet()
    pl.semaphore_wait(barrier, count)


def remote(src, dst, send, recv, device):
    return pltpu.make_async_remote_copy(
        src_ref=src,
        dst_ref=dst,
        send_sem=send,
        recv_sem=recv,
        device_id=device,
        device_id_type=MESH,
    )


def dma(*shape):
    return pltpu.SemaphoreType.DMA(shape)


def cost(micros):
    return pl.CostEstimate(flops=0, bytes_accessed=int(micros * 3e6), transcendentals=0)


def comm_params(number, limit=None):
    return pltpu.CompilerParams(
        collective_id=number, has_side_effects=True, vmem_limit_bytes=limit
    )


GROUPS = 4
ORDER = (4, 12, 2, 5, 13, 3, 8, 6, 14, 9, 7, 15, 10, 11, 1)
STEPS = (1, 3, 2, 4, 5, 7, 6)
CHUNKS = ((0, 48), (48, 64))


def sems(*counts):
    return [dma(*c) if isinstance(c, tuple) else dma(c) for c in counts]


def dp_peers():
    me = lax.axis_index("dp")
    return [{"dp": me ^ k} for k in range(1, N_DP)]


def tensor_peers():
    me = lax.axis_index("tensor")
    return [{"tensor": me ^ k} for k in range(1, N_T)]


def coordinates():
    d, t = lax.axis_index("dp"), lax.axis_index("tensor")
    return d, d // 4, t // 4, t % 4


def route_plane():
    d, z, _, y = coordinates()
    plane = 2 * ((z + d // 2) % 2) + d % 2
    return plane, y ^ plane


class Rows:
    def __init__(self, x_ref, out_ref, send, recv, local, back=False):
        self.x, self.out, self.send, self.recv, self.local, self.back = x_ref, out_ref, send, recv, local, back
        d, z, half, y = coordinates()
        plane, offset = route_plane()
        if back:
            experts = [{"dp": 4 * k + offset, "tensor": 4 * half + plane} for k in range(GROUPS)]
            target = y ^ (d % 4)
        else:
            experts = [{"dp": 4 * (z ^ offset) + j, "tensor": 4 * half + plane} for j in range(GROUPS)]
        groups = [
            {
                "dp": 4 * g + 2 * ((y // 2 + g) % 2) + y % 2,
                "tensor": 4 * half + (target if back else y ^ g ^ z),
            }
            for g in range(GROUPS)
        ]
        self.peers, self.sources = (groups, experts) if back else (experts, groups)
        self.slot = z
        self.mine = z if back else d % 4
        self.own = offset == 0
        if back:
            self.own = jnp.logical_and(self.own, d % 4 == 0)
        self.d = d

    def is_own(self, j):
        return jnp.logical_and(self.own, self.mine == j)

    def greet(self):
        barrier = pltpu.get_barrier_semaphore()
        for j in range(GROUPS):
            source = self.sources[j]

            @pl.when(jnp.logical_not(jnp.logical_and(self.own, self.slot == j)))
            def _():
                pl.semaphore_signal(barrier, inc=1, device_id=source, device_id_type=MESH)

        return GROUPS - self.own.astype(jnp.int32)

    def copy(self, j, c):
        rows = pl.ds(*CHUNKS[c])
        return remote(
            self.x.at[j, rows],
            self.out.at[self.slot, rows],
            self.send.at[c, j],
            self.recv.at[c, self.slot],
            self.peers[j],
        )

    def arrival(self, j, c):
        rows = pl.ds(*CHUNKS[c])
        return remote(
            self.x.at[j, rows],
            self.out.at[j, rows],
            self.send.at[c, j],
            self.recv.at[c, j],
            self.peers[j],
        )

    def inside(self):
        return pltpu.make_async_copy(self.x.at[self.mine], self.out.at[self.slot], self.local.at[0])

    def start(self):
        for c in range(len(CHUNKS)):
            for j in range(GROUPS):

                @pl.when(jnp.logical_not(self.is_own(j)))
                def _():
                    self.copy(j, c).start()

        @pl.when(self.own)
        def _():
            self.inside().start()

    def wait(self):
        @pl.when(self.own)
        def _():
            self.inside().wait()

        for c in range(len(CHUNKS)):
            for j in range(GROUPS):

                @pl.when(jnp.logical_not(self.is_own(j)))
                def _():
                    self.copy(j, c).wait_send()

                @pl.when(jnp.logical_not(jnp.logical_and(self.own, self.slot == j)))
                def _():
                    self.arrival(j, c).wait_recv()


ROW_SEMS = sems((len(CHUNKS), GROUPS), (len(CHUNKS), GROUPS), 1)


class Exchange:
    def __init__(self, x_ref, out_ref, send, recv, local):
        me = lax.axis_index("dp")
        self.copies = [
            remote(x_ref.at[me ^ k], out_ref.at[me], send.at[k], recv.at[k], {"dp": me ^ k})
            for k in ORDER
        ]
        self.copies.append(pltpu.make_async_copy(x_ref.at[me], out_ref.at[me], local.at[0]))

    def start(self):
        for copy in self.copies:
            copy.start()

    def wait(self):
        for copy in self.copies:
            copy.wait()


DP_SEMS = sems(N_DP, N_DP, 1)


class Swap:
    def __init__(self, x_ref, out_ref, send, recv, local):
        me = lax.axis_index("dp")
        core = lax.rem(me, 2)
        self.copies = [
            remote(x_ref.at[1 - core], out_ref.at[core], send.at[0], recv.at[0], {"dp": me ^ 1}),
            pltpu.make_async_copy(x_ref.at[core], out_ref.at[core], local.at[0]),
        ]

    start = Exchange.start
    wait = Exchange.wait


SWAP_SEMS = sems(1, 1, 1)


class DirectScatter:
    def __init__(self, part_ref, got, send, recv):
        self.me = lax.axis_index("tensor")
        self.part, self.got = part_ref, got
        self.copies = [
            remote(
                part_ref.at[self.me ^ k], got.at[k], send.at[k], recv.at[k], {"tensor": self.me ^ k}
            )
            for k in STEPS
        ]

    def start(self):
        for copy in self.copies:
            copy.start()

    def total(self):
        value = self.part[self.me].astype(f32)
        for k, copy in zip(STEPS, self.copies):
            copy.wait_recv()
            value = value + self.got[k].astype(f32)
        return value

    def wait_send(self):
        for copy in self.copies:
            copy.wait_send()


class DirectGather:
    def __init__(self, mine, full_ref, send, recv, local):
        me = lax.axis_index("tensor")
        self.mine = mine
        self.copies = [
            remote(mine, full_ref.at[me], send.at[k], recv.at[k], {"tensor": me ^ k}) for k in STEPS
        ]
        self.copies.append(pltpu.make_async_copy(mine, full_ref.at[me], local.at[0]))

    def start(self, value):
        self.mine[...] = value.astype(bf16)
        for copy in self.copies:
            copy.start()

    def wait(self):
        for copy in self.copies:
            copy.wait()


def direct_scratch(rows, width):
    return [
        pltpu.VMEM((N_T, rows, width), bf16),
        pltpu.VMEM((rows, width), bf16),
    ] + sems(N_T, N_T, N_T, N_T, 1)


N_DIRECT = 7


def direct_parts(part_ref, full_ref, scratch):
    got, mine, send, recv, asend, arecv, local = scratch
    return DirectScatter(part_ref, got, send, recv), DirectGather(mine, full_ref, asend, arecv, local)


class Scatter:
    def __init__(self, part_ref, got, mid, last, send, recv):
        t = lax.axis_index("tensor")
        y, half = t % 4, t // 4
        self.part, self.got, self.mid, self.last = part_ref, got, mid, last
        self.slots = (4 * (1 - half) + y, t)
        self.copies = [
            [
                remote(
                    part_ref.at[slot ^ k],
                    got.at[a, k],
                    send.at[a, k],
                    recv.at[a, k],
                    {"tensor": t ^ k},
                )
                for k in (1, 3, 2)
            ]
            for a, slot in enumerate(self.slots)
        ]
        self.across = remote(mid, last, send.at[0, 0], recv.at[0, 0], {"tensor": t ^ 4})

    def start(self):
        for copies in self.copies:
            for copy in copies:
                copy.start()

    def over_y(self, a):
        value = self.part[self.slots[a]].astype(f32)
        for k, copy in zip((1, 3, 2), self.copies[a]):
            copy.wait_recv()
            value = value + self.got[a, k].astype(f32)
        return value

    def middle(self):
        self.mid[...] = self.over_y(0).astype(bf16)
        self.across.start()

    def total(self):
        value = self.over_y(1)
        self.across.wait_recv()
        return value + self.last[...].astype(f32)

    def wait_send(self):
        for copies in self.copies:
            for copy in copies:
                copy.wait_send()
        self.across.wait_send()


class Gather:
    def __init__(self, mine, full_ref, send, recv, local):
        t = lax.axis_index("tensor")
        self.mine = mine
        self.across = remote(
            mine, full_ref.at[t], send.at[0, 0], recv.at[0, 0], {"tensor": t ^ 4}
        )
        self.first = [
            remote(mine, full_ref.at[t], send.at[0, k], recv.at[0, k], {"tensor": t ^ k})
            for k in (1, 3, 2)
        ]
        self.second = [
            remote(
                full_ref.at[t ^ 4],
                full_ref.at[t ^ 4],
                send.at[1, k],
                recv.at[1, k],
                {"tensor": t ^ k},
            )
            for k in (1, 3, 2)
        ]
        self.own = pltpu.make_async_copy(mine, full_ref.at[t], local.at[0])

    def start(self, value):
        self.mine[...] = value.astype(bf16)
        for copy in [self.across] + self.first + [self.own]:
            copy.start()

    def relay(self):
        self.across.wait_recv()
        for copy in self.second:
            copy.start()

    def wait(self):
        self.across.wait_send()
        for copy in self.first + self.second + [self.own]:
            copy.wait()


JOIN_SEMS = sems((2, 4), (2, 4), (2, 4), (2, 4), 1)


def join_scratch(rows, width):
    return [
        pltpu.VMEM((2, 4, rows, width), bf16),
        pltpu.VMEM((rows, width), bf16),
        pltpu.VMEM((rows, width), bf16),
        pltpu.VMEM((rows, width), bf16),
    ] + JOIN_SEMS


N_JOIN = 9


def join_parts(part_ref, full_ref, scratch):
    got, mid, last, mine, send, recv, asend, arecv, local = scratch
    return Scatter(part_ref, got, mid, last, send, recv), Gather(mine, full_ref, asend, arecv, local)


class Sends:
    def __init__(self, messages, send, recv):
        self.copies = [
            remote(src, dst, send.at[i], recv.at[i], peer) for i, (src, dst, peer) in enumerate(messages)
        ]

    start = Exchange.start
    wait = Exchange.wait


def struct(shape, dtype):
    return jax.ShapeDtypeStruct(shape, dtype)


def column_sum(value):
    return jnp.sum(value, axis=0, keepdims=True)


def second_moment(value):
    return lax.rsqrt(jnp.mean(value * value, axis=1, keepdims=True) + EPSILON)


def gather_keys(k, v, q, number):
    tok, size = k.shape[1:]

    def kernel(k_ref, v_ref, q_ref, keys_ref, values_ref, pair_ref, send, recv, local, *more):
        me = lax.axis_index("dp")
        core = lax.rem(me, 2)
        greet(dp_peers())
        swap = Swap(q_ref, pair_ref, *more)
        swap.start()
        rows = pl.ds(pl.multiple_of(me * tok, tok), tok)
        copies = []
        for i, (own, full) in enumerate(((k_ref, keys_ref), (v_ref, values_ref))):
            for step in ORDER:
                head = core if step % 2 == 0 else 1 - core
                copies.append(
                    remote(
                        own.at[head],
                        full.at[rows],
                        send.at[i, step],
                        recv.at[i, step],
                        {"dp": me ^ step},
                    )
                )
            copies.append(pltpu.make_async_copy(own.at[core], full.at[rows], local.at[i]))
        for copy in copies:
            copy.start()
        swap.wait()
        for copy in copies:
            copy.wait()

    return pl.pallas_call(
        kernel,
        out_shape=(
            struct((N_DP * tok, size), bf16),
            struct((N_DP * tok, size), bf16),
            struct(q.shape, bf16),
        ),
        in_specs=[HBM] * 3,
        out_specs=(HBM,) * 3,
        scratch_shapes=sems((2, N_DP), (2, N_DP), 2) + SWAP_SEMS,
        compiler_params=comm_params(number),
        name="gather_keys",
        cost_estimate=cost(41),
    )(k, v, q)


def swap_cores(x, number):
    def kernel(x_ref, out_ref, *scratch):
        greet([{"dp": lax.axis_index("dp") ^ 1}])
        swap = Swap(x_ref, out_ref, *scratch)
        swap.start()
        swap.wait()

    return pl.pallas_call(
        kernel,
        out_shape=struct(x.shape, x.dtype),
        in_specs=[HBM],
        out_specs=HBM,
        scratch_shapes=SWAP_SEMS,
        compiler_params=comm_params(number),
        name="swap_cores",
        cost_estimate=cost(4),
    )(x)


def rows_out(xs, number):
    count = len(xs)

    def kernel(*refs):
        rows = [
            Rows(refs[i], refs[count + i], *refs[2 * count + 3 * i : 2 * count + 3 * i + 3])
            for i in range(count)
        ]
        greet([], rows[0])
        for one in rows:
            one.start()
        for one in rows:
            one.wait()

    return pl.pallas_call(
        kernel,
        out_shape=tuple(struct(x.shape, x.dtype) for x in xs),
        in_specs=[HBM] * count,
        out_specs=(HBM,) * count,
        scratch_shapes=ROW_SEMS * count,
        compiler_params=comm_params(number),
        name="rows_out",
        cost_estimate=cost(42),
    )(*xs)


def rows_back(xs, weights, number):
    count, n = len(xs), len(xs) + len(weights)

    def kernel(*refs):
        d = lax.axis_index("dp")
        scratch = refs[2 * n :]
        rows = [
            Rows(refs[i], refs[n + i], *scratch[3 * i : 3 * i + 3], back=True) for i in range(count)
        ]
        greet([{"dp": d ^ 1}], rows[0])
        sides = Sends(
            [
                (refs[i].at[chip, 1 - lax.rem(d, 2)], refs[n + i].at[chip], {"dp": d ^ 1})
                for i in range(count, n)
                for chip in range(8)
            ],
            *scratch[3 * count :],
        )
        for one in rows:
            one.start()
        sides.start()
        for one in rows:
            one.wait()
        sides.wait()

    return pl.pallas_call(
        kernel,
        out_shape=tuple(struct(x.shape, x.dtype) for x in xs)
        + tuple(struct((w.shape[0],) + w.shape[2:], w.dtype) for w in weights),
        in_specs=[HBM] * n,
        out_specs=(HBM,) * n,
        scratch_shapes=ROW_SEMS * count + sems(8 * len(weights), 8 * len(weights)),
        compiler_params=comm_params(number),
        name="rows_back",
        cost_estimate=cost(42),
    )(*xs, *weights)


def join_attn(part, layer_input, gain, number):
    _, rows, width = part.shape

    def kernel(part_ref, x_ref, gain_ref, full_ref, middle_ref, stats_ref, *scratch):
        greet(tensor_peers())
        scatter, gather = direct_parts(part_ref, full_ref, scratch)
        scatter.start()
        resid = x_ref[lax.axis_index("tensor")].astype(f32)
        attn_out = scatter.total()
        middle = resid + attn_out
        gather.start(middle * second_moment(middle) * gain_ref[...])
        middle_ref[...] = middle
        stats_ref[0:1] = column_sum(resid * resid)
        stats_ref[1:2] = column_sum(attn_out * attn_out)
        stats_ref[2:3] = column_sum(middle * middle)
        scatter.wait_send()
        gather.wait()

    return pl.pallas_call(
        kernel,
        out_shape=(struct(part.shape, bf16), struct((rows, width), f32), struct((8, width), f32)),
        in_specs=[VMEM] * 3,
        out_specs=(HBM, VMEM, VMEM),
        scratch_shapes=direct_scratch(rows, width),
        compiler_params=comm_params(number, LIMIT),
        name="join_attn",
        cost_estimate=cost(40),
    )(part, layer_input, gain)


def join_ffn(part, cotangent, middle, gain, weights, number):
    _, rows, width = part.shape
    n = len(weights)

    def kernel(part_ref, up_ref, middle_ref, gain_ref, *refs):
        w_refs, (full_ref, d_ref, sums_ref), got_refs = refs[:n], refs[n : n + 3], refs[n + 3 : 2 * n + 3]
        scratch = refs[2 * n + 3 :]
        d, z, _, _ = coordinates()
        greet(tensor_peers() + [{"dp": d ^ (4 * k)} for k in (1, 2, 3)])
        scatter, gather = direct_parts(part_ref, full_ref, scratch[:N_DIRECT])
        scatter.start()
        sides = Sends(
            [
                (w_ref.at[z ^ k], got_ref.at[k], {"dp": d ^ (4 * k)})
                for k in (1, 3, 2)
                for w_ref, got_ref in zip(w_refs, got_refs)
            ],
            *scratch[N_DIRECT:],
        )
        sides.start()
        middle = middle_ref[...]
        inv = second_moment(middle)
        d_normed = scatter.total()
        scaled = d_normed * gain_ref[...]
        d_middle = (
            up_ref[lax.axis_index("tensor")].astype(f32)
            + inv * scaled
            - middle * (inv * inv * inv) * jnp.mean(scaled * middle, axis=1, keepdims=True)
        )
        gather.start(d_middle)
        d_ref[...] = d_middle
        sums_ref[0:1] = column_sum(d_normed * middle * inv)
        scatter.wait_send()
        gather.wait()
        sides.wait()

    return pl.pallas_call(
        kernel,
        out_shape=(
            struct(part.shape, bf16),
            struct((rows, width), f32),
            struct((8, width), f32),
        )
        + tuple(struct(w.shape, w.dtype) for w in weights),
        in_specs=[VMEM] * 4 + [HBM] * n,
        out_specs=(HBM, VMEM, VMEM) + (HBM,) * n,
        scratch_shapes=direct_scratch(rows, width) + sems(3 * n, 3 * n),
        compiler_params=comm_params(number, LIMIT),
        name="join_ffn",
        cost_estimate=cost(50),
    )(part, cotangent, middle, gain, *weights)


def scatter_keys(dk, dv, out_part, dq, weights, number):
    n = len(weights)

    def kernel(dk_ref, dv_ref, part_ref, dq_ref, *refs):
        w_refs, (k_ref, v_ref, sum_ref, pair_ref), x_refs = refs[:n], refs[n : n + 4], refs[n + 4 : 2 * n + 4]
        scratch = refs[2 * n + 4 :]
        d = lax.axis_index("dp")
        greet(dp_peers())
        moves = [
            Exchange(dk_ref, k_ref, *scratch[:3]),
            Exchange(dv_ref, v_ref, *scratch[3:6]),
            Swap(dq_ref, pair_ref, *scratch[6:9]),
            Exchange(part_ref, sum_ref, *scratch[9:12]),
            Sends(
                [
                    (w_ref.at[1 - (d // 2) % 2], x_ref, {"dp": d ^ 2})
                    for w_ref, x_ref in zip(w_refs, x_refs)
                ],
                *scratch[12:],
            ),
        ]
        for move in moves:
            move.start()
        for move in moves:
            move.wait()

    return pl.pallas_call(
        kernel,
        out_shape=(
            struct(dk.shape, bf16),
            struct(dv.shape, bf16),
            struct(out_part.shape, out_part.dtype),
            struct(dq.shape, dq.dtype),
        )
        + tuple(struct(w.shape[1:], w.dtype) for w in weights),
        in_specs=[HBM] * (4 + n),
        out_specs=(HBM,) * (4 + n),
        scratch_shapes=DP_SEMS * 2 + SWAP_SEMS + DP_SEMS + sems(n, n),
        compiler_params=comm_params(number),
        name="scatter_keys",
        cost_estimate=cost(50),
    )(dk, dv, out_part, dq, *weights)


def join_tail(part, moe_part, layer_input, middle, d_middle, gain, qkv_part, pack, number):
    _, rows, width = part.shape
    small = pack.shape[1]

    def kernel(part_ref, moe_ref, x_ref, middle_ref, d_ref, gain_ref, qkv_ref, pack_ref, *refs):
        full_ref, out_ref, got_ref, one_ref, both_ref = refs[:5]
        scratch = refs[5:]
        greet(tensor_peers() + dp_peers())
        scatter, gather = join_parts(part_ref, full_ref, scratch[:N_JOIN])
        scatter_moe, gather_moe = join_parts(moe_ref, out_ref, scratch[N_JOIN : 2 * N_JOIN])
        scatter.start()
        scatter_moe.start()
        weights = Exchange(qkv_ref, got_ref, *scratch[2 * N_JOIN : 2 * N_JOIN + 3])
        weights.start()
        own, few, mine, more, send, recv, tsend, trecv = scratch[2 * N_JOIN + 3 :]
        me, t = lax.axis_index("dp"), lax.axis_index("tensor")
        resid = x_ref[t].astype(f32)
        inv = second_moment(resid)
        scatter.middle()
        d_normed = scatter.total()
        scaled = d_normed * gain_ref[...]
        gather.start(
            d_ref[...]
            + inv * scaled
            - resid * (inv * inv * inv) * jnp.mean(scaled * resid, axis=1, keepdims=True)
        )
        gain_grad = column_sum(d_normed * resid * inv)
        scatter_moe.middle()
        moe_out = scatter_moe.total()
        output = middle_ref[...] + moe_out
        gather_moe.start(output)

        def folded(value):
            row = column_sum(value)
            return sum(row[:, i * 128 : (i + 1) * 128] for i in range(width // 128))

        moe_row, out_row = folded(moe_out * moe_out), folded(output * output)
        own[...] = pack_ref[...]
        for i in range(N_DP):
            own[i, small - 3 : small - 2] = moe_row
            own[i, small - 2 : small - 1] = out_row
            own[i, small - 1 : small] = gain_grad[:, i * 128 : (i + 1) * 128]
        firsts = [
            remote(own.at[me ^ k], few.at[k], send.at[k], recv.at[k], {"dp": me ^ k})
            for k in range(1, N_DP)
        ]
        for copy in firsts:
            copy.start()
        gather.relay()
        gather_moe.relay()
        value = own[me]
        for k in range(1, N_DP):
            firsts[k - 1].wait_recv()
            value = value + few[k]
        one_ref[...] = value
        mine[...] = value
        seconds = [
            remote(mine, more.at[k], tsend.at[k], trecv.at[k], {"tensor": t ^ k}) for k in range(1, N_T)
        ]
        for copy in seconds:
            copy.start()
        for k in range(1, N_T):
            seconds[k - 1].wait_recv()
            value = value + more[k]
        both_ref[...] = value
        for copy in firsts + seconds:
            copy.wait_send()
        scatter.wait_send()
        scatter_moe.wait_send()
        gather.wait()
        gather_moe.wait()
        weights.wait()

    return pl.pallas_call(
        kernel,
        out_shape=(
            struct(part.shape, bf16),
            struct(part.shape, bf16),
            struct(qkv_part.shape, qkv_part.dtype),
            struct((small, 128), f32),
            struct((small, 128), f32),
        ),
        in_specs=[VMEM] * 6 + [HBM, VMEM],
        out_specs=(HBM, HBM, HBM, VMEM, VMEM),
        scratch_shapes=join_scratch(rows, width) * 2
        + DP_SEMS
        + [
            pltpu.VMEM((N_DP, small, 128), f32),
            pltpu.VMEM((N_DP, small, 128), f32),
            pltpu.VMEM((small, 128), f32),
            pltpu.VMEM((N_T, small, 128), f32),
        ]
        + sems(N_DP, N_DP, N_T, N_T),
        compiler_params=comm_params(number, LIMIT),
        name="join_tail",
        cost_estimate=cost(60),
    )(part, moe_part, layer_input, middle, d_middle, gain, qkv_part, pack)


KEYS = 256
NT = (((1,), (1,)), ((), ()))
TN = (((0,), (0,)), ((), ()))


def mm(a, b, dims=(((1,), (0,)), ((), ()))):
    return lax.dot_general(a, b, dims, preferred_element_type=f32)


def attend(queries, keys, values, codes, bounds):
    count, size = queries.shape
    stream = keys.shape[0]
    factor = size ** (-0.5) * math.log2(math.e)

    def kernel(q_ref, k_ref, v_ref, code_ref, bound_ref, low_ref, wide_ref, log_ref):
        q = q_ref[...]
        lowest, highest = bound_ref[0:1], bound_ref[1:2]

        def step(i, carry):
            peak, total, acc = carry
            rows = pl.ds(pl.multiple_of(i * KEYS, KEYS), KEYS)
            scores = mm(k_ref[rows], q, NT) * factor
            code = code_ref[rows][:, 0:1]
            seen = (code >= lowest) & (code <= highest)
            scores = jnp.where(seen, scores, NEG_FILL)
            new_peak = jnp.maximum(peak, jnp.max(scores, axis=0, keepdims=True))
            terms = jnp.exp2(scores - new_peak)
            shrink = jnp.exp2(peak - new_peak)
            total = total * shrink + jnp.sum(terms, axis=0, keepdims=True)
            acc = acc * shrink + mm(v_ref[rows], terms.astype(bf16), TN)
            return new_peak, total, acc

        peak, total, acc = lax.fori_loop(
            0,
            stream // KEYS,
            step,
            (
                jnp.full((1, count), NEG_FILL, f32),
                jnp.zeros((1, count), f32),
                jnp.zeros((size, count), f32),
            ),
        )
        out = (acc / total).T
        wide_ref[...] = out
        low_ref[...] = out.astype(bf16)
        log_ref[...] = jnp.broadcast_to(peak + jnp.log2(total), (8, count))

    return pl.pallas_call(
        kernel,
        out_shape=(struct((count, size), bf16), struct((count, size), f32), struct((8, count), f32)),
        in_specs=[VMEM] * 5,
        out_specs=(VMEM,) * 3,
        compiler_params=pltpu.CompilerParams(vmem_limit_bytes=LIMIT),
        name="attend",
        cost_estimate=cost(12),
    )(queries, keys, values, codes, bounds)


def attend_back(queries, keys, values, codes, bounds, wide, logs, d_heads):
    count, size = queries.shape
    stream = keys.shape[0]
    scale = size ** (-0.5)
    factor = scale * math.log2(math.e)

    def kernel(q_ref, k_ref, v_ref, code_ref, bound_ref, wide_ref, log_ref, d_ref, dq_ref, dk_ref, dv_ref):
        q, d_out = q_ref[...], d_ref[...]
        lowest, highest = bound_ref[0:1], bound_ref[1:2]
        log = log_ref[0:1]
        delta = jnp.sum((wide_ref[...] * d_out.astype(f32)).T, axis=0, keepdims=True)

        def step(i, acc):
            rows = pl.ds(pl.multiple_of(i * KEYS, KEYS), KEYS)
            k = k_ref[rows]
            scores = mm(k, q, NT) * factor
            code = code_ref[rows][:, 0:1]
            seen = (code >= lowest) & (code <= highest)
            probs = jnp.where(seen, jnp.exp2(scores - log), 0.0)
            d_probs = mm(v_ref[rows], d_out, NT)
            d_scores = (probs * (d_probs - delta)).astype(bf16)
            dv_ref[rows] = mm(probs.astype(bf16), d_out).astype(bf16)
            dk_ref[rows] = (mm(d_scores, q) * scale).astype(bf16)
            return acc + mm(k, d_scores, TN)

        acc = lax.fori_loop(0, stream // KEYS, step, jnp.zeros((size, count), f32))
        dq_ref[...] = (acc.T * scale).astype(bf16)

    return pl.pallas_call(
        kernel,
        out_shape=(struct((count, size), bf16), struct((stream, size), bf16), struct((stream, size), bf16)),
        in_specs=[VMEM] * 8,
        out_specs=(VMEM,) * 3,
        compiler_params=pltpu.CompilerParams(vmem_limit_bytes=LIMIT),
        name="attend_back",
        cost_estimate=cost(15),
    )(queries, keys, values, codes, bounds, wide, logs, d_heads)


def doc_layout(lengths, token_index):
    doc_ends = jnp.cumsum(lengths)
    starts = doc_ends - lengths
    seq_ids = jnp.sum((token_index[:, None] >= doc_ends[None, :]).astype(jnp.int32), axis=1)
    member = seq_ids[:, None] == jnp.arange(lengths.shape[0], dtype=jnp.int32)[None, :]
    begins = jnp.sum(jnp.where(member, starts[None, :], 0), axis=1)
    offsets = token_index - begins
    return (seq_ids, offsets, offsets // DBLOCK)


def rope_tables(offsets, head_dim):
    half_dim = head_dim // 2
    frequencies = jnp.exp(
        jnp.arange(half_dim, dtype=f32) * (-2.0 * math.log(THETA) / head_dim)
    )
    angles = offsets.astype(f32)[:, None] * frequencies[None, :]
    return (jnp.cos(angles)[:, None, :], jnp.sin(angles)[:, None, :])


def rotate(vectors, cosine, sine):
    half_dim = vectors.shape[-1] // 2
    front, back = vectors[..., :half_dim], vectors[..., half_dim:]
    return jnp.concatenate([front * cosine - back * sine, back * cosine + front * sine], axis=-1)


def silu_back(gate_part, up_part, d_hidden):
    sigmoid_gate = jax.nn.sigmoid(gate_part)
    d_gate = d_hidden * up_part * sigmoid_gate * (1.0 + gate_part * (1.0 - sigmoid_gate))
    d_up = d_hidden * gate_part * sigmoid_gate
    return d_gate, d_up


def dot(pattern, a, b):
    return jnp.einsum(pattern, a, b, preferred_element_type=f32)


def on_device(
    layer_input,
    doc_lengths,
    expert_ids,
    attn_gain,
    qkv_weight,
    qkv_bias,
    out_weight,
    ffn_gain,
    router_weight,
    shared_gate,
    shared_in,
    shared_out,
    expert_in,
    expert_out,
    cotangent,
):
    tok, width = layer_input.shape
    dp, tn = lax.axis_index("dp"), lax.axis_index("tensor")
    experts = router_weight.shape[1]
    head_dim = qkv_weight.shape[3]
    stream = tok * N_DP
    part_rows = tok // N_T
    score_scale = head_dim ** (-0.5)
    eff = expert_out.shape[1]

    def permute(x, bits):
        return lax.ppermute(x, "tensor", [(i, i ^ bits) for i in range(N_T)])

    pieces = range(GROUPS)
    all_in = [expert_in[0]] + [permute(expert_in[0], i) for i in pieces[1:]]
    all_out = [expert_out[0]] + [permute(expert_out[0], i) for i in pieces[1:]]

    hot = jnp.sum(
        (expert_ids[:, :, None] == jnp.arange(experts, dtype=jnp.int32)[None, None, :]).astype(f32),
        axis=1,
    )
    before = (jnp.arange(tok)[:, None] > jnp.arange(tok)[None, :]).astype(bf16)
    rank = dot("ts,se->te", before, hot.astype(bf16))
    place = jnp.where(hot > 0, rank, -1.0).astype(jnp.int32).T
    _, offset = route_plane()
    served = lax.dynamic_slice_in_dim(place, GROUPS * ((dp // 4) ^ offset), GROUPS, 0)
    places = (
        (served[:, None, :] == jnp.arange(SLOTS, dtype=jnp.int32)[None, :, None])
        .astype(bf16)
        .reshape(GROUPS * SLOTS, tok)
    )
    returned = lax.dynamic_index_in_dim(place.reshape(GROUPS, 4, tok), offset, 1, keepdims=False)
    places_back = (
        (returned[:, None, :] == jnp.arange(SLOTS, dtype=jnp.int32)[None, :, None])
        .astype(bf16)
        .reshape(GROUPS * SLOTS, tok)
    )
    by_group = (GROUPS, SLOTS, width)
    up_send = dot("rt,td->rd", places, cotangent).astype(bf16)

    local_index = dp * tok + jnp.arange(tok, dtype=jnp.int32)
    pair_index = (dp // 2) * (2 * tok) + jnp.arange(2 * tok, dtype=jnp.int32)
    every_index = jnp.arange(stream, dtype=jnp.int32)
    _, pos_local, _ = doc_layout(doc_lengths, local_index)
    seq_pair, _, blk_pair = doc_layout(doc_lengths, pair_index)
    seq_all, _, blk_all = doc_layout(doc_lengths, every_index)
    codes = jnp.broadcast_to((seq_all * CODE + blk_all)[:, None], (stream, 128))
    bounds = jnp.stack([seq_pair * CODE, seq_pair * CODE + blk_pair] + [seq_pair] * 6)
    cosine, sine = rope_tables(pos_local, head_dim)
    residual = layer_input.astype(f32)
    inv_first = lax.rsqrt(jnp.mean(residual * residual, axis=1, keepdims=True) + EPSILON)
    normed_one = (residual * inv_first * attn_gain).astype(bf16)
    projected = dot("td,dshe->tshe", normed_one, qkv_weight) + qkv_bias.astype(f32)[None]
    q_own = rotate(projected[:, 0], cosine, sine).astype(bf16).transpose(1, 0, 2)
    k_own = rotate(projected[:, 1], cosine, sine).astype(bf16).transpose(1, 0, 2)
    v_own = projected[:, 2].astype(bf16).transpose(1, 0, 2)
    keys, values, queries = gather_keys(k_own, v_own, q_own, 1)
    queries = queries.reshape(2 * tok, head_dim)

    pair_out, pair_wide, logs = attend(queries, keys, values, codes, bounds)
    heads_out = swap_cores(pair_out.reshape(2, tok, head_dim), 3)
    heads_out = jnp.concatenate([heads_out[0], heads_out[1]], axis=1)
    out_flat = out_weight.reshape(2 * head_dim, width)
    attn_part = dot("qf,fd->qd", heads_out, out_flat).astype(bf16)
    by_slice = (N_T, part_rows, width)
    normed_two, middle, stats_one = join_attn(
        attn_part.reshape(by_slice), layer_input.reshape(by_slice), ffn_gain.reshape(1, width), 4
    )
    normed_two = normed_two.reshape(tok, width)

    row_send = dot("rt,td->rd", places, normed_two).astype(bf16)
    exp_rows, up_rows = rows_out([row_send.reshape(by_group), up_send.reshape(by_group)], 5)
    exp_rows, up_rows = exp_rows.reshape(-1, width), up_rows.reshape(-1, width)

    gate_value = jax.nn.sigmoid(dot("td,d->t", normed_two, shared_gate))
    shared_gu = dot("td,dsf->tsf", normed_two, shared_in)
    shared_hidden = (jax.nn.silu(shared_gu[:, 0]) * shared_gu[:, 1]).astype(bf16)
    shared_part = dot("tf,fd->td", shared_hidden, shared_out)
    upstream = cotangent.astype(f32)
    d_shared = (gate_value[:, None] * upstream).astype(bf16)
    gate_partial = jnp.sum(upstream * shared_part, axis=1) * gate_value * (1.0 - gate_value)
    d_shared_hidden = dot("td,fd->tf", d_shared, shared_out)
    d_gate, d_up = silu_back(shared_gu[:, 0], shared_gu[:, 1], d_shared_hidden)
    d_shared_gu = jnp.stack([d_gate, d_up], axis=1).astype(bf16)
    shared_out_part = dot("td,tf->df", d_shared, shared_hidden).astype(bf16)
    shared_in_part = dot("td,tf->df", normed_two, d_shared_gu.reshape(tok, -1)).astype(bf16)
    shared_d_normed = (
        dot("tsf,dsf->td", d_shared_gu, shared_in)
        + gate_partial[:, None] * shared_gate.astype(f32)[None, :]
    )
    gate_vec_part = jnp.einsum(
        "t,td->d", gate_partial, normed_two.astype(f32), precision=lax.Precision.HIGHEST
    )

    w_in = jnp.concatenate(all_in, axis=2)
    w_out = jnp.concatenate(all_out, axis=0)
    row_logits = dot("rd,de->re", exp_rows, router_weight)
    row_probs = jax.nn.softmax(row_logits, axis=1)
    own_expert = (jnp.arange(experts, dtype=jnp.int32) == dp).astype(f32)[None, :]
    row_gate = jnp.sum(row_probs * own_expert, axis=1, keepdims=True)
    expert_gu = dot("rd,dsf->rsf", exp_rows, w_in)
    expert_hidden = (jax.nn.silu(expert_gu[:, 0]) * expert_gu[:, 1]).astype(bf16)
    expert_part = (row_gate * dot("rf,fd->rd", expert_hidden, w_out)).astype(bf16)

    raw_hidden = dot("rd,fd->rf", up_rows, w_out)
    d_gate_row = jnp.sum(expert_hidden.astype(f32) * raw_hidden, axis=1, keepdims=True)
    d_row_logits = (d_gate_row * row_gate * (own_expert - row_probs)).astype(bf16)
    d_gate, d_up = silu_back(expert_gu[:, 0], expert_gu[:, 1], row_gate * raw_hidden)
    d_expert_gu = jnp.stack([d_gate, d_up], axis=1).astype(bf16)
    d_rows = (
        dot("rsf,dsf->rd", d_expert_gu, w_in) + dot("re,de->rd", d_row_logits, router_weight)
    ).astype(bf16)
    router_part = dot("re,rd->ed", d_row_logits, exp_rows)
    gated_hidden = (expert_hidden.astype(f32) * row_gate).astype(bf16)

    def piece_grads(i):
        units = slice(i * eff, (i + 1) * eff)
        return (
            dot("rd,rsf->dsf", exp_rows, d_expert_gu[:, :, units]),
            dot("rf,rd->fd", gated_hidden[:, units], up_rows),
        )

    sent = [tuple(g.astype(bf16) for g in piece_grads(i)) for i in pieces[1:]]

    def sum_of(own, other):
        return (own.astype(f32) + other.astype(f32)).astype(bf16)

    by_chip = [
        g.reshape(8, 2, width // N_DP, -1) for g in (shared_in_part, shared_out_part)
    ]
    back_grads, back_out, *got = rows_back(
        [d_rows.reshape(by_group), expert_part.reshape(by_group)], by_chip, 6
    )
    core, z_index, x_index = dp % 2, dp // 4, (dp // 2) % 2

    def pick(x, index, axis=0):
        return lax.dynamic_index_in_dim(x, index, axis, keepdims=False)

    by_z = [
        sum_of(pick(own, core, 1), other).reshape(4, 2, width // N_DP, -1)
        for own, other in zip(by_chip, got)
    ]

    def combine(rows):
        return dot("rt,rd->td", places_back, rows.reshape(-1, width))

    d_normed_part = (shared_d_normed + combine(back_grads)).astype(bf16)
    d_attn, d_middle, stats_two, *got = join_ffn(
        d_normed_part.reshape(by_slice),
        cotangent.reshape(by_slice),
        middle,
        ffn_gain.reshape(1, width),
        by_z,
        7,
    )
    d_attn, sent = lax.optimization_barrier((d_attn, sent))
    received = [tuple(permute(g, i) for g in pair) for i, pair in zip(pieces[1:], sent)]
    by_x = [
        (pick(own, z_index).astype(f32) + sum(other[k].astype(f32) for k in (1, 2, 3))).astype(bf16)
        for own, other in zip(by_z, got)
    ]
    d_attn = d_attn.reshape(tok, width)
    moe_part = (gate_value[:, None] * shared_part + combine(back_out)).astype(bf16)

    outproj_part = dot("qd,qf->df", d_attn, heads_out).astype(bf16)
    d_heads = dot("qd,fd->qf", d_attn, out_flat).astype(bf16)
    d_heads = jnp.stack([d_heads[:, :head_dim], d_heads[:, head_dim:]])
    d_heads = swap_cores(d_heads, 8).reshape(2 * tok, head_dim)
    d_queries, d_keys, d_values = attend_back(
        queries, keys, values, codes, bounds, pair_wide, logs, d_heads
    )
    got_k, got_v, got_out_part, d_queries, *got = scatter_keys(
        d_keys.reshape(N_DP, tok, head_dim),
        d_values.reshape(N_DP, tok, head_dim),
        outproj_part.reshape(N_DP, width // N_DP, -1),
        d_queries.reshape(2, tok, head_dim),
        by_x,
        9,
    )
    got_k, received = lax.optimization_barrier((got_k, received))
    shared_in_grad, shared_out_grad = [
        pick(own, x_index).astype(f32) + other.astype(f32) for own, other in zip(by_x, got)
    ]
    outproj_grad = jnp.sum(got_out_part.astype(f32), axis=0)
    def summed(x):
        x = jnp.sum(x.astype(f32).reshape(8, 2, tok, head_dim), axis=0)
        return x[0], x[1]

    cosine, sine = cosine[:, 0], sine[:, 0]
    d_proj = jnp.concatenate(
        [rotate(d_queries[h].astype(f32), cosine, -sine) for h in range(2)]
        + [rotate(x, cosine, -sine) for x in summed(got_k)]
        + list(summed(got_v)),
        axis=1,
    ).astype(bf16)
    d_normed_one = dot("tf,df->td", d_proj, qkv_weight.reshape(width, -1)).astype(bf16)
    qkv_part = dot("td,tf->df", normed_one, d_proj).astype(bf16)
    bias_part = jnp.sum(d_proj.astype(f32), axis=0)

    def slices(row):
        return row.reshape(-1, N_DP, 128).transpose(1, 0, 2)

    three = jnp.sum(stats_one[:3], axis=1)
    pack = jnp.concatenate(
        [
            slices(router_part),
            slices(gate_vec_part),
            slices(stats_two[0]),
            jnp.broadcast_to(jnp.pad(three, (0, 125))[None, None], (N_DP, 1, 128)),
            jnp.pad(
                bias_part.reshape(6, N_DP, 8).transpose(1, 0, 2).reshape(N_DP, 1, 48),
                ((0, 0), (0, 4), (0, 80)),
            ),
        ],
        axis=1,
    )
    input_grad, output, got_qkv, over_dp, over_both = join_tail(
        d_normed_one.reshape(by_slice),
        moe_part.reshape(by_slice),
        layer_input.reshape(by_slice),
        middle,
        d_middle,
        attn_gain.reshape(1, width),
        qkv_part.reshape(N_DP, width // N_DP, -1),
        pack,
        10,
    )
    bias_grad = over_dp[19, :48].reshape(3, 2, 8)
    five = jnp.concatenate([over_both[18, :3], jnp.sum(over_both[21:23], axis=1)])
    rms_stats = jnp.sqrt(five / (stream * width))
    qkv_grad = jnp.sum(got_qkv.astype(f32), axis=0)

    expert_in_grad, expert_out_grad = piece_grads(0)
    for got_in, got_out in received:
        expert_in_grad = expert_in_grad + got_in.astype(f32)
        expert_out_grad = expert_out_grad + got_out.astype(f32)

    return (
        output.reshape(tok, width),
        input_grad.reshape(tok, width).astype(f32),
        qkv_grad.reshape(width // N_DP, 3, 2, head_dim),
        bias_grad,
        outproj_grad.T.reshape(2, head_dim, width // N_DP),
        over_both[23],
        over_both[17],
        over_both[:16].T,
        over_both[16],
        shared_in_grad.reshape(width // N_DP, 2, -1),
        shared_out_grad.T,
        expert_in_grad[None],
        expert_out_grad[None],
        rms_stats,
    )


def solution(mesh):
    in_specs = (
        P("dp", None),
        P(),
        P("dp", None),
        P(),
        P(None, None, "tensor", None),
        P(None, "tensor", None),
        P("tensor", None, None),
        P(),
        P(),
        P(),
        P(None, None, "tensor"),
        P("tensor", None),
        P("dp", None, None, "tensor"),
        P("dp", "tensor", None),
        P("dp", None),
    )
    out_specs = (
        P("dp", None),
        P("dp", None),
        P("dp", None, "tensor", None),
        P(None, "tensor", "dp"),
        P("tensor", None, "dp"),
        P("dp"),
        P("dp"),
        P("dp", None),
        P("dp"),
        P("dp", None, "tensor"),
        P("tensor", "dp"),
        P("dp", None, None, "tensor"),
        P("dp", "tensor", None),
        P(),
    )
    return jax.shard_map(
        on_device, mesh=mesh, in_specs=in_specs, out_specs=out_specs, check_vma=False
    )
```

```python
import math

import jax
import jax.numpy as jnp
from jax import lax
from jax.experimental import pallas as pl
from jax.experimental.pallas import tpu as pltpu
from jax.sharding import PartitionSpec as P

DBLOCK = 256
EPSILON = 1e-06
THETA = 1000000.0
NEG_FILL = -1e30
MESH = pl.DeviceIdType.MESH
f32 = jnp.float32
bf16 = jnp.bfloat16
N_DP = 16
N_T = 8
SLOTS = 112
LIMIT = 48 * 1024 * 1024
CODE = 1 << 16

HBM = pl.BlockSpec(memory_space=pl.ANY)
VMEM = pl.BlockSpec(memory_space=pltpu.VMEM)


def greet(peers, more=None):
    barrier = pltpu.get_barrier_semaphore()
    for peer in peers:
        pl.semaphore_signal(barrier, inc=1, device_id=peer, device_id_type=MESH)
    count = len(peers)
    if more is not None:
        count = count + more.greet()
    pl.semaphore_wait(barrier, count)


def remote(src, dst, send, recv, device):
    return pltpu.make_async_remote_copy(
        src_ref=src,
        dst_ref=dst,
        send_sem=send,
        recv_sem=recv,
        device_id=device,
        device_id_type=MESH,
    )


def dma(*shape):
    return pltpu.SemaphoreType.DMA(shape)


def cost(micros):
    return pl.CostEstimate(flops=0, bytes_accessed=int(micros * 3e6), transcendentals=0)


def comm_params(number, limit=None):
    return pltpu.CompilerParams(
        collective_id=number, has_side_effects=True, vmem_limit_bytes=limit
    )


NT = (((1,), (1,)), ((), ()))
TN = (((0,), (0,)), ((), ()))


def mm(a, b, dims=(((1,), (0,)), ((), ()))):
    return lax.dot_general(a, b, dims, preferred_element_type=f32)


GROUPS = 4
ORDER = (4, 12, 2, 5, 13, 3, 8, 6, 14, 9, 7, 15, 10, 11, 1)
STEPS = (1, 3, 2, 4, 5, 7, 6)
CHUNKS = ((0, 48), (48, 64))


def sems(*counts):
    return [dma(*c) if isinstance(c, tuple) else dma(c) for c in counts]


def dp_peers():
    me = lax.axis_index("dp")
    return [{"dp": me ^ k} for k in range(1, N_DP)]


def tensor_peers():
    me = lax.axis_index("tensor")
    return [{"tensor": me ^ k} for k in range(1, N_T)]


def coordinates():
    d, t = lax.axis_index("dp"), lax.axis_index("tensor")
    return d, d // 4, t // 4, t % 4


def route_plane():
    d, z, _, y = coordinates()
    plane = 2 * ((z + d // 2) % 2) + d % 2
    return plane, y ^ plane


class Rows:
    def __init__(self, x_ref, out_ref, send, recv, local, back=False):
        self.x, self.out, self.send, self.recv, self.local, self.back = x_ref, out_ref, send, recv, local, back
        d, z, half, y = coordinates()
        plane, offset = route_plane()
        if back:
            experts = [{"dp": 4 * k + offset, "tensor": 4 * half + plane} for k in range(GROUPS)]
            target = y ^ (d % 4)
        else:
            experts = [{"dp": 4 * (z ^ offset) + j, "tensor": 4 * half + plane} for j in range(GROUPS)]
        groups = [
            {
                "dp": 4 * g + 2 * ((y // 2 + g) % 2) + y % 2,
                "tensor": 4 * half + (target if back else y ^ g ^ z),
            }
            for g in range(GROUPS)
        ]
        self.peers, self.sources = (groups, experts) if back else (experts, groups)
        self.slot = z
        self.mine = z if back else d % 4
        self.own = offset == 0
        if back:
            self.own = jnp.logical_and(self.own, d % 4 == 0)
        self.d = d

    def is_own(self, j):
        return jnp.logical_and(self.own, self.mine == j)

    def greet(self):
        barrier = pltpu.get_barrier_semaphore()
        for j in range(GROUPS):
            source = self.sources[j]

            @pl.when(jnp.logical_not(jnp.logical_and(self.own, self.slot == j)))
            def _():
                pl.semaphore_signal(barrier, inc=1, device_id=source, device_id_type=MESH)

        return GROUPS - self.own.astype(jnp.int32)

    def copy(self, j, c):
        rows = pl.ds(*CHUNKS[c])
        return remote(
            self.x.at[j, rows],
            self.out.at[self.slot, rows],
            self.send.at[c, j],
            self.recv.at[c, self.slot],
            self.peers[j],
        )

    def arrival(self, j, c):
        rows = pl.ds(*CHUNKS[c])
        return remote(
            self.x.at[j, rows],
            self.out.at[j, rows],
            self.send.at[c, j],
            self.recv.at[c, j],
            self.peers[j],
        )

    def inside(self):
        return pltpu.make_async_copy(self.x.at[self.mine], self.out.at[self.slot], self.local.at[0])

    def start(self):
        for c in range(len(CHUNKS)):
            for j in range(GROUPS):

                @pl.when(jnp.logical_not(self.is_own(j)))
                def _():
                    self.copy(j, c).start()

        @pl.when(self.own)
        def _():
            self.inside().start()

    def wait(self):
        @pl.when(self.own)
        def _():
            self.inside().wait()

        for c in range(len(CHUNKS)):
            for j in range(GROUPS):

                @pl.when(jnp.logical_not(self.is_own(j)))
                def _():
                    self.copy(j, c).wait_send()

                @pl.when(jnp.logical_not(jnp.logical_and(self.own, self.slot == j)))
                def _():
                    self.arrival(j, c).wait_recv()


ROW_SEMS = sems((len(CHUNKS), GROUPS), (len(CHUNKS), GROUPS), 1)


class Exchange:
    def __init__(self, x_ref, out_ref, send, recv, local):
        me = lax.axis_index("dp")
        self.copies = [
            remote(x_ref.at[me ^ k], out_ref.at[me], send.at[k], recv.at[k], {"dp": me ^ k})
            for k in ORDER
        ]
        self.copies.append(pltpu.make_async_copy(x_ref.at[me], out_ref.at[me], local.at[0]))

    def start(self):
        for copy in self.copies:
            copy.start()

    def wait(self):
        for copy in self.copies:
            copy.wait()


DP_SEMS = sems(N_DP, N_DP, 1)


class Swap:
    def __init__(self, x_ref, out_ref, send, recv, local):
        me = lax.axis_index("dp")
        core = lax.rem(me, 2)
        self.copies = [
            remote(x_ref.at[1 - core], out_ref.at[core], send.at[0], recv.at[0], {"dp": me ^ 1}),
            pltpu.make_async_copy(x_ref.at[core], out_ref.at[core], local.at[0]),
        ]

    start = Exchange.start
    wait = Exchange.wait


SWAP_SEMS = sems(1, 1, 1)


class DirectScatter:
    def __init__(self, part_ref, got, send, recv):
        self.me = lax.axis_index("tensor")
        self.part, self.got = part_ref, got
        self.copies = [
            remote(
                part_ref.at[self.me ^ k], got.at[k], send.at[k], recv.at[k], {"tensor": self.me ^ k}
            )
            for k in STEPS
        ]

    def start(self):
        for copy in self.copies:
            copy.start()

    def total(self):
        value = self.part[self.me].astype(f32)
        for k, copy in zip(STEPS, self.copies):
            copy.wait_recv()
            value = value + self.got[k].astype(f32)
        return value

    def wait_send(self):
        for copy in self.copies:
            copy.wait_send()


class DirectGather:
    def __init__(self, mine, full_ref, send, recv, local):
        me = lax.axis_index("tensor")
        self.mine = mine
        self.copies = [
            remote(mine, full_ref.at[me], send.at[k], recv.at[k], {"tensor": me ^ k}) for k in STEPS
        ]
        self.copies.append(pltpu.make_async_copy(mine, full_ref.at[me], local.at[0]))

    def start(self, value):
        self.mine[...] = value.astype(bf16)
        for copy in self.copies:
            copy.start()

    def wait(self):
        for copy in self.copies:
            copy.wait()


def direct_scratch(rows, width):
    return [
        pltpu.VMEM((N_T, rows, width), bf16),
        pltpu.VMEM((rows, width), bf16),
    ] + sems(N_T, N_T, N_T, N_T, 1)


N_DIRECT = 7


def direct_parts(part_ref, full_ref, scratch):
    got, mine, send, recv, asend, arecv, local = scratch
    return DirectScatter(part_ref, got, send, recv), DirectGather(mine, full_ref, asend, arecv, local)


class Scatter:
    def __init__(self, part_ref, got, mid, last, send, recv):
        t = lax.axis_index("tensor")
        y, half = t % 4, t // 4
        self.part, self.got, self.mid, self.last = part_ref, got, mid, last
        self.slots = (4 * (1 - half) + y, t)
        self.copies = [
            [
                remote(
                    part_ref.at[slot ^ k],
                    got.at[a, k],
                    send.at[a, k],
                    recv.at[a, k],
                    {"tensor": t ^ k},
                )
                for k in (1, 3, 2)
            ]
            for a, slot in enumerate(self.slots)
        ]
        self.across = remote(mid, last, send.at[0, 0], recv.at[0, 0], {"tensor": t ^ 4})

    def start(self):
        for copies in self.copies:
            for copy in copies:
                copy.start()

    def over_y(self, a):
        value = self.part[self.slots[a]].astype(f32)
        for k, copy in zip((1, 3, 2), self.copies[a]):
            copy.wait_recv()
            value = value + self.got[a, k].astype(f32)
        return value

    def middle(self):
        self.mid[...] = self.over_y(0).astype(bf16)
        self.across.start()

    def total(self):
        value = self.over_y(1)
        self.across.wait_recv()
        return value + self.last[...].astype(f32)

    def wait_send(self):
        for copies in self.copies:
            for copy in copies:
                copy.wait_send()
        self.across.wait_send()


class Gather:
    def __init__(self, mine, full_ref, send, recv, local):
        t = lax.axis_index("tensor")
        self.mine = mine
        self.across = remote(
            mine, full_ref.at[t], send.at[0, 0], recv.at[0, 0], {"tensor": t ^ 4}
        )
        self.first = [
            remote(mine, full_ref.at[t], send.at[0, k], recv.at[0, k], {"tensor": t ^ k})
            for k in (1, 3, 2)
        ]
        self.second = [
            remote(
                full_ref.at[t ^ 4],
                full_ref.at[t ^ 4],
                send.at[1, k],
                recv.at[1, k],
                {"tensor": t ^ k},
            )
            for k in (1, 3, 2)
        ]
        self.own = pltpu.make_async_copy(mine, full_ref.at[t], local.at[0])

    def start(self, value):
        self.mine[...] = value.astype(bf16)
        for copy in [self.across] + self.first + [self.own]:
            copy.start()

    def relay(self):
        self.across.wait_recv()
        for copy in self.second:
            copy.start()

    def wait(self):
        self.across.wait_send()
        for copy in self.first + self.second + [self.own]:
            copy.wait()


JOIN_SEMS = sems((2, 4), (2, 4), (2, 4), (2, 4), 1)


def join_scratch(rows, width):
    return [
        pltpu.VMEM((2, 4, rows, width), bf16),
        pltpu.VMEM((rows, width), bf16),
        pltpu.VMEM((rows, width), bf16),
        pltpu.VMEM((rows, width), bf16),
    ] + JOIN_SEMS


N_JOIN = 9


def join_parts(part_ref, full_ref, scratch):
    got, mid, last, mine, send, recv, asend, arecv, local = scratch
    return Scatter(part_ref, got, mid, last, send, recv), Gather(mine, full_ref, asend, arecv, local)


class Sends:
    def __init__(self, messages, send, recv):
        self.copies = [
            remote(src, dst, send.at[i], recv.at[i], peer) for i, (src, dst, peer) in enumerate(messages)
        ]

    start = Exchange.start
    wait = Exchange.wait


def struct(shape, dtype):
    return jax.ShapeDtypeStruct(shape, dtype)


def column_sum(value):
    return jnp.sum(value, axis=0, keepdims=True)


def second_moment(value):
    return lax.rsqrt(jnp.mean(value * value, axis=1, keepdims=True) + EPSILON)


def gather_keys(k, v, q, number):
    tok, size = k.shape[1:]

    def kernel(k_ref, v_ref, q_ref, keys_ref, values_ref, pair_ref, send, recv, local, *more):
        me = lax.axis_index("dp")
        core = lax.rem(me, 2)
        greet(dp_peers())
        swap = Swap(q_ref, pair_ref, *more)
        swap.start()
        rows = pl.ds(pl.multiple_of(me * tok, tok), tok)
        copies = []
        for i, (own, full) in enumerate(((k_ref, keys_ref), (v_ref, values_ref))):
            for step in ORDER:
                head = core if step % 2 == 0 else 1 - core
                copies.append(
                    remote(
                        own.at[head],
                        full.at[rows],
                        send.at[i, step],
                        recv.at[i, step],
                        {"dp": me ^ step},
                    )
                )
            copies.append(pltpu.make_async_copy(own.at[core], full.at[rows], local.at[i]))
        for copy in copies:
            copy.start()
        swap.wait()
        for copy in copies:
            copy.wait()

    return pl.pallas_call(
        kernel,
        out_shape=(
            struct((N_DP * tok, size), bf16),
            struct((N_DP * tok, size), bf16),
            struct(q.shape, bf16),
        ),
        in_specs=[HBM] * 3,
        out_specs=(HBM,) * 3,
        scratch_shapes=sems((2, N_DP), (2, N_DP), 2) + SWAP_SEMS,
        compiler_params=comm_params(number),
        name="gather_keys",
        cost_estimate=cost(41),
    )(k, v, q)


def swap_cores(x, number):
    def kernel(x_ref, out_ref, *scratch):
        greet([{"dp": lax.axis_index("dp") ^ 1}])
        swap = Swap(x_ref, out_ref, *scratch)
        swap.start()
        swap.wait()

    return pl.pallas_call(
        kernel,
        out_shape=struct(x.shape, x.dtype),
        in_specs=[HBM],
        out_specs=HBM,
        scratch_shapes=SWAP_SEMS,
        compiler_params=comm_params(number),
        name="swap_cores",
        cost_estimate=cost(4),
    )(x)


def sigmoid(x):
    return 1.0 / (1.0 + jnp.exp(-x))


TILE = 176


def shared_expert(x_ref, up_ref, in_ref, out_ref, vec_ref, part_ref, d_ref, grads_ref, row_ref, low_ref):
    hidden = out_ref.shape[0]
    x = x_ref[...]
    vec = vec_ref[...]
    gate = sigmoid(jnp.sum(x.astype(f32) * vec, axis=1, keepdims=True))
    low_ref[...] = (gate * up_ref[...].astype(f32)).astype(bf16)
    part_ref[...] = jnp.zeros_like(part_ref)
    d_ref[...] = jnp.zeros_like(d_ref)

    def tile(i, carry):
        rows = [pl.ds(pl.multiple_of(i * TILE + k * hidden, 16), TILE) for k in range(3)]
        w_gate, w_up, w_out = in_ref[rows[0]], in_ref[rows[1]], out_ref[rows[0]]
        x, d_out = x_ref[...], low_ref[...]
        gate_part = mm(w_gate, x, NT)
        up_part = mm(w_up, x, NT)
        sig = sigmoid(gate_part)
        act = gate_part * sig
        unit = (act * up_part).astype(bf16)
        d_unit = mm(w_out, d_out, NT)
        d_gate = (d_unit * up_part * sig * (1.0 + gate_part * (1.0 - sig))).astype(bf16)
        d_up = (d_unit * act).astype(bf16)

        def block(j, carry):
            cols = pl.ds(pl.multiple_of(j * 256, 256), 256)
            xs, ds = x_ref[:, cols], low_ref[:, cols]
            part_ref[:, cols] += mm(unit, out_ref[rows[0], cols], TN)
            d_ref[:, cols] += mm(d_gate, in_ref[rows[0], cols], TN) + mm(d_up, in_ref[rows[1], cols], TN)
            for k, grad in enumerate((mm(d_gate, xs), mm(d_up, xs), mm(unit, ds))):
                grad = grad.astype(bf16)
                grads_ref[j, 0, rows[k]] = grad[:, :128]
                grads_ref[j, 1, rows[k]] = grad[:, 128:]
            return carry

        return lax.fori_loop(0, x.shape[1] // 256, block, carry)

    lax.fori_loop(0, hidden // TILE, tile, 0)
    total = part_ref[...]
    d_logit = jnp.sum(up_ref[...].astype(f32) * total, axis=1, keepdims=True) * gate * (1.0 - gate)
    part_ref[...] = gate * total
    d_ref[...] += d_logit * vec
    row_ref[...] = column_sum(d_logit * x_ref[...].astype(f32))


def rows_out(xs, tokens, upstream, w_in, w_out, vec, number):
    count = len(xs)
    tok, width = tokens.shape
    hidden = w_out.shape[0]

    def kernel(*refs):
        n_in, n_out = count + 5, count + 4
        outs = refs[n_in : n_in + n_out]
        low = refs[n_in + n_out]
        scratch = refs[n_in + n_out + 1 :]
        rows = [Rows(refs[i], outs[i], *scratch[3 * i : 3 * i + 3]) for i in range(count)]
        greet([], rows[0])
        for one in rows:
            one.start()
        shared_expert(*refs[count:n_in], *outs[count:], low)
        for one in rows:
            one.wait()

    return pl.pallas_call(
        kernel,
        out_shape=tuple(struct(x.shape, x.dtype) for x in xs)
        + (
            struct((tok, width), f32),
            struct((tok, width), f32),
            struct((8, 2, 3 * hidden, 128), bf16),
            struct((1, width), f32),
        ),
        in_specs=[HBM] * count + [VMEM] * 5,
        out_specs=(HBM,) * count + (VMEM,) * 4,
        scratch_shapes=[pltpu.VMEM((tok, width), bf16)] + ROW_SEMS * count,
        compiler_params=comm_params(number, LIMIT),
        name="rows_out",
        cost_estimate=cost(45),
    )(*xs, tokens, upstream, w_in, w_out, vec)


def routed_expert(x, up, weights, router, own):
    rows, width = x.shape
    units = weights[0].shape[0] // 3

    def kernel(x_ref, up_ref, w0, w1, w2, w3, router_ref, own_ref, *refs):
        out_ref, d_ref, dgu_ref, unit_ref, router_grad_ref, w_ref, out_acc, d_acc, sem = refs
        loads = [
            pltpu.make_async_copy(w, w_ref.at[i], sem.at[i]) for i, w in enumerate((w0, w1, w2, w3))
        ]
        for load in loads:
            load.start()
        own = own_ref[:, 0:1]
        logits = mm(router_ref[...], x_ref[...], NT)
        terms = jnp.exp(logits - jnp.max(logits, axis=0, keepdims=True))
        probs = terms / jnp.sum(terms, axis=0, keepdims=True)
        gate = jnp.sum(probs * own, axis=0, keepdims=True)
        out_acc[...] = jnp.zeros_like(out_acc)
        d_acc[...] = jnp.zeros_like(d_acc)
        for load in loads:
            load.wait()

        def piece(i, d_gate_row):
            w = w_ref.at[i]
            gate_part = mm(w[0:units], x_ref[...], NT)
            up_part = mm(w[units : 2 * units], x_ref[...], NT)
            raw = mm(w[2 * units : 3 * units], up_ref[...], NT)
            sig = sigmoid(gate_part)
            act = gate_part * sig
            unit = (act * up_part).astype(bf16).astype(f32)
            d_unit = gate * raw
            gated = (unit * gate).astype(bf16)
            d_gate = (d_unit * up_part * sig * (1.0 + gate_part * (1.0 - sig))).astype(bf16)
            d_up = (d_unit * act).astype(bf16)
            unit_ref[i] = gated
            dgu_ref[i, 0:units] = d_gate
            dgu_ref[i, units : 2 * units] = d_up

            def block(j, carry):
                cols = pl.ds(pl.multiple_of(j * 512, 512), 512)
                out_acc[:, cols] += mm(gated, w_ref[i, 2 * units : 3 * units, cols], TN)
                d_acc[:, cols] += mm(d_gate, w_ref[i, 0:units, cols], TN) + mm(
                    d_up, w_ref[i, units : 2 * units, cols], TN
                )
                return carry

            lax.fori_loop(0, width // 512, block, 0)
            return d_gate_row + jnp.sum(unit * raw, axis=0, keepdims=True)

        d_gate_row = lax.fori_loop(0, GROUPS, piece, jnp.zeros((1, rows), f32))
        d_logits = (d_gate_row * gate * (own - probs)).astype(bf16)
        router_grad_ref[...] = mm(d_logits, x_ref[...])
        out_ref[...] = out_acc[...].astype(bf16)
        d_ref[...] = (d_acc[...] + mm(d_logits, router_ref[...], TN)).astype(bf16)

    return pl.pallas_call(
        kernel,
        out_shape=(
            struct((rows, width), bf16),
            struct((rows, width), bf16),
            struct((GROUPS, 2 * units, rows), bf16),
            struct((GROUPS, units, rows), bf16),
            struct((router.shape[0], width), f32),
        ),
        in_specs=[VMEM] * 2 + [HBM] * GROUPS + [VMEM] * 2,
        out_specs=(VMEM,) * 5,
        scratch_shapes=[
            pltpu.VMEM((GROUPS, 3 * units, width), bf16),
            pltpu.VMEM((rows, width), f32),
            pltpu.VMEM((rows, width), f32),
            dma(GROUPS),
        ],
        compiler_params=pltpu.CompilerParams(vmem_limit_bytes=LIMIT),
        name="routed_expert",
        cost_estimate=cost(22),
    )(x, up, *weights, router, own)


def rows_back(xs, shared, d_gu, units, x, up, number):
    count = len(xs)
    n_hidden, width = units.shape[1], x.shape[1]

    def kernel(*refs):
        d = lax.axis_index("dp")
        n_in, n_out = count + 5, count + 3
        shared_ref, d_gu_ref, units_ref, x_ref, up_ref = refs[count:n_in]
        outs = refs[n_in : n_in + n_out]
        got_ref, mine_ref, others_ref = outs[count:]
        scratch = refs[n_in + n_out :]
        rows = [Rows(refs[i], outs[i], *scratch[3 * i : 3 * i + 3], back=True) for i in range(count)]
        greet([{"dp": d ^ 1}], rows[0])
        side = Sends(
            [
                (shared_ref.at[chip, 1 - lax.rem(d, 2)], got_ref.at[chip], {"dp": d ^ 1})
                for chip in range(8)
            ],
            *scratch[3 * count :],
        )
        for one in rows:
            one.start()
        side.start()

        def block(j, carry):
            cols = pl.ds(pl.multiple_of(j * 256, 256), 256)
            xs, ups = x_ref[:, cols], up_ref[:, cols]
            mine_ref[0 : 2 * n_hidden, cols] = mm(d_gu_ref[0], xs)
            mine_ref[2 * n_hidden :, cols] = mm(units_ref[0], ups)
            for i in range(1, GROUPS):
                others_ref[i - 1, 0 : 2 * n_hidden, cols] = mm(d_gu_ref[i], xs).astype(bf16)
                others_ref[i - 1, 2 * n_hidden :, cols] = mm(units_ref[i], ups).astype(bf16)
            return carry

        lax.fori_loop(0, width // 256, block, 0)
        for one in rows:
            one.wait()
        side.wait()

    return pl.pallas_call(
        kernel,
        out_shape=tuple(struct(r.shape, r.dtype) for r in xs)
        + (
            struct((8,) + shared.shape[2:], bf16),
            struct((3 * n_hidden, width), f32),
            struct((GROUPS - 1, 3 * n_hidden, width), bf16),
        ),
        in_specs=[HBM] * (count + 1) + [VMEM] * 4,
        out_specs=(HBM,) * (count + 1) + (VMEM,) * 2,
        scratch_shapes=ROW_SEMS * count + sems(8, 8),
        compiler_params=comm_params(number, LIMIT),
        name="rows_back",
        cost_estimate=cost(50),
    )(*xs, shared, d_gu, units, x, up)


def join_attn(part, layer_input, gain, number):
    _, rows, width = part.shape

    def kernel(part_ref, x_ref, gain_ref, full_ref, middle_ref, stats_ref, *scratch):
        greet(tensor_peers())
        scatter, gather = direct_parts(part_ref, full_ref, scratch)
        scatter.start()
        resid = x_ref[lax.axis_index("tensor")].astype(f32)
        attn_out = scatter.total()
        middle = resid + attn_out
        gather.start(middle * second_moment(middle) * gain_ref[...])
        middle_ref[...] = middle
        stats_ref[0:1] = column_sum(resid * resid)
        stats_ref[1:2] = column_sum(attn_out * attn_out)
        stats_ref[2:3] = column_sum(middle * middle)
        scatter.wait_send()
        gather.wait()

    return pl.pallas_call(
        kernel,
        out_shape=(struct(part.shape, bf16), struct((rows, width), f32), struct((8, width), f32)),
        in_specs=[VMEM] * 3,
        out_specs=(HBM, VMEM, VMEM),
        scratch_shapes=direct_scratch(rows, width),
        compiler_params=comm_params(number, LIMIT),
        name="join_attn",
        cost_estimate=cost(40),
    )(part, layer_input, gain)


def join_ffn(part, moe_part, cotangent, middle, gain, weights, number):
    _, rows, width = part.shape

    def kernel(part_ref, moe_ref, up_ref, middle_ref, gain_ref, w_ref, full_ref, out_ref, d_ref, sums_ref, got_ref, *scratch):
        d, z, _, _ = coordinates()
        greet(tensor_peers() + [{"dp": d ^ (4 * k)} for k in (1, 2, 3)])
        scatter, gather = direct_parts(part_ref, full_ref, scratch[:N_DIRECT])
        scatter.start()
        side = Sends(
            [(w_ref.at[z ^ k], got_ref.at[k], {"dp": d ^ (4 * k)}) for k in (1, 3, 2)],
            *scratch[2 * N_DIRECT :],
        )
        side.start()
        scatter_moe, gather_moe = direct_parts(moe_ref, out_ref, scratch[N_DIRECT : 2 * N_DIRECT])
        scatter_moe.start()
        middle = middle_ref[...]
        inv = second_moment(middle)
        d_normed = scatter.total()
        scaled = d_normed * gain_ref[...]
        d_middle = (
            up_ref[lax.axis_index("tensor")].astype(f32)
            + inv * scaled
            - middle * (inv * inv * inv) * jnp.mean(scaled * middle, axis=1, keepdims=True)
        )
        gather.start(d_middle)
        d_ref[...] = d_middle
        sums_ref[0:1] = column_sum(d_normed * middle * inv)
        moe_out = scatter_moe.total()
        output = middle_ref[...] + moe_out
        gather_moe.start(output)
        sums_ref[1:2] = column_sum(moe_out * moe_out)
        sums_ref[2:3] = column_sum(output * output)
        scatter.wait_send()
        scatter_moe.wait_send()
        gather.wait()
        gather_moe.wait()
        side.wait()

    return pl.pallas_call(
        kernel,
        out_shape=(
            struct(part.shape, bf16),
            struct(part.shape, bf16),
            struct((rows, width), f32),
            struct((8, width), f32),
            struct(weights.shape, weights.dtype),
        ),
        in_specs=[VMEM] * 5 + [HBM],
        out_specs=(HBM, HBM, VMEM, VMEM, HBM),
        scratch_shapes=direct_scratch(rows, width) * 2 + sems(3, 3),
        compiler_params=comm_params(number, LIMIT),
        name="join_ffn",
        cost_estimate=cost(60),
    )(part, moe_part, cotangent, middle, gain, weights)


def scatter_keys(dk, dv, out_part, dq, weights, number):
    n = len(weights)

    def kernel(dk_ref, dv_ref, part_ref, dq_ref, *refs):
        w_refs, (k_ref, v_ref, sum_ref, pair_ref), x_refs = refs[:n], refs[n : n + 4], refs[n + 4 : 2 * n + 4]
        scratch = refs[2 * n + 4 :]
        d = lax.axis_index("dp")
        greet(dp_peers())
        moves = [
            Exchange(dk_ref, k_ref, *scratch[:3]),
            Exchange(dv_ref, v_ref, *scratch[3:6]),
            Swap(dq_ref, pair_ref, *scratch[6:9]),
            Exchange(part_ref, sum_ref, *scratch[9:12]),
            Sends(
                [
                    (w_ref.at[1 - (d // 2) % 2], x_ref, {"dp": d ^ 2})
                    for w_ref, x_ref in zip(w_refs, x_refs)
                ],
                *scratch[12:],
            ),
        ]
        for move in moves:
            move.start()
        for move in moves:
            move.wait()

    return pl.pallas_call(
        kernel,
        out_shape=(
            struct(dk.shape, bf16),
            struct(dv.shape, bf16),
            struct(out_part.shape, out_part.dtype),
            struct(dq.shape, dq.dtype),
        )
        + tuple(struct(w.shape[1:], w.dtype) for w in weights),
        in_specs=[HBM] * (4 + n),
        out_specs=(HBM,) * (4 + n),
        scratch_shapes=DP_SEMS * 2 + SWAP_SEMS + DP_SEMS + sems(n, n),
        compiler_params=comm_params(number),
        name="scatter_keys",
        cost_estimate=cost(50),
    )(dk, dv, out_part, dq, *weights)


def join_tail(part, layer_input, d_middle, gain, qkv_part, pack, number):
    _, rows, width = part.shape
    small = pack.shape[1]

    def kernel(part_ref, x_ref, d_ref, gain_ref, qkv_ref, pack_ref, *refs):
        full_ref, got_ref, one_ref, both_ref = refs[:4]
        scratch = refs[4:]
        greet(tensor_peers() + dp_peers())
        scatter, gather = join_parts(part_ref, full_ref, scratch[:N_JOIN])
        scatter.start()
        weights = Exchange(qkv_ref, got_ref, *scratch[N_JOIN : N_JOIN + 3])
        weights.start()
        own, few, mine, more, send, recv, tsend, trecv = scratch[N_JOIN + 3 :]
        me, t = lax.axis_index("dp"), lax.axis_index("tensor")
        resid = x_ref[t].astype(f32)
        inv = second_moment(resid)
        scatter.middle()
        d_normed = scatter.total()
        scaled = d_normed * gain_ref[...]
        gather.start(
            d_ref[...]
            + inv * scaled
            - resid * (inv * inv * inv) * jnp.mean(scaled * resid, axis=1, keepdims=True)
        )
        gain_grad = column_sum(d_normed * resid * inv)
        own[...] = pack_ref[...]
        for i in range(N_DP):
            own[i, small - 1 : small] = gain_grad[:, i * 128 : (i + 1) * 128]
        firsts = [
            remote(own.at[me ^ k], few.at[k], send.at[k], recv.at[k], {"dp": me ^ k})
            for k in range(1, N_DP)
        ]
        for copy in firsts:
            copy.start()
        gather.relay()
        value = own[me]
        for k in range(1, N_DP):
            firsts[k - 1].wait_recv()
            value = value + few[k]
        one_ref[...] = value
        mine[...] = value
        seconds = [
            remote(mine, more.at[k], tsend.at[k], trecv.at[k], {"tensor": t ^ k}) for k in range(1, N_T)
        ]
        for copy in seconds:
            copy.start()
        for k in range(1, N_T):
            seconds[k - 1].wait_recv()
            value = value + more[k]
        both_ref[...] = value
        for copy in firsts + seconds:
            copy.wait_send()
        scatter.wait_send()
        gather.wait()
        weights.wait()

    return pl.pallas_call(
        kernel,
        out_shape=(
            struct(part.shape, bf16),
            struct(qkv_part.shape, qkv_part.dtype),
            struct((small, 128), f32),
            struct((small, 128), f32),
        ),
        in_specs=[VMEM] * 4 + [HBM, VMEM],
        out_specs=(HBM, HBM, VMEM, VMEM),
        scratch_shapes=join_scratch(rows, width)
        + DP_SEMS
        + [
            pltpu.VMEM((N_DP, small, 128), f32),
            pltpu.VMEM((N_DP, small, 128), f32),
            pltpu.VMEM((small, 128), f32),
            pltpu.VMEM((N_T, small, 128), f32),
        ]
        + sems(N_DP, N_DP, N_T, N_T),
        compiler_params=comm_params(number, LIMIT),
        name="join_tail",
        cost_estimate=cost(60),
    )(part, layer_input, d_middle, gain, qkv_part, pack)


KEYS = 256


def attend(queries, keys, values, codes, bounds):
    count, size = queries.shape
    stream = keys.shape[0]
    factor = size ** (-0.5) * math.log2(math.e)

    def kernel(q_ref, k_ref, v_ref, code_ref, bound_ref, low_ref, wide_ref, log_ref):
        q = q_ref[...]
        lowest, highest = bound_ref[0:1], bound_ref[1:2]

        def step(i, carry):
            peak, total, acc = carry
            rows = pl.ds(pl.multiple_of(i * KEYS, KEYS), KEYS)
            scores = mm(k_ref[rows], q, NT) * factor
            code = code_ref[rows][:, 0:1]
            seen = (code >= lowest) & (code <= highest)
            scores = jnp.where(seen, scores, NEG_FILL)
            new_peak = jnp.maximum(peak, jnp.max(scores, axis=0, keepdims=True))
            terms = jnp.exp2(scores - new_peak)
            shrink = jnp.exp2(peak - new_peak)
            total = total * shrink + jnp.sum(terms, axis=0, keepdims=True)
            acc = acc * shrink + mm(v_ref[rows], terms.astype(bf16), TN)
            return new_peak, total, acc

        peak, total, acc = lax.fori_loop(
            0,
            stream // KEYS,
            step,
            (
                jnp.full((1, count), NEG_FILL, f32),
                jnp.zeros((1, count), f32),
                jnp.zeros((size, count), f32),
            ),
        )
        out = (acc / total).T
        wide_ref[...] = out
        low_ref[...] = out.astype(bf16)
        log_ref[...] = jnp.broadcast_to(peak + jnp.log2(total), (8, count))

    return pl.pallas_call(
        kernel,
        out_shape=(struct((count, size), bf16), struct((count, size), f32), struct((8, count), f32)),
        in_specs=[VMEM] * 5,
        out_specs=(VMEM,) * 3,
        compiler_params=pltpu.CompilerParams(vmem_limit_bytes=LIMIT),
        name="attend",
        cost_estimate=cost(12),
    )(queries, keys, values, codes, bounds)


def attend_back(queries, keys, values, codes, bounds, wide, logs, d_heads):
    count, size = queries.shape
    stream = keys.shape[0]
    scale = size ** (-0.5)
    factor = scale * math.log2(math.e)

    def kernel(q_ref, k_ref, v_ref, code_ref, bound_ref, wide_ref, log_ref, d_ref, dq_ref, dk_ref, dv_ref):
        q, d_out = q_ref[...], d_ref[...]
        lowest, highest = bound_ref[0:1], bound_ref[1:2]
        log = log_ref[0:1]
        delta = jnp.sum((wide_ref[...] * d_out.astype(f32)).T, axis=0, keepdims=True)

        def step(i, acc):
            rows = pl.ds(pl.multiple_of(i * KEYS, KEYS), KEYS)
            k = k_ref[rows]
            scores = mm(k, q, NT) * factor
            code = code_ref[rows][:, 0:1]
            seen = (code >= lowest) & (code <= highest)
            probs = jnp.where(seen, jnp.exp2(scores - log), 0.0)
            d_probs = mm(v_ref[rows], d_out, NT)
            d_scores = (probs * (d_probs - delta)).astype(bf16)
            dv_ref[rows] = mm(probs.astype(bf16), d_out).astype(bf16)
            dk_ref[rows] = (mm(d_scores, q) * scale).astype(bf16)
            return acc + mm(k, d_scores, TN)

        acc = lax.fori_loop(0, stream // KEYS, step, jnp.zeros((size, count), f32))
        dq_ref[...] = (acc.T * scale).astype(bf16)

    return pl.pallas_call(
        kernel,
        out_shape=(struct((count, size), bf16), struct((stream, size), bf16), struct((stream, size), bf16)),
        in_specs=[VMEM] * 8,
        out_specs=(VMEM,) * 3,
        compiler_params=pltpu.CompilerParams(vmem_limit_bytes=LIMIT),
        name="attend_back",
        cost_estimate=cost(15),
    )(queries, keys, values, codes, bounds, wide, logs, d_heads)


def doc_layout(lengths, token_index):
    doc_ends = jnp.cumsum(lengths)
    starts = doc_ends - lengths
    seq_ids = jnp.sum((token_index[:, None] >= doc_ends[None, :]).astype(jnp.int32), axis=1)
    member = seq_ids[:, None] == jnp.arange(lengths.shape[0], dtype=jnp.int32)[None, :]
    begins = jnp.sum(jnp.where(member, starts[None, :], 0), axis=1)
    offsets = token_index - begins
    return (seq_ids, offsets, offsets // DBLOCK)


def rope_tables(offsets, head_dim):
    half_dim = head_dim // 2
    frequencies = jnp.exp(
        jnp.arange(half_dim, dtype=f32) * (-2.0 * math.log(THETA) / head_dim)
    )
    angles = offsets.astype(f32)[:, None] * frequencies[None, :]
    return (jnp.cos(angles)[:, None, :], jnp.sin(angles)[:, None, :])


def rotate(vectors, cosine, sine):
    half_dim = vectors.shape[-1] // 2
    front, back = vectors[..., :half_dim], vectors[..., half_dim:]
    return jnp.concatenate([front * cosine - back * sine, back * cosine + front * sine], axis=-1)


def dot(pattern, a, b):
    return jnp.einsum(pattern, a, b, preferred_element_type=f32)


def on_device(
    layer_input,
    doc_lengths,
    expert_ids,
    attn_gain,
    qkv_weight,
    qkv_bias,
    out_weight,
    ffn_gain,
    router_weight,
    shared_gate,
    shared_in,
    shared_out,
    expert_in,
    expert_out,
    cotangent,
):
    tok, width = layer_input.shape
    dp, tn = lax.axis_index("dp"), lax.axis_index("tensor")
    experts = router_weight.shape[1]
    head_dim = qkv_weight.shape[3]
    stream = tok * N_DP
    part_rows = tok // N_T
    score_scale = head_dim ** (-0.5)
    eff = expert_out.shape[1]

    def permute(x, bits):
        return lax.ppermute(x, "tensor", [(i, i ^ bits) for i in range(N_T)])

    pieces = range(1, GROUPS)
    own_weights = jnp.concatenate(
        [expert_in[0].transpose(1, 2, 0).reshape(2 * eff, width), expert_out[0]], axis=0
    )
    weights = [own_weights] + [permute(own_weights, i) for i in pieces]

    hot = jnp.sum(
        (expert_ids[:, :, None] == jnp.arange(experts, dtype=jnp.int32)[None, None, :]).astype(f32),
        axis=1,
    )
    before = (jnp.arange(tok)[:, None] > jnp.arange(tok)[None, :]).astype(bf16)
    rank = dot("ts,se->te", before, hot.astype(bf16))
    place = jnp.where(hot > 0, rank, -1.0).astype(jnp.int32).T
    _, offset = route_plane()
    served = lax.dynamic_slice_in_dim(place, GROUPS * ((dp // 4) ^ offset), GROUPS, 0)
    places = (
        (served[:, None, :] == jnp.arange(SLOTS, dtype=jnp.int32)[None, :, None])
        .astype(bf16)
        .reshape(GROUPS * SLOTS, tok)
    )
    returned = lax.dynamic_index_in_dim(place.reshape(GROUPS, 4, tok), offset, 1, keepdims=False)
    places_back = (
        (returned[:, None, :] == jnp.arange(SLOTS, dtype=jnp.int32)[None, :, None])
        .astype(bf16)
        .reshape(GROUPS * SLOTS, tok)
    )
    by_group = (GROUPS, SLOTS, width)
    up_send = dot("rt,td->rd", places, cotangent).astype(bf16)

    local_index = dp * tok + jnp.arange(tok, dtype=jnp.int32)
    pair_index = (dp // 2) * (2 * tok) + jnp.arange(2 * tok, dtype=jnp.int32)
    every_index = jnp.arange(stream, dtype=jnp.int32)
    _, pos_local, _ = doc_layout(doc_lengths, local_index)
    seq_pair, _, blk_pair = doc_layout(doc_lengths, pair_index)
    seq_all, _, blk_all = doc_layout(doc_lengths, every_index)
    codes = jnp.broadcast_to((seq_all * CODE + blk_all)[:, None], (stream, 128))
    bounds = jnp.stack([seq_pair * CODE, seq_pair * CODE + blk_pair] + [seq_pair] * 6)
    cosine, sine = rope_tables(pos_local, head_dim)
    residual = layer_input.astype(f32)
    inv_first = lax.rsqrt(jnp.mean(residual * residual, axis=1, keepdims=True) + EPSILON)
    normed_one = (residual * inv_first * attn_gain).astype(bf16)
    projected = dot("td,dshe->tshe", normed_one, qkv_weight) + qkv_bias.astype(f32)[None]
    q_own = rotate(projected[:, 0], cosine, sine).astype(bf16).transpose(1, 0, 2)
    k_own = rotate(projected[:, 1], cosine, sine).astype(bf16).transpose(1, 0, 2)
    v_own = projected[:, 2].astype(bf16).transpose(1, 0, 2)
    keys, values, queries = gather_keys(k_own, v_own, q_own, 1)
    queries = queries.reshape(2 * tok, head_dim)

    pair_out, pair_wide, logs = attend(queries, keys, values, codes, bounds)
    heads_out = swap_cores(pair_out.reshape(2, tok, head_dim), 3)
    heads_out = jnp.concatenate([heads_out[0], heads_out[1]], axis=1)
    out_flat = out_weight.reshape(2 * head_dim, width)
    attn_part = dot("qf,fd->qd", heads_out, out_flat).astype(bf16)
    by_slice = (N_T, part_rows, width)
    normed_two, middle, stats_one = join_attn(
        attn_part.reshape(by_slice), layer_input.reshape(by_slice), ffn_gain.reshape(1, width), 4
    )
    normed_two = normed_two.reshape(tok, width)

    row_send = dot("rt,td->rd", places, normed_two).astype(bf16)
    router_rows = router_weight.T
    exp_rows, up_rows, mixed, shared_d_normed, shared_grads, gate_vec_part = rows_out(
        [row_send.reshape(by_group), up_send.reshape(by_group)],
        normed_two,
        cotangent,
        shared_in.transpose(1, 2, 0).reshape(-1, width),
        shared_out,
        shared_gate.astype(f32).reshape(1, width),
        5,
    )
    exp_rows, up_rows = exp_rows.reshape(-1, width), up_rows.reshape(-1, width)

    own_expert = jnp.broadcast_to(
        (jnp.arange(experts, dtype=jnp.int32) == dp).astype(f32)[:, None], (experts, 128)
    )
    expert_part, d_rows, d_expert_gu, gated_hidden, router_part = routed_expert(
        exp_rows, up_rows, weights, router_rows, own_expert
    )

    back_grads, back_out, got, own_grads, sent = rows_back(
        [d_rows.reshape(by_group), expert_part.reshape(by_group)],
        shared_grads,
        d_expert_gu,
        gated_hidden,
        exp_rows,
        up_rows,
        6,
    )
    core, z_index, x_index = dp % 2, dp // 4, (dp // 2) % 2

    def pick(x, index, axis=0):
        return lax.dynamic_index_in_dim(x, index, axis, keepdims=False)

    by_z = (pick(shared_grads, core, 1).astype(f32) + got.astype(f32)).astype(bf16)
    by_z = by_z.reshape((4, 2) + by_z.shape[1:])

    def combine(rows):
        return dot("rt,rd->td", places_back, rows.reshape(-1, width))

    d_normed_part = (shared_d_normed + combine(back_grads)).astype(bf16)
    moe_part = (mixed + combine(back_out)).astype(bf16)
    d_attn, output, d_middle, stats_two, got = join_ffn(
        d_normed_part.reshape(by_slice),
        moe_part.reshape(by_slice),
        cotangent.reshape(by_slice),
        middle,
        ffn_gain.reshape(1, width),
        by_z,
        7,
    )
    d_attn, sent = lax.optimization_barrier((d_attn, sent))
    received = [permute(sent[i - 1], i) for i in pieces]
    by_x = (pick(by_z, z_index).astype(f32) + sum(got[k].astype(f32) for k in (1, 2, 3))).astype(bf16)
    d_attn = d_attn.reshape(tok, width)

    outproj_part = dot("qd,qf->df", d_attn, heads_out).astype(bf16)
    d_heads = dot("qd,fd->qf", d_attn, out_flat).astype(bf16)
    d_heads = jnp.stack([d_heads[:, :head_dim], d_heads[:, head_dim:]])
    d_heads = swap_cores(d_heads, 8).reshape(2 * tok, head_dim)
    d_queries, d_keys, d_values = attend_back(
        queries, keys, values, codes, bounds, pair_wide, logs, d_heads
    )
    got_k, got_v, got_out_part, d_queries, got = scatter_keys(
        d_keys.reshape(N_DP, tok, head_dim),
        d_values.reshape(N_DP, tok, head_dim),
        outproj_part.reshape(N_DP, width // N_DP, -1),
        d_queries.reshape(2, tok, head_dim),
        [by_x],
        9,
    )
    got_k, received = lax.optimization_barrier((got_k, received))
    shared_grads = pick(by_x, x_index).astype(f32) + got.astype(f32)
    n_shared = shared_in.shape[2]
    outproj_grad = jnp.sum(got_out_part.astype(f32), axis=0)
    def summed(x):
        x = jnp.sum(x.astype(f32).reshape(8, 2, tok, head_dim), axis=0)
        return x[0], x[1]

    cosine, sine = cosine[:, 0], sine[:, 0]
    d_proj = jnp.concatenate(
        [rotate(d_queries[h].astype(f32), cosine, -sine) for h in range(2)]
        + [rotate(x, cosine, -sine) for x in summed(got_k)]
        + list(summed(got_v)),
        axis=1,
    ).astype(bf16)
    d_normed_one = dot("tf,df->td", d_proj, qkv_weight.reshape(width, -1)).astype(bf16)
    qkv_part = dot("td,tf->df", normed_one, d_proj).astype(bf16)
    bias_part = jnp.sum(d_proj.astype(f32), axis=0)

    def slices(row):
        return row.reshape(-1, N_DP, 128).transpose(1, 0, 2)

    five = jnp.sum(jnp.concatenate([stats_one[:3], stats_two[1:3]]), axis=1)
    pack = jnp.concatenate(
        [
            slices(router_part),
            slices(gate_vec_part[0]),
            slices(stats_two[0]),
            jnp.broadcast_to(jnp.pad(five, (0, 123))[None, None], (N_DP, 1, 128)),
            jnp.pad(
                bias_part.reshape(6, N_DP, 8).transpose(1, 0, 2).reshape(N_DP, 1, 48),
                ((0, 0), (0, 4), (0, 80)),
            ),
        ],
        axis=1,
    )
    input_grad, got_qkv, over_dp, over_both = join_tail(
        d_normed_one.reshape(by_slice),
        layer_input.reshape(by_slice),
        d_middle,
        attn_gain.reshape(1, width),
        qkv_part.reshape(N_DP, width // N_DP, -1),
        pack,
        10,
    )
    bias_grad = over_dp[19, :48].reshape(3, 2, 8)
    rms_stats = jnp.sqrt(over_both[18, :5] / (stream * width))
    qkv_grad = jnp.sum(got_qkv.astype(f32), axis=0)

    expert_grads = own_grads + sum(g.astype(f32) for g in received)

    return (
        output.reshape(tok, width),
        input_grad.reshape(tok, width).astype(f32),
        qkv_grad.reshape(width // N_DP, 3, 2, head_dim),
        bias_grad,
        outproj_grad.T.reshape(2, head_dim, width // N_DP),
        over_both[23],
        over_both[17],
        over_both[:16].T,
        over_both[16],
        shared_grads[: 2 * n_shared].reshape(2, n_shared, -1).transpose(2, 0, 1),
        shared_grads[2 * n_shared :],
        expert_grads[: 2 * eff].reshape(2, eff, width).transpose(2, 0, 1)[None],
        expert_grads[2 * eff :][None],
        rms_stats,
    )


def solution(mesh):
    in_specs = (
        P("dp", None),
        P(),
        P("dp", None),
        P(),
        P(None, None, "tensor", None),
        P(None, "tensor", None),
        P("tensor", None, None),
        P(),
        P(),
        P(),
        P(None, None, "tensor"),
        P("tensor", None),
        P("dp", None, None, "tensor"),
        P("dp", "tensor", None),
        P("dp", None),
    )
    out_specs = (
        P("dp", None),
        P("dp", None),
        P("dp", None, "tensor", None),
        P(None, "tensor", "dp"),
        P("tensor", None, "dp"),
        P("dp"),
        P("dp"),
        P("dp", None),
        P("dp"),
        P("dp", None, "tensor"),
        P("tensor", "dp"),
        P("dp", None, None, "tensor"),
        P("dp", "tensor", None),
        P(),
    )
    return jax.shard_map(
        on_device, mesh=mesh, in_specs=in_specs, out_specs=out_specs, check_vma=False
    )
```

```python
import math

import jax
import jax.numpy as jnp
from jax import lax
from jax.experimental import pallas as pl
from jax.experimental.pallas import tpu as pltpu
from jax.sharding import PartitionSpec as P

DBLOCK = 256
EPSILON = 1e-06
THETA = 1000000.0
NEG_FILL = -1e30
MESH = pl.DeviceIdType.MESH
f32 = jnp.float32
bf16 = jnp.bfloat16
N_DP = 16
N_T = 8
SLOTS = 112
LIMIT = 48 * 1024 * 1024
CODE = 1 << 16

HBM = pl.BlockSpec(memory_space=pl.ANY)
VMEM = pl.BlockSpec(memory_space=pltpu.VMEM)


def greet(peers, *more):
    barrier = pltpu.get_barrier_semaphore()
    for peer in peers:
        pl.semaphore_signal(barrier, inc=1, device_id=peer, device_id_type=MESH)
    count = len(peers)
    for rows in more:
        count = count + rows.greet()
    pl.semaphore_wait(barrier, count)


def remote(src, dst, send, recv, device):
    return pltpu.make_async_remote_copy(
        src_ref=src,
        dst_ref=dst,
        send_sem=send,
        recv_sem=recv,
        device_id=device,
        device_id_type=MESH,
    )


def dma(*shape):
    return pltpu.SemaphoreType.DMA(shape)


def cost(micros):
    return pl.CostEstimate(flops=0, bytes_accessed=int(micros * 3e6), transcendentals=0)


def comm_params(number, limit=None):
    return pltpu.CompilerParams(
        collective_id=number, has_side_effects=True, vmem_limit_bytes=limit
    )


NT = (((1,), (1,)), ((), ()))
TN = (((0,), (0,)), ((), ()))


def mm(a, b, dims=(((1,), (0,)), ((), ()))):
    return lax.dot_general(a, b, dims, preferred_element_type=f32)


GROUPS = 4
ORDER = (4, 12, 2, 5, 13, 3, 8, 6, 14, 9, 7, 15, 10, 11, 1)
STEPS = (1, 3, 2, 4, 5, 7, 6)
CHUNKS = ((0, 48), (48, 64))


def sems(*counts):
    return [dma(*c) if isinstance(c, tuple) else dma(c) for c in counts]


def dp_peers():
    me = lax.axis_index("dp")
    return [{"dp": me ^ k} for k in range(1, N_DP)]


def tensor_peers():
    me = lax.axis_index("tensor")
    return [{"tensor": me ^ k} for k in range(1, N_T)]


def coordinates():
    d, t = lax.axis_index("dp"), lax.axis_index("tensor")
    return d, d // 4, t // 4, t % 4


def route_plane():
    d, z, _, y = coordinates()
    plane = 2 * ((z + d // 2) % 2) + d % 2
    return plane, y ^ plane


class Rows:
    def __init__(self, x_ref, out_ref, send, recv, local, back=False):
        self.x, self.out, self.send, self.recv, self.local, self.back = x_ref, out_ref, send, recv, local, back
        d, z, half, y = coordinates()
        plane, offset = route_plane()
        if back:
            experts = [{"dp": 4 * k + offset, "tensor": 4 * half + plane} for k in range(GROUPS)]
            target = y ^ (d % 4)
        else:
            experts = [{"dp": 4 * (z ^ offset) + j, "tensor": 4 * half + plane} for j in range(GROUPS)]
        groups = [
            {
                "dp": 4 * g + 2 * ((y // 2 + g) % 2) + y % 2,
                "tensor": 4 * half + (target if back else y ^ g ^ z),
            }
            for g in range(GROUPS)
        ]
        self.peers, self.sources = (groups, experts) if back else (experts, groups)
        self.slot = z
        self.mine = z if back else d % 4
        self.own = offset == 0
        if back:
            self.own = jnp.logical_and(self.own, d % 4 == 0)
        self.d = d

    def is_own(self, j):
        return jnp.logical_and(self.own, self.mine == j)

    def greet(self):
        barrier = pltpu.get_barrier_semaphore()
        for j in range(GROUPS):
            source = self.sources[j]

            @pl.when(jnp.logical_not(jnp.logical_and(self.own, self.slot == j)))
            def _():
                pl.semaphore_signal(barrier, inc=1, device_id=source, device_id_type=MESH)

        return GROUPS - self.own.astype(jnp.int32)

    def copy(self, j, c):
        rows = pl.ds(*CHUNKS[c])
        return remote(
            self.x.at[j, rows],
            self.out.at[self.slot, rows],
            self.send.at[c, j],
            self.recv.at[c, self.slot],
            self.peers[j],
        )

    def arrival(self, j, c):
        rows = pl.ds(*CHUNKS[c])
        return remote(
            self.x.at[j, rows],
            self.out.at[j, rows],
            self.send.at[c, j],
            self.recv.at[c, j],
            self.peers[j],
        )

    def inside(self):
        return pltpu.make_async_copy(self.x.at[self.mine], self.out.at[self.slot], self.local.at[0])

    def start(self):
        for c in range(len(CHUNKS)):
            for j in range(GROUPS):

                @pl.when(jnp.logical_not(self.is_own(j)))
                def _():
                    self.copy(j, c).start()

        @pl.when(self.own)
        def _():
            self.inside().start()

    def wait(self):
        @pl.when(self.own)
        def _():
            self.inside().wait()

        for c in range(len(CHUNKS)):
            for j in range(GROUPS):

                @pl.when(jnp.logical_not(self.is_own(j)))
                def _():
                    self.copy(j, c).wait_send()

                @pl.when(jnp.logical_not(jnp.logical_and(self.own, self.slot == j)))
                def _():
                    self.arrival(j, c).wait_recv()


ROW_SEMS = sems((len(CHUNKS), GROUPS), (len(CHUNKS), GROUPS), 1)


class Exchange:
    def __init__(self, x_ref, out_ref, send, recv, local):
        me = lax.axis_index("dp")
        self.copies = [
            remote(x_ref.at[me ^ k], out_ref.at[me], send.at[k], recv.at[k], {"dp": me ^ k})
            for k in ORDER
        ]
        self.copies.append(pltpu.make_async_copy(x_ref.at[me], out_ref.at[me], local.at[0]))

    def start(self):
        for copy in self.copies:
            copy.start()

    def wait(self):
        for copy in self.copies:
            copy.wait()


DP_SEMS = sems(N_DP, N_DP, 1)


class Swap:
    def __init__(self, x_ref, out_ref, send, recv, local):
        me = lax.axis_index("dp")
        core = lax.rem(me, 2)
        self.copies = [
            remote(x_ref.at[1 - core], out_ref.at[core], send.at[0], recv.at[0], {"dp": me ^ 1}),
            pltpu.make_async_copy(x_ref.at[core], out_ref.at[core], local.at[0]),
        ]

    start = Exchange.start
    wait = Exchange.wait


SWAP_SEMS = sems(1, 1, 1)


class DirectScatter:
    def __init__(self, part_ref, got, send, recv):
        self.me = lax.axis_index("tensor")
        self.part, self.got = part_ref, got
        self.copies = [
            remote(
                part_ref.at[self.me ^ k], got.at[k], send.at[k], recv.at[k], {"tensor": self.me ^ k}
            )
            for k in STEPS
        ]

    def start(self):
        for copy in self.copies:
            copy.start()

    def total(self):
        value = self.part[self.me].astype(f32)
        for k, copy in zip(STEPS, self.copies):
            copy.wait_recv()
            value = value + self.got[k].astype(f32)
        return value

    def wait_send(self):
        for copy in self.copies:
            copy.wait_send()


class DirectGather:
    def __init__(self, mine, full_ref, send, recv, local):
        me = lax.axis_index("tensor")
        self.mine = mine
        self.copies = [
            remote(mine, full_ref.at[me], send.at[k], recv.at[k], {"tensor": me ^ k}) for k in STEPS
        ]
        self.copies.append(pltpu.make_async_copy(mine, full_ref.at[me], local.at[0]))

    def start(self, value):
        self.mine[...] = value.astype(bf16)
        for copy in self.copies:
            copy.start()

    def wait(self):
        for copy in self.copies:
            copy.wait()


def direct_scratch(rows, width):
    return [
        pltpu.VMEM((N_T, rows, width), bf16),
        pltpu.VMEM((rows, width), bf16),
    ] + sems(N_T, N_T, N_T, N_T, 1)


N_DIRECT = 7


def direct_parts(part_ref, full_ref, scratch):
    got, mine, send, recv, asend, arecv, local = scratch
    return DirectScatter(part_ref, got, send, recv), DirectGather(mine, full_ref, asend, arecv, local)


class Scatter:
    def __init__(self, part_ref, got, mid, last, send, recv):
        t = lax.axis_index("tensor")
        y, half = t % 4, t // 4
        self.part, self.got, self.mid, self.last = part_ref, got, mid, last
        self.slots = (4 * (1 - half) + y, t)
        self.copies = [
            [
                remote(
                    part_ref.at[slot ^ k],
                    got.at[a, k],
                    send.at[a, k],
                    recv.at[a, k],
                    {"tensor": t ^ k},
                )
                for k in (1, 3, 2)
            ]
            for a, slot in enumerate(self.slots)
        ]
        self.across = remote(mid, last, send.at[0, 0], recv.at[0, 0], {"tensor": t ^ 4})

    def start(self):
        for copies in self.copies:
            for copy in copies:
                copy.start()

    def over_y(self, a):
        value = self.part[self.slots[a]].astype(f32)
        for k, copy in zip((1, 3, 2), self.copies[a]):
            copy.wait_recv()
            value = value + self.got[a, k].astype(f32)
        return value

    def middle(self):
        self.mid[...] = self.over_y(0).astype(bf16)
        self.across.start()

    def total(self):
        value = self.over_y(1)
        self.across.wait_recv()
        return value + self.last[...].astype(f32)

    def wait_send(self):
        for copies in self.copies:
            for copy in copies:
                copy.wait_send()
        self.across.wait_send()


class Gather:
    def __init__(self, mine, full_ref, send, recv, local):
        t = lax.axis_index("tensor")
        self.mine = mine
        self.across = remote(
            mine, full_ref.at[t], send.at[0, 0], recv.at[0, 0], {"tensor": t ^ 4}
        )
        self.first = [
            remote(mine, full_ref.at[t], send.at[0, k], recv.at[0, k], {"tensor": t ^ k})
            for k in (1, 3, 2)
        ]
        self.second = [
            remote(
                full_ref.at[t ^ 4],
                full_ref.at[t ^ 4],
                send.at[1, k],
                recv.at[1, k],
                {"tensor": t ^ k},
            )
            for k in (1, 3, 2)
        ]
        self.own = pltpu.make_async_copy(mine, full_ref.at[t], local.at[0])

    def start(self, value):
        self.mine[...] = value.astype(bf16)
        for copy in [self.across] + self.first + [self.own]:
            copy.start()

    def relay(self):
        self.across.wait_recv()
        for copy in self.second:
            copy.start()

    def wait(self):
        self.across.wait_send()
        for copy in self.first + self.second + [self.own]:
            copy.wait()


JOIN_SEMS = sems((2, 4), (2, 4), (2, 4), (2, 4), 1)


def join_scratch(rows, width):
    return [
        pltpu.VMEM((2, 4, rows, width), bf16),
        pltpu.VMEM((rows, width), bf16),
        pltpu.VMEM((rows, width), bf16),
        pltpu.VMEM((rows, width), bf16),
    ] + JOIN_SEMS


N_JOIN = 9


def join_parts(part_ref, full_ref, scratch):
    got, mid, last, mine, send, recv, asend, arecv, local = scratch
    return Scatter(part_ref, got, mid, last, send, recv), Gather(mine, full_ref, asend, arecv, local)


class Sends:
    def __init__(self, messages, send, recv):
        self.copies = [
            remote(src, dst, send.at[i], recv.at[i], peer) for i, (src, dst, peer) in enumerate(messages)
        ]

    start = Exchange.start
    wait = Exchange.wait


def struct(shape, dtype):
    return jax.ShapeDtypeStruct(shape, dtype)


def column_sum(value):
    return jnp.sum(value, axis=0, keepdims=True)


def second_moment(value):
    return lax.rsqrt(jnp.mean(value * value, axis=1, keepdims=True) + EPSILON)


def attend(q, rows, state, k, v, code, bounds, factor):
    peak, total, acc = state
    scores = mm(k, q, NT) * factor
    seen = (code >= bounds[0:1]) & (code <= bounds[1:2])
    scores = jnp.where(seen, scores, NEG_FILL)
    new_peak = jnp.maximum(peak, jnp.max(scores, axis=0, keepdims=True))
    terms = jnp.exp2(scores - new_peak)
    shrink = jnp.exp2(peak - new_peak)
    total = total * shrink + jnp.sum(terms, axis=0, keepdims=True)
    acc = acc * shrink + mm(v, terms.astype(bf16), TN)
    return new_peak, total, acc


def along_y(shift):
    t = lax.axis_index("tensor")
    return {"tensor": 4 * (t // 4) + (t + shift) % 4}


def weights_along_y(weight_refs, n_rows, results, send, recv):
    messages = []
    for result, shift in zip(results, (1, 3)):
        at = 0
        for ref, count in zip(weight_refs, n_rows):
            messages.append((ref, result.at[pl.ds(at, count)], along_y(shift)))
            at += count
    return Sends(messages, send, recv)


def attend_forward(k, v, q, codes, bounds, out_weight, layer_input, gain, weights, number):
    _, tok, size = q.shape
    n_rows = [w.shape[0] for w in weights]
    stream, count = N_DP * tok, 2 * tok
    _, rows, width = layer_input.shape
    factor = size ** (-0.5) * math.log2(math.e)

    def kernel(k_ref, v_ref, q_ref, code_ref, bound_ref, w_ref, x_ref, gain_ref, *refs):
        weight_refs, outs, scratch = refs[:2], refs[2:13], refs[13:]
        keys_ref, values_ref, pair_ref, wide_ref, log_ref, heads_ref, full_ref, middle_ref, stats_ref = outs[:9]
        keys, values, pair, own_out, heads, part = scratch[:6]
        send, recv, local = scratch[6:9]
        swap_sems, out_sems, store_sems, weight_sems = scratch[9:12], scratch[12:14], scratch[14], scratch[15:17]
        join = scratch[17:]
        me = lax.axis_index("dp")
        core = lax.rem(me, 2)
        greet(tensor_peers() + dp_peers())
        both = weights_along_y(weight_refs, n_rows, outs[9:], *weight_sems)
        both.start()
        swap = Swap(q_ref, pair, *swap_sems)
        swap.start()

        def place(group):
            return pl.ds(pl.multiple_of(group * tok, tok), tok)

        def copies(step, head):
            return [
                remote(
                    own.at[head],
                    full.at[place(me)],
                    send.at[i, step],
                    recv.at[i, step],
                    {"dp": me ^ step},
                )
                for i, (own, full) in enumerate(((k_ref, keys), (v_ref, values)))
            ]

        for step in ORDER:
            for copy in copies(step, core if step % 2 == 0 else 1 - core):
                copy.start()
        locals_ = [
            pltpu.make_async_copy(own.at[core], full.at[place(me)], local.at[i])
            for i, (own, full) in enumerate(((k_ref, keys), (v_ref, values)))
        ]
        for copy in locals_:
            copy.start()
        swap.wait()
        for copy in locals_:
            copy.wait()
        queries = pair[...].reshape(count, size)
        limits = bound_ref[...]

        def block(group, state):
            at = place(group)
            return attend(
                queries, at, state, keys[at], values[at], code_ref[at][:, 0:1], limits, factor
            )

        def arrived(step, state):
            group = me ^ step
            for i, (own, full) in enumerate(((k_ref, keys), (v_ref, values))):
                remote(
                    own.at[core], full.at[place(group)], send.at[i, step], recv.at[i, step], {"dp": group}
                ).wait_recv()
            return block(group, state)

        state = block(
            me,
            (
                jnp.full((1, count), NEG_FILL, f32),
                jnp.zeros((1, count), f32),
                jnp.zeros((size, count), f32),
            ),
        )
        peak, total, acc = lax.fori_loop(1, N_DP, arrived, state)
        out = (acc / total).T
        wide_ref[...] = out
        log_ref[...] = jnp.broadcast_to(peak + jnp.log2(total), (8, count))
        own_out[...] = out.astype(bf16).reshape(2, tok, size)
        across = remote(
            own_out.at[1 - core], heads.at[core], out_sems[0].at[0], out_sems[1].at[0], {"dp": me ^ 1}
        )
        across.start()
        heads[core] = own_out[core]
        stores = [
            pltpu.make_async_copy(keys, keys_ref, store_sems.at[0]),
            pltpu.make_async_copy(values, values_ref, store_sems.at[1]),
            pltpu.make_async_copy(pair, pair_ref, store_sems.at[2]),
        ]
        for store in stores:
            store.start()
        across.wait_recv()
        heads_ref[:, 0:size] = heads[0]
        heads_ref[:, size : 2 * size] = heads[1]

        def project(j, carry):
            cols = pl.ds(pl.multiple_of(j * 512, 512), 512)
            value = mm(heads_ref[...], w_ref[:, cols])
            part[:, :, cols] = value.reshape(N_T, rows, 512).astype(bf16)
            return carry

        lax.fori_loop(0, width // 512, project, 0)
        scatter, gather = direct_parts(part, full_ref, join)
        scatter.start()
        resid = x_ref[lax.axis_index("tensor")].astype(f32)
        attn_out = scatter.total()
        middle = resid + attn_out
        gather.start(middle * second_moment(middle) * gain_ref[...])
        middle_ref[...] = middle
        stats_ref[0:1] = column_sum(resid * resid)
        stats_ref[1:2] = column_sum(attn_out * attn_out)
        stats_ref[2:3] = column_sum(middle * middle)
        for step in ORDER:
            for copy in copies(step, core):
                copy.wait_send()
        across.wait_send()
        scatter.wait_send()
        for store in stores:
            store.wait()
        gather.wait()
        both.wait()

    return pl.pallas_call(
        kernel,
        out_shape=(
            struct((stream, size), bf16),
            struct((stream, size), bf16),
            struct(q.shape, bf16),
            struct((count, size), f32),
            struct((8, count), f32),
            struct((tok, 2 * size), bf16),
            struct(layer_input.shape, bf16),
            struct((rows, width), f32),
            struct((8, width), f32),
            struct((sum(n_rows), width), bf16),
            struct((sum(n_rows), width), bf16),
        ),
        in_specs=[HBM] * 3 + [VMEM] * 5 + [HBM] * 2,
        out_specs=(HBM,) * 3 + (VMEM,) * 3 + (HBM,) + (VMEM,) * 2 + (HBM,) * 2,
        scratch_shapes=[
            pltpu.VMEM((stream, size), bf16),
            pltpu.VMEM((stream, size), bf16),
            pltpu.VMEM(q.shape, bf16),
            pltpu.VMEM(q.shape, bf16),
            pltpu.VMEM(q.shape, bf16),
            pltpu.VMEM(layer_input.shape, bf16),
        ]
        + sems((2, N_DP), (2, N_DP), 2)
        + SWAP_SEMS
        + sems(1, 1, 3, 4, 4)
        + direct_scratch(rows, width),
        compiler_params=comm_params(number, LIMIT),
        name="attend_forward",
        cost_estimate=cost(85),
    )(k, v, q, codes, bounds, out_weight, layer_input, gain, *weights)


def sigmoid(x):
    return 1.0 / (1.0 + jnp.exp(-x))


TILE = 176
HALF = 256


def shared_expert(x_ref, up_ref, w_ref, vec_ref, part_ref, d_ref, grads_ref, row_ref, low_ref):
    hidden = w_ref.shape[0] // 3
    vec = vec_ref[...]
    gate = sigmoid(jnp.sum(x_ref[...].astype(f32) * vec, axis=1, keepdims=True))
    low_ref[...] = (gate * up_ref[...].astype(f32)).astype(bf16)
    part_ref[...] = jnp.zeros_like(part_ref)
    d_ref[...] = jnp.zeros_like(d_ref)

    def tile(i, carry):
        rows = [pl.ds(pl.multiple_of(i * TILE + k * hidden, 16), TILE) for k in range(3)]
        x, d_out = x_ref[...], low_ref[...]
        gate_part = mm(w_ref[rows[0]], x, NT)
        up_part = mm(w_ref[rows[1]], x, NT)
        sig = sigmoid(gate_part)
        act = gate_part * sig
        unit = (act * up_part).astype(bf16)
        d_unit = mm(w_ref[rows[2]], d_out, NT)
        d_gate = (d_unit * up_part * sig * (1.0 + gate_part * (1.0 - sig))).astype(bf16)
        d_up = (d_unit * act).astype(bf16)

        def block(j, carry):
            cols = pl.ds(pl.multiple_of(j * 256, 256), 256)
            xs, ds = x_ref[:, cols], low_ref[:, cols]
            part_ref[:, cols] += mm(unit, w_ref[rows[2], cols], TN)
            d_ref[:, cols] += mm(d_gate, w_ref[rows[0], cols], TN) + mm(d_up, w_ref[rows[1], cols], TN)
            for k, grad in enumerate((mm(d_gate, xs), mm(d_up, xs), mm(unit, ds))):
                grad = grad.astype(bf16)
                grads_ref[j, 0, rows[k]] = grad[:, :128]
                grads_ref[j, 1, rows[k]] = grad[:, 128:]
            return carry

        return lax.fori_loop(0, x.shape[1] // 256, block, carry)

    lax.fori_loop(0, hidden // TILE, tile, 0)
    total = part_ref[...]
    d_logit = jnp.sum(up_ref[...].astype(f32) * total, axis=1, keepdims=True) * gate * (1.0 - gate)
    part_ref[...] = gate * total
    d_ref[...] += d_logit * vec
    row_ref[...] = column_sum(d_logit * x_ref[...].astype(f32))


def routed_expert(x_ref, up_ref, w_ref, router_ref, own, acc, dgu_ref, unit_ref, router_grad_ref, before_far):
    groups, slots, width = x_ref.shape
    rows = groups * slots
    units = w_ref.shape[1] // 3

    def flat(ref):
        return ref[...].reshape(rows, width)

    logits = mm(router_ref[...], flat(x_ref), NT)
    terms = jnp.exp(logits - jnp.max(logits, axis=0, keepdims=True))
    probs = terms / jnp.sum(terms, axis=0, keepdims=True)
    gate = jnp.sum(probs * own, axis=0, keepdims=True)
    acc[...] = jnp.zeros_like(acc)

    def piece(step, d_gate_row):
        i = jnp.where(step < 2, step, 5 - step)

        @pl.when(step == 3)
        def _():
            before_far()

        gate_part = mm(w_ref[i, 0:units], flat(x_ref), NT)
        up_part = mm(w_ref[i, units : 2 * units], flat(x_ref), NT)
        raw = mm(w_ref[i, 2 * units : 3 * units], flat(up_ref), NT)
        sig = sigmoid(gate_part)
        act = gate_part * sig
        unit = (act * up_part).astype(bf16).astype(f32)
        d_unit = gate * raw
        gated = (unit * gate).astype(bf16)
        d_gate = (d_unit * up_part * sig * (1.0 + gate_part * (1.0 - sig))).astype(bf16)
        d_up = (d_unit * act).astype(bf16)
        unit_ref[i] = gated
        dgu_ref[i, 0:units] = d_gate
        dgu_ref[i, units : 2 * units] = d_up

        def block(j, carry):
            cols = pl.ds(pl.multiple_of(j * 512, 512), 512)
            acc[0:rows, cols] += mm(gated, w_ref[i, 2 * units : 3 * units, cols], TN)
            acc[rows : 2 * rows, cols] += mm(d_gate, w_ref[i, 0:units, cols], TN) + mm(
                d_up, w_ref[i, units : 2 * units, cols], TN
            )
            return carry

        lax.fori_loop(0, width // 512, block, 0)
        return d_gate_row + jnp.sum(unit * raw, axis=0, keepdims=True)

    d_gate_row = lax.fori_loop(0, GROUPS, piece, jnp.zeros((1, rows), f32))
    d_logits = (d_gate_row * gate * (own - probs)).astype(bf16)
    router_grad_ref[...] = mm(d_logits, flat(x_ref))
    acc[rows : 2 * rows] += mm(d_logits, router_ref[...], TN)


def experts(rows, ups, below, above, in_rows, out_rows, tokens, upstream, w_in, w_out, vec, router, own, number):
    _, slots, width = rows.shape
    tok = tokens.shape[0]
    hidden, units = w_out.shape[0], out_rows.shape[0]
    n_rows = GROUPS * slots
    half, rest = pl.ds(0, HALF), pl.ds(HALF, 3 * units - HALF)

    def kernel(*refs):
        (rows_ref, ups_ref, below_ref, above_ref, in_ref, out_ref, w_in_ref, w_out_ref), refs = refs[:8], refs[8:]
        (x_ref, up_ref, vec_ref, router_ref, own_ref), refs = refs[:5], refs[5:]
        (back_d, back_out, part_ref, d_ref, by_z_ref, row_ref, router_grad_ref, mine_ref, *sent_refs), refs = (
            refs[:11],
            refs[11:],
        )
        (weights, low, grads, xs, us, w, acc, dgu, unit, far, send_d, send_out), refs = refs[:12], refs[12:]
        row_sems, refs = [refs[3 * i : 3 * i + 3] for i in range(4)], refs[12:]
        rsend, rrecv, csend, crecv, loaded, stored = refs
        d = lax.axis_index("dp")
        core = lax.rem(d, 2)
        out_x = Rows(rows_ref, xs, *row_sems[0])
        out_u = Rows(ups_ref, us, *row_sems[1])
        in_d = Rows(send_d, back_d, *row_sems[2], back=True)
        in_out = Rows(send_out, back_out, *row_sems[3], back=True)
        greet([along_y(1), along_y(3), {"dp": d ^ 1}], out_x, in_d)
        out_x.start()
        out_u.start()
        relay = Sends(
            [
                (below_ref.at[half], w.at[2, half], along_y(1)),
                (above_ref.at[rest], w.at[2, rest], along_y(3)),
            ],
            rsend,
            rrecv,
        )
        relay.start()
        loads = [
            pltpu.make_async_copy(src, dst, loaded.at[i])
            for i, (src, dst) in enumerate(
                (
                    (w_in_ref, weights.at[pl.ds(0, 2 * hidden)]),
                    (w_out_ref, weights.at[pl.ds(2 * hidden, hidden)]),
                    (in_ref, w.at[0, pl.ds(0, 2 * units)]),
                    (out_ref, w.at[0, pl.ds(2 * units, units)]),
                    (above_ref, w.at[1]),
                    (below_ref, w.at[3]),
                )
            )
        ]
        for load in loads:
            load.start()
        for load in loads[:2]:
            load.wait()
        shared_expert(x_ref, up_ref, weights, vec_ref, part_ref, d_ref, grads, row_ref, low)
        cores = Sends(
            [(grads.at[chip, 1 - core], far.at[chip], {"dp": d ^ 1}) for chip in range(8)], csend, crecv
        )
        cores.start()
        for load in loads[2:]:
            load.wait()
        out_x.wait()
        out_u.wait()

        def before_far():
            for copy in relay.copies:
                copy.wait_recv()

        routed_expert(
            xs,
            us,
            w,
            router_ref,
            own_ref[:, 0:1],
            acc,
            dgu,
            unit,
            router_grad_ref,
            before_far,
        )
        send_d[...] = acc[n_rows : 2 * n_rows].astype(bf16).reshape(GROUPS, slots, width)
        in_d.start()
        send_out[...] = acc[0:n_rows].astype(bf16).reshape(GROUPS, slots, width)
        in_out.start()

        def block(j, carry):
            cols = pl.ds(pl.multiple_of(j * 256, 256), 256)
            x, up = xs[:, :, cols].reshape(n_rows, 256), us[:, :, cols].reshape(n_rows, 256)
            acc[0 : 2 * units, cols] = mm(dgu[0], x)
            acc[2 * units : 3 * units, cols] = mm(unit[0], up)
            for i in range(1, GROUPS):
                at = 3 * units * (i - 1)
                weights[at : at + 2 * units, cols] = mm(dgu[i], x).astype(bf16)
                weights[at + 2 * units : at + 3 * units, cols] = mm(unit[i], up).astype(bf16)
            return carry

        lax.fori_loop(0, width // 256, block, 0)
        stores = [pltpu.make_async_copy(acc.at[pl.ds(0, 3 * units)], mine_ref, stored.at[0])] + [
            pltpu.make_async_copy(weights.at[pl.ds(3 * units * i, 3 * units)], ref, stored.at[i + 1])
            for i, ref in enumerate(sent_refs)
        ]
        for store in stores:
            store.start()
        for chip in range(8):
            cores.copies[chip].wait_recv()
            far[chip] = (far[chip].astype(f32) + grads[chip, core].astype(f32)).astype(bf16)
            stores.append(pltpu.make_async_copy(far.at[chip], by_z_ref.at[chip], stored.at[4 + chip]))
            stores[-1].start()
        for copy in relay.copies + cores.copies:
            copy.wait_send()
        in_d.wait()
        in_out.wait()
        for store in stores:
            store.wait()

    row = struct(rows.shape, bf16)
    return pl.pallas_call(
        kernel,
        out_shape=(
            row,
            row,
            struct((tok, width), f32),
            struct((tok, width), f32),
            struct((8, 3 * hidden, 128), bf16),
            struct((1, width), f32),
            struct((router.shape[0], width), f32),
            struct((3 * units, width), f32),
        )
        + (struct((3 * units, width), bf16),) * 3,
        in_specs=[HBM] * 8 + [VMEM] * 5,
        out_specs=(HBM, HBM, VMEM, VMEM, HBM, VMEM, VMEM) + (HBM,) * 4,
        scratch_shapes=[
            pltpu.VMEM((3 * hidden, width), bf16),
            pltpu.VMEM((tok, width), bf16),
            pltpu.VMEM((8, 2, 3 * hidden, 128), bf16),
            pltpu.VMEM(rows.shape, bf16),
            pltpu.VMEM(rows.shape, bf16),
            pltpu.VMEM((GROUPS, 3 * units, width), bf16),
            pltpu.VMEM((2 * n_rows, width), f32),
            pltpu.VMEM((GROUPS, 2 * units, n_rows), bf16),
            pltpu.VMEM((GROUPS, units, n_rows), bf16),
            pltpu.VMEM((8, 3 * hidden, 128), bf16),
            pltpu.VMEM(rows.shape, bf16),
            pltpu.VMEM(rows.shape, bf16),
        ]
        + ROW_SEMS * 4
        + sems(2, 2, 8, 8, 6, 12),
        compiler_params=comm_params(number, 61 * 1024 * 1024),
        name="experts",
        cost_estimate=cost(115),
    )(rows, ups, below, above, in_rows, out_rows, w_in, w_out, tokens, upstream, vec, router, own)


def join_ffn(part, moe_part, cotangent, middle, gain, weights, number):
    _, rows, width = part.shape

    def kernel(part_ref, moe_ref, up_ref, middle_ref, gain_ref, w_ref, full_ref, out_ref, d_ref, sums_ref, got_ref, *scratch):
        d, z, _, _ = coordinates()
        greet(tensor_peers() + [{"dp": d ^ (4 * k)} for k in (1, 2, 3)])
        scatter, gather = direct_parts(part_ref, full_ref, scratch[:N_DIRECT])
        scatter.start()
        got, send, recv, local = scratch[2 * N_DIRECT :]
        side = Sends(
            [(w_ref.at[z ^ k], got.at[k], {"dp": d ^ (4 * k)}) for k in (1, 3, 2)], send, recv
        )
        side.start()
        load = pltpu.make_async_copy(w_ref.at[z], got.at[0], local.at[0])
        load.start()
        scatter_moe, gather_moe = direct_parts(moe_ref, out_ref, scratch[N_DIRECT : 2 * N_DIRECT])
        scatter_moe.start()
        middle = middle_ref[...]
        inv = second_moment(middle)
        d_normed = scatter.total()
        scaled = d_normed * gain_ref[...]
        d_middle = (
            up_ref[lax.axis_index("tensor")].astype(f32)
            + inv * scaled
            - middle * (inv * inv * inv) * jnp.mean(scaled * middle, axis=1, keepdims=True)
        )
        gather.start(d_middle)
        d_ref[...] = d_middle
        sums_ref[0:1] = column_sum(d_normed * middle * inv)
        moe_out = scatter_moe.total()
        output = middle_ref[...] + moe_out
        gather_moe.start(output)
        sums_ref[1:2] = column_sum(moe_out * moe_out)
        sums_ref[2:3] = column_sum(output * output)
        scatter.wait_send()
        scatter_moe.wait_send()
        gather.wait()
        gather_moe.wait()
        load.wait()
        side.wait()
        for half in range(2):
            total = got[0, half].astype(f32)
            for k in (1, 2, 3):
                total = total + got[k, half].astype(f32)
            got_ref[half] = total.astype(bf16)

    return pl.pallas_call(
        kernel,
        out_shape=(
            struct(part.shape, bf16),
            struct(part.shape, bf16),
            struct((rows, width), f32),
            struct((8, width), f32),
            struct(weights.shape[1:], weights.dtype),
        ),
        in_specs=[VMEM] * 5 + [HBM],
        out_specs=(HBM, HBM, VMEM, VMEM, VMEM),
        scratch_shapes=direct_scratch(rows, width) * 2
        + [pltpu.VMEM(weights.shape, weights.dtype)]
        + sems(3, 3, 1),
        compiler_params=comm_params(number, LIMIT),
        name="join_ffn",
        cost_estimate=cost(60),
    )(part, moe_part, cotangent, middle, gain, weights)


def attend_backward(d_attn, out_weight, heads, q, keys, values, codes, bounds, wide, logs, by_x, sent, number):
    n_sent = sent[0].shape[0]
    half, rest = pl.ds(0, HALF), pl.ds(HALF, n_sent - HALF)
    tok, width = d_attn.shape
    size = q.shape[2]
    stream, count = N_DP * tok, 2 * tok
    scale = size ** (-0.5)
    factor = scale * math.log2(math.e)

    def kernel(
        d_ref, w_ref, heads_ref, q_ref, k_ref, v_ref, code_ref, bound_ref, wide_ref, log_ref, x_ref, *refs
    ):
        (one_up, two_up, one_down), refs = refs[:3], refs[3:]
        (sums_ref, pair_ref, out_ref, shared_ref, below_ref, above_ref), scratch = refs[:6], refs[6:]
        d_heads, d_pair, made, got, d_query, out_part, out_got, x_got, up, down, far = scratch[:11]
        send, recv, osend, orecv, small_send, small_recv, fsend, frecv, wsend, wrecv, loaded = scratch[11:]
        me = lax.axis_index("dp")
        core, x_index = lax.rem(me, 2), lax.rem(me // 2, 2)
        greet(dp_peers() + [along_y(1), along_y(3)])
        first = Sends(
            [
                (two_up.at[half], far.at[half], along_y(1)),
                (two_up.at[rest], far.at[rest], along_y(3)),
            ],
            fsend,
            frecv,
        )
        first.start()
        loads = [
            pltpu.make_async_copy(one_up, up, loaded.at[0]),
            pltpu.make_async_copy(one_down, down, loaded.at[1]),
        ]
        for load in loads:
            load.start()
        second = Sends(
            [(up, below_ref, along_y(1)), (down, above_ref, along_y(3))], wsend, wrecv
        )
        along_x = remote(
            x_ref.at[1 - x_index], x_got, small_send.at[0], small_recv.at[0], {"dp": me ^ 2}
        )
        along_x.start()
        value = mm(d_ref[...], w_ref[...], NT).astype(bf16)
        d_heads[0] = value[:, 0:size]
        d_heads[1] = value[:, size : 2 * size]
        swap = remote(
            d_heads.at[1 - core], d_pair.at[core], small_send.at[1], small_recv.at[1], {"dp": me ^ 1}
        )
        swap.start()
        d_pair[core] = d_heads[core]
        for d in range(N_DP):
            out_part[d] = mm(d_ref[:, d * 128 : (d + 1) * 128], heads_ref[...], TN).astype(bf16)
        outs = [
            remote(out_part.at[me ^ k], out_got.at[k], osend.at[k], orecv.at[k], {"dp": me ^ k})
            for k in range(1, N_DP)
        ]
        swap.wait_recv()
        q, d_out = q_ref[...].reshape(count, size), d_pair[...].reshape(count, size)
        lowest, highest = bound_ref[0:1], bound_ref[1:2]
        log = log_ref[0:1]
        delta = jnp.sum((wide_ref[...] * d_out.astype(f32)).T, axis=0, keepdims=True)

        def send_to(step):
            return remote(
                made.at[me ^ step], got.at[step], send.at[step], recv.at[step], {"dp": me ^ step}
            )

        def block(group, acc):
            at = pl.ds(pl.multiple_of(group * tok, tok), tok)
            k = k_ref[at]
            scores = mm(k, q, NT) * factor
            code = code_ref[at][:, 0:1]
            seen = (code >= lowest) & (code <= highest)
            probs = jnp.where(seen, jnp.exp2(scores - log), 0.0)
            d_probs = mm(v_ref[at], d_out, NT)
            d_scores = (probs * (d_probs - delta)).astype(bf16)
            made[group, 0:tok] = (mm(d_scores, q) * scale).astype(bf16)
            made[group, tok : 2 * tok] = mm(probs.astype(bf16), d_out).astype(bf16)
            return acc + mm(k, d_scores, TN)

        def other(step, acc):
            acc = block(me ^ step, acc)
            send_to(step).start()
            return acc

        acc = lax.fori_loop(1, N_DP, other, jnp.zeros((size, count), f32))
        for copy in outs:
            copy.start()
        acc = block(me, acc)
        for load in loads:
            load.wait()
        for copy in first.copies:
            copy.wait_recv()

        def add(rows, target):
            def step(j, carry):
                cols = pl.ds(pl.multiple_of(j * 512, 512), 512)
                target[rows, cols] = (target[rows, cols].astype(f32) + far[rows, cols].astype(f32)).astype(bf16)
                return carry

            lax.fori_loop(0, width // 512, step, 0)

        add(half, up)
        add(rest, down)
        second.start()
        d_query[...] = (acc.T * scale).astype(bf16).reshape(2, tok, size)
        back = remote(
            d_query.at[1 - core], pair_ref.at[core], small_send.at[2], small_recv.at[2], {"dp": me ^ 1}
        )
        back.start()
        pair_ref[core] = d_query[core]
        got[0] = made[me]
        along_x.wait_recv()
        shared_ref[...] = x_got[...].astype(f32)
        for k in range(1, N_DP):
            send_to(k).wait_recv()
        for head in range(2):
            total = jnp.zeros((2 * tok, size), f32)
            for k in range(N_DP // 2):
                total = total + got[2 * k + (core + head) % 2].astype(f32)
            sums_ref[head] = total
        total = out_part[me].astype(f32)
        for k, copy in enumerate(outs):
            copy.wait_recv()
            total = total + out_got[k + 1].astype(f32)
        out_ref[...] = total
        back.wait_recv()
        for copy in [along_x, swap, back] + outs + first.copies:
            copy.wait_send()
        second.wait()
        for k in range(1, N_DP):
            send_to(k).wait_send()

    return pl.pallas_call(
        kernel,
        out_shape=(
            struct((2, 2 * tok, size), f32),
            struct(q.shape, bf16),
            struct((width // N_DP, 2 * size), f32),
            struct(by_x.shape[1:], f32),
            struct((n_sent, width), bf16),
            struct((n_sent, width), bf16),
        ),
        in_specs=[VMEM] * 10 + [HBM] * 4,
        out_specs=(VMEM,) * 4 + (HBM,) * 2,
        scratch_shapes=[
            pltpu.VMEM(q.shape, bf16),
            pltpu.VMEM(q.shape, bf16),
            pltpu.VMEM((N_DP, 2 * tok, size), bf16),
            pltpu.VMEM((N_DP, 2 * tok, size), bf16),
            pltpu.VMEM(q.shape, bf16),
            pltpu.VMEM((N_DP, 128, 2 * size), bf16),
            pltpu.VMEM((N_DP, 128, 2 * size), bf16),
            pltpu.VMEM(by_x.shape[1:], bf16),
        ]
        + [pltpu.VMEM((n_sent, width), bf16)] * 3
        + sems(N_DP, N_DP, N_DP, N_DP, 3, 3, 2, 2, 2, 2, 2),
        compiler_params=comm_params(number, LIMIT),
        name="attend_backward",
        cost_estimate=cost(65),
    )(d_attn, out_weight, heads, q, keys, values, codes, bounds, wide, logs, by_x, *sent)


def join_tail(part, layer_input, d_middle, gain, normed, d_proj, pack, own_grads, received, number):
    _, rows, width = part.shape
    small = pack.shape[1]
    wide = d_proj.shape[1]
    n_in, n_out = 8 + len(received), 6
    n_expert = own_grads.shape[0]
    units = n_expert // 3

    def kernel(*refs):
        part_ref, x_ref, d_ref, gain_ref, n_ref, proj_ref, pack_ref, own_grads_ref = refs[:8]
        received_refs = refs[8:n_in]
        full_ref, qkv_ref, one_ref, both_ref, in_ref, out_ref = refs[n_in : n_in + n_out]
        scratch = refs[n_in + n_out :]
        join, scratch = scratch[:N_JOIN], scratch[N_JOIN:]
        own, few, mine, more, send, recv, tsend, trecv = scratch[:8]
        qbuf, qgot, qsum, qin, csend, crecv, ksend, krecv = scratch[8:16]
        acc, others, lsem, osem = scratch[16:]
        me, t = lax.axis_index("dp"), lax.axis_index("tensor")
        core, chip = me % 2, me // 2
        greet(tensor_peers() + dp_peers())
        scatter, gather = join_parts(part_ref, full_ref, join)
        scatter.start()
        loads = [pltpu.make_async_copy(own_grads_ref, acc, lsem.at[0])] + [
            pltpu.make_async_copy(r, others.at[i], lsem.at[i + 1]) for i, r in enumerate(received_refs)
        ]
        for load in loads:
            load.start()
        across = []
        for c in range(8):
            for side in range(2):
                cols = slice((2 * c + side) * 128, (2 * c + side + 1) * 128)
                qbuf[c, side] = mm(n_ref[:, cols], proj_ref[...], TN).astype(bf16)
            across.append(
                remote(qbuf.at[c, 1 - core], qgot.at[c], csend.at[c], crecv.at[c], {"dp": me ^ 1})
            )
            across[-1].start()
        for c in range(8):
            across[c].wait_recv()
            qsum[c] = (qbuf[c, core].astype(f32) + qgot[c].astype(f32)).astype(bf16)
        chips = [
            remote(
                qsum.at[chip ^ k], qin.at[k], ksend.at[k], krecv.at[k], {"dp": me ^ (2 * k)}
            )
            for k in range(1, 8)
        ]
        for copy in chips:
            copy.start()
        resid = x_ref[t].astype(f32)
        inv = second_moment(resid)
        scatter.middle()
        d_normed = scatter.total()
        scaled = d_normed * gain_ref[...]
        gather.start(
            d_ref[...]
            + inv * scaled
            - resid * (inv * inv * inv) * jnp.mean(scaled * resid, axis=1, keepdims=True)
        )
        gain_grad = column_sum(d_normed * resid * inv)
        own[...] = pack_ref[...]
        for i in range(N_DP):
            own[i, small - 1 : small] = gain_grad[:, i * 128 : (i + 1) * 128]
        firsts = [
            remote(own.at[me ^ k], few.at[k], send.at[k], recv.at[k], {"dp": me ^ k})
            for k in range(1, N_DP)
        ]
        for copy in firsts:
            copy.start()
        gather.relay()
        value = own[me]
        for k in range(1, N_DP):
            firsts[k - 1].wait_recv()
            value = value + few[k]
        one_ref[...] = value
        mine[...] = value
        seconds = [
            remote(mine, more.at[k], tsend.at[k], trecv.at[k], {"tensor": t ^ k}) for k in range(1, N_T)
        ]
        for copy in seconds:
            copy.start()
        for load in loads:
            load.wait()

        def add(j, carry):
            cols = pl.ds(pl.multiple_of(j * 256, 256), 256)
            total = acc[:, cols]
            for i in range(len(received)):
                total = total + others[i, :, cols].astype(f32)
            acc[:, cols] = total
            return carry

        lax.fori_loop(0, width // 256, add, 0)
        stores = [
            pltpu.make_async_copy(acc.at[pl.ds(0, 2 * units)], in_ref, osem.at[0]),
            pltpu.make_async_copy(acc.at[pl.ds(2 * units, units)], out_ref, osem.at[1]),
        ]
        for store in stores:
            store.start()
        total = qsum[chip].astype(f32)
        for k in range(1, 8):
            chips[k - 1].wait_recv()
            total = total + qin[k].astype(f32)
        qkv_ref[...] = total
        for k in range(1, N_T):
            seconds[k - 1].wait_recv()
            value = value + more[k]
        both_ref[...] = value
        for copy in firsts + seconds + across + chips:
            copy.wait_send()
        scatter.wait_send()
        gather.wait()
        for store in stores:
            store.wait()

    return pl.pallas_call(
        kernel,
        out_shape=(
            struct(part.shape, bf16),
            struct((width // N_DP, wide), f32),
            struct((small, 128), f32),
            struct((small, 128), f32),
            struct((2 * units, width), f32),
            struct((units, width), f32),
        ),
        in_specs=[VMEM] * 7 + [HBM] * (n_in - 7),
        out_specs=(HBM, VMEM, VMEM, VMEM, HBM, HBM),
        scratch_shapes=join_scratch(rows, width)
        + [
            pltpu.VMEM((N_DP, small, 128), f32),
            pltpu.VMEM((N_DP, small, 128), f32),
            pltpu.VMEM((small, 128), f32),
            pltpu.VMEM((N_T, small, 128), f32),
        ]
        + sems(N_DP, N_DP, N_T, N_T)
        + [
            pltpu.VMEM((8, 2, 128, wide), bf16),
            pltpu.VMEM((8, 128, wide), bf16),
            pltpu.VMEM((8, 128, wide), bf16),
            pltpu.VMEM((8, 128, wide), bf16),
        ]
        + sems(8, 8, 8, 8)
        + [
            pltpu.VMEM((n_expert, width), f32),
            pltpu.VMEM((len(received), n_expert, width), bf16),
        ]
        + sems(n_in - 7, 2),
        compiler_params=comm_params(number, LIMIT),
        name="join_tail",
        cost_estimate=cost(55),
    )(part, layer_input, d_middle, gain, normed, d_proj, pack, own_grads, *received)


def doc_layout(lengths, token_index):
    doc_ends = jnp.cumsum(lengths)
    starts = doc_ends - lengths
    seq_ids = jnp.sum((token_index[:, None] >= doc_ends[None, :]).astype(jnp.int32), axis=1)
    member = seq_ids[:, None] == jnp.arange(lengths.shape[0], dtype=jnp.int32)[None, :]
    begins = jnp.sum(jnp.where(member, starts[None, :], 0), axis=1)
    offsets = token_index - begins
    return (seq_ids, offsets, offsets // DBLOCK)


def rope_tables(offsets, head_dim):
    half_dim = head_dim // 2
    frequencies = jnp.exp(
        jnp.arange(half_dim, dtype=f32) * (-2.0 * math.log(THETA) / head_dim)
    )
    angles = offsets.astype(f32)[:, None] * frequencies[None, :]
    return (jnp.cos(angles)[:, None, :], jnp.sin(angles)[:, None, :])


def rotate(vectors, cosine, sine):
    half_dim = vectors.shape[-1] // 2
    front, back = vectors[..., :half_dim], vectors[..., half_dim:]
    return jnp.concatenate([front * cosine - back * sine, back * cosine + front * sine], axis=-1)


def dot(pattern, a, b):
    return jnp.einsum(pattern, a, b, preferred_element_type=f32)


def on_device(
    layer_input,
    doc_lengths,
    expert_ids,
    attn_gain,
    qkv_weight,
    qkv_bias,
    out_weight,
    ffn_gain,
    router_weight,
    shared_gate,
    shared_in,
    shared_out,
    expert_in,
    expert_out,
    cotangent,
):
    tok, width = layer_input.shape
    dp, tn = lax.axis_index("dp"), lax.axis_index("tensor")
    experts_n = router_weight.shape[1]
    head_dim = qkv_weight.shape[3]
    stream = tok * N_DP
    part_rows = tok // N_T
    score_scale = head_dim ** (-0.5)
    eff = expert_out.shape[1]

    in_rows = expert_in[0].transpose(1, 2, 0).reshape(2 * eff, width)

    hot = jnp.sum(
        (expert_ids[:, :, None] == jnp.arange(experts_n, dtype=jnp.int32)[None, None, :]).astype(f32),
        axis=1,
    )
    before = (jnp.arange(tok)[:, None] > jnp.arange(tok)[None, :]).astype(bf16)
    rank = dot("ts,se->te", before, hot.astype(bf16))
    place = jnp.where(hot > 0, rank, -1.0).astype(jnp.int32).T
    _, offset = route_plane()
    served = lax.dynamic_slice_in_dim(place, GROUPS * ((dp // 4) ^ offset), GROUPS, 0)
    places = (
        (served[:, None, :] == jnp.arange(SLOTS, dtype=jnp.int32)[None, :, None])
        .astype(bf16)
        .reshape(GROUPS * SLOTS, tok)
    )
    returned = lax.dynamic_index_in_dim(place.reshape(GROUPS, 4, tok), offset, 1, keepdims=False)
    places_back = (
        (returned[:, None, :] == jnp.arange(SLOTS, dtype=jnp.int32)[None, :, None])
        .astype(bf16)
        .reshape(GROUPS * SLOTS, tok)
    )
    by_group = (GROUPS, SLOTS, width)
    up_send = dot("rt,td->rd", places, cotangent).astype(bf16)

    local_index = dp * tok + jnp.arange(tok, dtype=jnp.int32)
    pair_index = (dp // 2) * (2 * tok) + jnp.arange(2 * tok, dtype=jnp.int32)
    every_index = jnp.arange(stream, dtype=jnp.int32)
    _, pos_local, _ = doc_layout(doc_lengths, local_index)
    seq_pair, _, blk_pair = doc_layout(doc_lengths, pair_index)
    seq_all, _, blk_all = doc_layout(doc_lengths, every_index)
    codes = jnp.broadcast_to((seq_all * CODE + blk_all)[:, None], (stream, 128))
    bounds = jnp.stack([seq_pair * CODE, seq_pair * CODE + blk_pair] + [seq_pair] * 6)
    cosine, sine = rope_tables(pos_local, head_dim)
    residual = layer_input.astype(f32)
    inv_first = lax.rsqrt(jnp.mean(residual * residual, axis=1, keepdims=True) + EPSILON)
    normed_one = (residual * inv_first * attn_gain).astype(bf16)
    projected = dot("td,dshe->tshe", normed_one, qkv_weight) + qkv_bias.astype(f32)[None]
    q_own = rotate(projected[:, 0], cosine, sine).astype(bf16).transpose(1, 0, 2)
    k_own = rotate(projected[:, 1], cosine, sine).astype(bf16).transpose(1, 0, 2)
    v_own = projected[:, 2].astype(bf16).transpose(1, 0, 2)
    by_slice = (N_T, part_rows, width)
    out_flat = out_weight.reshape(2 * head_dim, width)
    keys, values, queries, wide, logs, heads_out, normed_two, middle, stats_one, *neighbours = attend_forward(
        k_own,
        v_own,
        q_own,
        codes,
        bounds,
        out_flat,
        layer_input.reshape(by_slice),
        ffn_gain.reshape(1, width),
        [in_rows, expert_out[0]],
        1,
    )
    normed_two = normed_two.reshape(tok, width)

    row_send = dot("rt,td->rd", places, normed_two).astype(bf16)
    own_expert = jnp.broadcast_to(
        (jnp.arange(experts_n, dtype=jnp.int32) == dp).astype(f32)[:, None], (experts_n, 128)
    )
    back_grads, back_out, mixed, shared_d_normed, got, gate_vec_part, router_part, own_grads, *sent = experts(
        row_send.reshape(by_group),
        up_send.reshape(by_group),
        *neighbours,
        in_rows,
        expert_out[0],
        normed_two,
        cotangent,
        shared_in.transpose(1, 2, 0).reshape(-1, width),
        shared_out,
        shared_gate.astype(f32).reshape(1, width),
        router_weight.T,
        own_expert,
        5,
    )

    by_z = got.reshape((4, 2) + got.shape[1:])

    def combine(rows):
        return dot("rt,rd->td", places_back, rows.reshape(-1, width))

    d_normed_part = (shared_d_normed + combine(back_grads)).astype(bf16)
    moe_part = (mixed + combine(back_out)).astype(bf16)
    d_attn, output, d_middle, stats_two, by_x = join_ffn(
        d_normed_part.reshape(by_slice),
        moe_part.reshape(by_slice),
        cotangent.reshape(by_slice),
        middle,
        ffn_gain.reshape(1, width),
        by_z,
        7,
    )
    d_attn = d_attn.reshape(tok, width)

    d_keys, d_queries, outproj_grad, shared_far, *received = attend_backward(
        d_attn, out_flat, heads_out, queries, keys, values, codes, bounds, wide, logs, by_x, sent, 9
    )
    shared_grads = lax.dynamic_index_in_dim(by_x, (dp // 2) % 2, 0, keepdims=False).astype(f32) + shared_far
    n_shared = shared_in.shape[2]

    cosine, sine = cosine[:, 0], sine[:, 0]
    d_proj = jnp.concatenate(
        [rotate(d_queries[h].astype(f32), cosine, -sine) for h in range(2)]
        + [rotate(d_keys[h, :tok], cosine, -sine) for h in range(2)]
        + [d_keys[h, tok:] for h in range(2)],
        axis=1,
    ).astype(bf16)
    d_normed_one = dot(
        "tshe,dshe->td", d_proj.reshape(tok, 3, 2, head_dim), qkv_weight
    ).astype(bf16)
    bias_part = jnp.sum(d_proj.astype(f32), axis=0)

    def slices(row):
        return row.reshape(-1, N_DP, 128).transpose(1, 0, 2)

    five = jnp.sum(jnp.concatenate([stats_one[:3], stats_two[1:3]]), axis=1)
    pack = jnp.concatenate(
        [
            slices(router_part),
            slices(gate_vec_part[0]),
            slices(stats_two[0]),
            jnp.broadcast_to(jnp.pad(five, (0, 123))[None, None], (N_DP, 1, 128)),
            jnp.pad(
                bias_part.reshape(6, N_DP, 8).transpose(1, 0, 2).reshape(N_DP, 1, 48),
                ((0, 0), (0, 4), (0, 80)),
            ),
        ],
        axis=1,
    )
    input_grad, qkv_grad, over_dp, over_both, expert_in_grad, expert_out_grad = join_tail(
        d_normed_one.reshape(by_slice),
        layer_input.reshape(by_slice),
        d_middle,
        attn_gain.reshape(1, width),
        normed_one,
        d_proj,
        pack,
        own_grads,
        received,
        10,
    )
    bias_grad = over_dp[19, :48].reshape(3, 2, 8)
    rms_stats = jnp.sqrt(over_both[18, :5] / (stream * width))

    return (
        output.reshape(tok, width),
        input_grad.reshape(tok, width).astype(f32),
        qkv_grad.reshape(width // N_DP, 3, 2, head_dim),
        bias_grad,
        outproj_grad.T.reshape(2, head_dim, width // N_DP),
        over_both[23],
        over_both[17],
        over_both[:16].T,
        over_both[16],
        shared_grads[: 2 * n_shared].reshape(2, n_shared, -1).transpose(2, 0, 1),
        shared_grads[2 * n_shared :],
        expert_in_grad.reshape(2, eff, width).transpose(2, 0, 1)[None],
        expert_out_grad[None],
        rms_stats,
    )


def solution(mesh):
    in_specs = (
        P("dp", None),
        P(),
        P("dp", None),
        P(),
        P(None, None, "tensor", None),
        P(None, "tensor", None),
        P("tensor", None, None),
        P(),
        P(),
        P(),
        P(None, None, "tensor"),
        P("tensor", None),
        P("dp", None, None, "tensor"),
        P("dp", "tensor", None),
        P("dp", None),
    )
    out_specs = (
        P("dp", None),
        P("dp", None),
        P("dp", None, "tensor", None),
        P(None, "tensor", "dp"),
        P("tensor", None, "dp"),
        P("dp"),
        P("dp"),
        P("dp", None),
        P("dp"),
        P("dp", None, "tensor"),
        P("tensor", "dp"),
        P("dp", None, None, "tensor"),
        P("dp", "tensor", None),
        P(),
    )
    return jax.shard_map(
        on_device, mesh=mesh, in_specs=in_specs, out_specs=out_specs, check_vma=False
    )
```

```python
import math

import jax
import jax.numpy as jnp
from jax import lax
from jax.experimental import pallas as pl
from jax.experimental.pallas import tpu as pltpu
from jax.sharding import PartitionSpec as P

DBLOCK = 256
EPSILON = 1e-06
THETA = 1000000.0
NEG_FILL = -1e30
MESH = pl.DeviceIdType.MESH
f32 = jnp.float32
bf16 = jnp.bfloat16
N_DP = 16
N_T = 8
SLOTS = 112
LIMIT = 48 * 1024 * 1024
CODE = 1 << 16

HBM = pl.BlockSpec(memory_space=pl.ANY)
VMEM = pl.BlockSpec(memory_space=pltpu.VMEM)
SMEM = pl.BlockSpec(memory_space=pltpu.SMEM)


def greet(peers, *more):
    barrier = pltpu.get_barrier_semaphore()
    for peer in peers:
        pl.semaphore_signal(barrier, inc=1, device_id=peer, device_id_type=MESH)
    count = len(peers)
    for rows in more:
        count = count + rows.greet()
    pl.semaphore_wait(barrier, count)


def remote(src, dst, send, recv, device):
    return pltpu.make_async_remote_copy(
        src_ref=src,
        dst_ref=dst,
        send_sem=send,
        recv_sem=recv,
        device_id=device,
        device_id_type=MESH,
    )


def dma(*shape):
    return pltpu.SemaphoreType.DMA(shape)


def cost(micros):
    return pl.CostEstimate(flops=0, bytes_accessed=int(micros * 3e6), transcendentals=0)


def comm_params(number, limit=None):
    return pltpu.CompilerParams(
        collective_id=number, has_side_effects=True, vmem_limit_bytes=limit
    )


NT = (((1,), (1,)), ((), ()))
TN = (((0,), (0,)), ((), ()))


def mm(a, b, dims=(((1,), (0,)), ((), ()))):
    return lax.dot_general(a, b, dims, preferred_element_type=f32)


GROUPS = 4
HALF = 256
ORDER = (4, 12, 2, 5, 13, 3, 8, 6, 14, 9, 7, 15, 10, 11, 1)
STEPS = (1, 3, 2, 4, 5, 7, 6)
CHUNKS = ((0, 48), (48, 64))


def sems(*counts):
    return [dma(*c) if isinstance(c, tuple) else dma(c) for c in counts]


def dp_peers():
    me = lax.axis_index("dp")
    return [{"dp": me ^ k} for k in range(1, N_DP)]


def tensor_peers():
    me = lax.axis_index("tensor")
    return [{"tensor": me ^ k} for k in range(1, N_T)]


def coordinates():
    d, t = lax.axis_index("dp"), lax.axis_index("tensor")
    return d, d // 4, t // 4, t % 4


def route_plane():
    d, z, _, y = coordinates()
    plane = 2 * ((z + d // 2) % 2) + d % 2
    return plane, y ^ plane


class Rows:
    def __init__(self, x_ref, out_ref, send, recv, local, back=False):
        self.x, self.out, self.send, self.recv, self.local, self.back = x_ref, out_ref, send, recv, local, back
        d, z, half, y = coordinates()
        plane, offset = route_plane()
        if back:
            experts = [{"dp": 4 * k + offset, "tensor": 4 * half + plane} for k in range(GROUPS)]
            target = y ^ (d % 4)
        else:
            experts = [{"dp": 4 * (z ^ offset) + j, "tensor": 4 * half + plane} for j in range(GROUPS)]
        groups = [
            {
                "dp": 4 * g + 2 * ((y // 2 + g) % 2) + y % 2,
                "tensor": 4 * half + (target if back else y ^ g ^ z),
            }
            for g in range(GROUPS)
        ]
        self.peers, self.sources = (groups, experts) if back else (experts, groups)
        self.slot = z
        self.mine = z if back else d % 4
        self.own = offset == 0
        if back:
            self.own = jnp.logical_and(self.own, d % 4 == 0)
        self.d = d

    def is_own(self, j):
        return jnp.logical_and(self.own, self.mine == j)

    def greet(self):
        barrier = pltpu.get_barrier_semaphore()
        for j in range(GROUPS):
            source = self.sources[j]

            @pl.when(jnp.logical_not(jnp.logical_and(self.own, self.slot == j)))
            def _():
                pl.semaphore_signal(barrier, inc=1, device_id=source, device_id_type=MESH)

        return GROUPS - self.own.astype(jnp.int32)

    def copy(self, j, c):
        rows = pl.ds(*CHUNKS[c])
        return remote(
            self.x.at[j, rows],
            self.out.at[self.slot, rows],
            self.send.at[c, j],
            self.recv.at[c, self.slot],
            self.peers[j],
        )

    def arrival(self, j, c):
        rows = pl.ds(*CHUNKS[c])
        return remote(
            self.x.at[j, rows],
            self.out.at[j, rows],
            self.send.at[c, j],
            self.recv.at[c, j],
            self.peers[j],
        )

    def inside(self):
        return pltpu.make_async_copy(self.x.at[self.mine], self.out.at[self.slot], self.local.at[0])

    def start_one(self, j):
        @pl.when(jnp.logical_not(self.is_own(j)))
        def _():
            for c in range(len(CHUNKS)):
                self.copy(j, c).start()

        @pl.when(self.is_own(j))
        def _():
            self.inside().start()

    def start(self):
        for j in range(GROUPS):
            self.start_one(j)

    def wait(self):
        @pl.when(self.own)
        def _():
            self.inside().wait()

        for c in range(len(CHUNKS)):
            for j in range(GROUPS):

                @pl.when(jnp.logical_not(self.is_own(j)))
                def _():
                    self.copy(j, c).wait_send()

                @pl.when(jnp.logical_not(jnp.logical_and(self.own, self.slot == j)))
                def _():
                    self.arrival(j, c).wait_recv()


ROW_SEMS = sems((len(CHUNKS), GROUPS), (len(CHUNKS), GROUPS), 1)


class Exchange:
    def __init__(self, x_ref, out_ref, send, recv, local):
        me = lax.axis_index("dp")
        self.copies = [
            remote(x_ref.at[me ^ k], out_ref.at[me], send.at[k], recv.at[k], {"dp": me ^ k})
            for k in ORDER
        ]
        self.copies.append(pltpu.make_async_copy(x_ref.at[me], out_ref.at[me], local.at[0]))

    def start(self):
        for copy in self.copies:
            copy.start()

    def wait(self):
        for copy in self.copies:
            copy.wait()


DP_SEMS = sems(N_DP, N_DP, 1)


class Swap:
    def __init__(self, x_ref, out_ref, send, recv, local):
        me = lax.axis_index("dp")
        core = lax.rem(me, 2)
        self.copies = [
            remote(x_ref.at[1 - core], out_ref.at[core], send.at[0], recv.at[0], {"dp": me ^ 1}),
            pltpu.make_async_copy(x_ref.at[core], out_ref.at[core], local.at[0]),
        ]

    start = Exchange.start
    wait = Exchange.wait


SWAP_SEMS = sems(1, 1, 1)


class DirectScatter:
    def __init__(self, part_ref, got, send, recv):
        self.me = lax.axis_index("tensor")
        self.part, self.got = part_ref, got
        self.copies = [
            remote(
                part_ref.at[self.me ^ k], got.at[k], send.at[k], recv.at[k], {"tensor": self.me ^ k}
            )
            for k in STEPS
        ]

    def start(self):
        for copy in self.copies:
            copy.start()

    def total(self):
        value = self.part[self.me].astype(f32)
        for k, copy in zip(STEPS, self.copies):
            copy.wait_recv()
            value = value + self.got[k].astype(f32)
        return value

    def wait_send(self):
        for copy in self.copies:
            copy.wait_send()


class DirectGather:
    def __init__(self, mine, full_ref, send, recv, local):
        me = lax.axis_index("tensor")
        self.mine = mine
        self.copies = [
            remote(mine, full_ref.at[me], send.at[k], recv.at[k], {"tensor": me ^ k}) for k in STEPS
        ]
        self.copies.append(pltpu.make_async_copy(mine, full_ref.at[me], local.at[0]))

    def start(self, value):
        self.mine[...] = value.astype(bf16)
        for copy in self.copies:
            copy.start()

    def wait(self):
        for copy in self.copies:
            copy.wait()


def direct_scratch(rows, width):
    return [
        pltpu.VMEM((N_T, rows, width), bf16),
        pltpu.VMEM((rows, width), bf16),
    ] + sems(N_T, N_T, N_T, N_T, 1)


N_DIRECT = 7


def direct_parts(part_ref, full_ref, scratch):
    got, mine, send, recv, asend, arecv, local = scratch
    return DirectScatter(part_ref, got, send, recv), DirectGather(mine, full_ref, asend, arecv, local)


class Scatter:
    def __init__(self, part_ref, got, mid, last, send, recv):
        t = lax.axis_index("tensor")
        y, half = t % 4, t // 4
        self.part, self.got, self.mid, self.last = part_ref, got, mid, last
        self.slots = (4 * (1 - half) + y, t)
        self.copies = [
            [
                remote(
                    part_ref.at[slot ^ k],
                    got.at[a, k],
                    send.at[a, k],
                    recv.at[a, k],
                    {"tensor": t ^ k},
                )
                for k in (1, 3, 2)
            ]
            for a, slot in enumerate(self.slots)
        ]
        self.across = remote(mid, last, send.at[0, 0], recv.at[0, 0], {"tensor": t ^ 4})

    def start(self):
        for copies in self.copies:
            for copy in copies:
                copy.start()

    def over_y(self, a):
        value = self.part[self.slots[a]].astype(f32)
        for k, copy in zip((1, 3, 2), self.copies[a]):
            copy.wait_recv()
            value = value + self.got[a, k].astype(f32)
        return value

    def middle(self):
        self.mid[...] = self.over_y(0).astype(bf16)
        self.across.start()

    def total(self):
        value = self.over_y(1)
        self.across.wait_recv()
        return value + self.last[...].astype(f32)

    def wait_send(self):
        for copies in self.copies:
            for copy in copies:
                copy.wait_send()
        self.across.wait_send()


class YGather:
    def __init__(self, mine, full_ref, send, recv, local):
        t = lax.axis_index("tensor")
        self.first = [
            remote(mine, full_ref.at[t], send.at[0, k], recv.at[0, k], {"tensor": t ^ k})
            for k in (1, 3, 2)
        ]
        self.second = [
            remote(full_ref.at[t ^ k], full_ref.at[t ^ k], send.at[1, k], recv.at[1, k], {"tensor": t ^ 4})
            for k in (1, 3, 2)
        ]
        self.across = remote(mine, full_ref.at[t], send.at[1, 0], recv.at[1, 0], {"tensor": t ^ 4})
        self.own = pltpu.make_async_copy(mine, full_ref.at[t], local.at[0])

    def start(self):
        for copy in self.first + [self.across, self.own]:
            copy.start()

    def relay(self):
        for first, second in zip(self.first, self.second):
            first.wait_recv()
            second.start()

    def wait(self):
        for copy in self.first:
            copy.wait_send()
        for copy in self.second + [self.across, self.own]:
            copy.wait()


class Sends:
    def __init__(self, messages, send, recv):
        self.copies = [
            remote(src, dst, send.at[i], recv.at[i], peer) for i, (src, dst, peer) in enumerate(messages)
        ]

    start = Exchange.start
    wait = Exchange.wait


def struct(shape, dtype):
    return jax.ShapeDtypeStruct(shape, dtype)


def column_sum(value):
    return jnp.sum(value, axis=0, keepdims=True)


def second_moment(value):
    return lax.rsqrt(jnp.mean(value * value, axis=1, keepdims=True) + EPSILON)


def codes_of(index, lengths_ref):
    end, seq, begin = 0, 0, 0
    for j in range(lengths_ref.shape[0]):
        end = end + lengths_ref[j]
        past = index >= end
        seq = seq + past.astype(jnp.int32)
        begin = jnp.where(past, end, begin)
    return seq * CODE, seq * CODE + lax.shift_right_arithmetic(index - begin, DBLOCK.bit_length() - 1)


def codes_of_keys(group, count, lengths_ref):
    index = group * count + lax.broadcasted_iota(jnp.int32, (count, 1), 0)
    return codes_of(index, lengths_ref)[1]


def codes_of_queries(chip, count, lengths_ref):
    index = chip * count + lax.broadcasted_iota(jnp.int32, (1, count), 1)
    return codes_of(index, lengths_ref)


def attend(q, state, k, v, code, bounds, factor):
    peak, total, acc = state
    scores = mm(k, q, NT) * factor
    seen = (code >= bounds[0]) & (code <= bounds[1])
    scores = jnp.where(seen, scores, NEG_FILL)
    new_peak = jnp.maximum(peak, jnp.max(scores, axis=0, keepdims=True))
    terms = jnp.exp2(scores - new_peak)
    shrink = jnp.exp2(peak - new_peak)
    total = total * shrink + jnp.sum(terms, axis=0, keepdims=True)
    acc = acc * shrink + mm(v, terms.astype(bf16), TN)
    return new_peak, total, acc


def along_y(shift):
    t = lax.axis_index("tensor")
    return {"tensor": 4 * (t // 4) + (t + shift) % 4}


def weights_along_y(weight_refs, n_rows, results, send, recv):
    messages = []
    for result, shift in zip(results, (1, 3)):
        at = 0
        for ref, count in zip(weight_refs, n_rows):
            messages.append((ref, result.at[pl.ds(at, count)], along_y(shift)))
            at += count
    return Sends(messages, send, recv)


def attend_forward(k, v, q, lengths, out_weight, layer_input, gain, weights, number):
    _, tok, size = q.shape
    n_rows = [w.shape[0] for w in weights]
    half, rest = pl.ds(0, HALF), pl.ds(HALF, sum(n_rows) - HALF)
    stream, count = N_DP * tok, 2 * tok
    _, rows, width = layer_input.shape
    factor = size ** (-0.5) * math.log2(math.e)

    def kernel(k_ref, v_ref, q_ref, lengths_ref, w_ref, x_ref, gain_ref, *refs):
        weight_refs, outs, scratch = refs[:2], refs[2:14], refs[14:]
        keys_ref, values_ref, pair_ref, wide_ref, log_ref, heads_ref, full_ref, middle_ref, stats_ref = outs[:9]
        keys, values, pair, own_out, heads, part = scratch[:6]
        send, recv, local = scratch[6:9]
        swap_sems, out_sems, store_sems, weight_sems = scratch[9:12], scratch[12:14], scratch[14], scratch[15:17]
        relay_sems, join = scratch[17:19], scratch[19:]
        me = lax.axis_index("dp")
        core = lax.rem(me, 2)
        greet(tensor_peers() + dp_peers())
        both = weights_along_y(weight_refs, n_rows, outs[9:11], *weight_sems)
        both.start()
        swap = Swap(q_ref, pair, *swap_sems)
        swap.start()

        def place(group):
            return pl.ds(pl.multiple_of(group * tok, tok), tok)

        def copies(step, head):
            return [
                remote(
                    own.at[head],
                    full.at[place(me)],
                    send.at[i, step],
                    recv.at[i, step],
                    {"dp": me ^ step},
                )
                for i, (own, full) in enumerate(((k_ref, keys), (v_ref, values)))
            ]

        for step in ORDER:
            for copy in copies(step, core if step % 2 == 0 else 1 - core):
                copy.start()
        locals_ = [
            pltpu.make_async_copy(own.at[core], full.at[place(me)], local.at[i])
            for i, (own, full) in enumerate(((k_ref, keys), (v_ref, values)))
        ]
        for copy in locals_:
            copy.start()
        swap.wait()
        for copy in locals_:
            copy.wait()
        queries = pair[...].reshape(count, size)
        limits = codes_of_queries(me // 2, count, lengths_ref)

        def block(group, state):
            at = place(group)
            code = codes_of_keys(group, tok, lengths_ref)
            return attend(queries, state, keys[at], values[at], code, limits, factor)

        def arrived(step, state):
            group = me ^ step
            for i, (own, full) in enumerate(((k_ref, keys), (v_ref, values))):
                remote(
                    own.at[core], full.at[place(group)], send.at[i, step], recv.at[i, step], {"dp": group}
                ).wait_recv()
            return block(group, state)

        state = block(
            me,
            (
                jnp.full((1, count), NEG_FILL, f32),
                jnp.zeros((1, count), f32),
                jnp.zeros((size, count), f32),
            ),
        )
        peak, total, acc = lax.fori_loop(1, N_DP, arrived, state)
        out = (acc / total).T
        wide_ref[...] = out
        log_ref[...] = jnp.broadcast_to(peak + jnp.log2(total), (8, count))
        own_out[...] = out.astype(bf16).reshape(2, tok, size)
        across = remote(
            own_out.at[1 - core], heads.at[core], out_sems[0].at[0], out_sems[1].at[0], {"dp": me ^ 1}
        )
        across.start()
        heads[core] = own_out[core]
        stores = [
            pltpu.make_async_copy(keys, keys_ref, store_sems.at[0]),
            pltpu.make_async_copy(values, values_ref, store_sems.at[1]),
            pltpu.make_async_copy(pair, pair_ref, store_sems.at[2]),
        ]
        for store in stores:
            store.start()
        across.wait_recv()
        heads_ref[:, 0:size] = heads[0]
        heads_ref[:, size : 2 * size] = heads[1]

        def project(j, carry):
            cols = pl.ds(pl.multiple_of(j * 512, 512), 512)
            value = mm(heads_ref[...], w_ref[:, cols])
            part[:, :, cols] = value.reshape(N_T, rows, 512).astype(bf16)
            return carry

        lax.fori_loop(0, width // 512, project, 0)
        scatter, gather = direct_parts(part, full_ref, join)
        scatter.start()
        for copy in both.copies:
            copy.wait_recv()
        below_ref, above_ref, far_ref = outs[9:]
        relay = Sends(
            [
                (below_ref.at[half], far_ref.at[half], along_y(1)),
                (above_ref.at[rest], far_ref.at[rest], along_y(3)),
            ],
            *relay_sems,
        )
        relay.start()
        resid = x_ref[lax.axis_index("tensor")].astype(f32)
        attn_out = scatter.total()
        middle = resid + attn_out
        gather.start(middle * second_moment(middle) * gain_ref[...])
        middle_ref[...] = middle
        stats_ref[0:1] = column_sum(resid * resid)
        stats_ref[1:2] = column_sum(attn_out * attn_out)
        stats_ref[2:3] = column_sum(middle * middle)
        for step in ORDER:
            for copy in copies(step, core):
                copy.wait_send()
        across.wait_send()
        scatter.wait_send()
        for store in stores:
            store.wait()
        gather.wait()
        for copy in both.copies:
            copy.wait_send()
        relay.wait()

    return pl.pallas_call(
        kernel,
        out_shape=(
            struct((stream, size), bf16),
            struct((stream, size), bf16),
            struct(q.shape, bf16),
            struct((count, size), f32),
            struct((8, count), f32),
            struct((tok, 2 * size), bf16),
            struct(layer_input.shape, bf16),
            struct((rows, width), f32),
            struct((8, width), f32),
        )
        + (struct((sum(n_rows), width), bf16),) * 3,
        in_specs=[HBM] * 3 + [SMEM] + [VMEM] * 3 + [HBM] * 2,
        out_specs=(HBM,) * 3 + (VMEM,) * 3 + (HBM,) + (VMEM,) * 2 + (HBM,) * 3,
        scratch_shapes=[
            pltpu.VMEM((stream, size), bf16),
            pltpu.VMEM((stream, size), bf16),
            pltpu.VMEM(q.shape, bf16),
            pltpu.VMEM(q.shape, bf16),
            pltpu.VMEM(q.shape, bf16),
            pltpu.VMEM(layer_input.shape, bf16),
        ]
        + sems((2, N_DP), (2, N_DP), 2)
        + SWAP_SEMS
        + sems(1, 1, 3, 4, 4, 2, 2)
        + direct_scratch(rows, width),
        compiler_params=comm_params(number, LIMIT),
        name="attend_forward",
        cost_estimate=cost(85),
    )(k, v, q, lengths, out_weight, layer_input, gain, *weights)


def sigmoid(x):
    return 1.0 / (1.0 + jnp.exp(-x))


TILE = 176
NOW = 256
SOON = 96


def shared_expert(x_ref, up_ref, w_ref, vec_ref, part_ref, d_ref, grads_ref, row_ref, low_ref):
    hidden = w_ref.shape[0] // 3
    vec = vec_ref[...]
    gate = sigmoid(jnp.sum(x_ref[...].astype(f32) * vec, axis=1, keepdims=True))
    low_ref[...] = (gate * up_ref[...].astype(f32)).astype(bf16)
    part_ref[...] = jnp.zeros_like(part_ref)
    d_ref[...] = jnp.zeros_like(d_ref)

    def tile(i, carry):
        rows = [pl.ds(pl.multiple_of(i * TILE + k * hidden, 16), TILE) for k in range(3)]
        x, d_out = x_ref[...], low_ref[...]
        gate_part = mm(w_ref[rows[0]], x, NT)
        up_part = mm(w_ref[rows[1]], x, NT)
        sig = sigmoid(gate_part)
        act = gate_part * sig
        unit = (act * up_part).astype(bf16)
        d_unit = mm(w_ref[rows[2]], d_out, NT)
        d_gate = (d_unit * up_part * sig * (1.0 + gate_part * (1.0 - sig))).astype(bf16)
        d_up = (d_unit * act).astype(bf16)

        def block(j, carry):
            cols = pl.ds(pl.multiple_of(j * 256, 256), 256)
            xs, ds = x_ref[:, cols], low_ref[:, cols]
            part_ref[:, cols] += mm(unit, w_ref[rows[2], cols], TN)
            d_ref[:, cols] += mm(d_gate, w_ref[rows[0], cols], TN) + mm(d_up, w_ref[rows[1], cols], TN)
            for k, grad in enumerate((mm(d_gate, xs), mm(d_up, xs), mm(unit, ds))):
                grad = grad.astype(bf16)
                grads_ref[j, 0, rows[k]] = grad[:, :128]
                grads_ref[j, 1, rows[k]] = grad[:, 128:]
            return carry

        return lax.fori_loop(0, x.shape[1] // 256, block, carry)

    lax.fori_loop(0, hidden // TILE, tile, 0)
    total = part_ref[...]
    d_logit = jnp.sum(up_ref[...].astype(f32) * total, axis=1, keepdims=True) * gate * (1.0 - gate)
    part_ref[...] = gate * total
    d_ref[...] += d_logit * vec
    row_ref[...] = column_sum(d_logit * x_ref[...].astype(f32))


class Routed:
    def __init__(self, x_ref, up_ref, w_ref, router_ref, own, acc, dgu_ref, unit_ref, slope_ref, router_grad_ref):
        groups, slots, self.width = x_ref.shape
        self.rows, self.units = groups * slots, w_ref.shape[1] // 3
        self.x_ref, self.up_ref, self.w_ref, self.router_ref, self.own = x_ref, up_ref, w_ref, router_ref, own
        self.acc, self.dgu_ref, self.unit_ref, self.slope_ref = acc, dgu_ref, unit_ref, slope_ref
        self.router_grad_ref = router_grad_ref

    def flat(self, ref):
        return ref[...].reshape(self.rows, self.width)

    def start(self):
        logits = mm(self.router_ref[...], self.flat(self.x_ref), NT)
        terms = jnp.exp(logits - jnp.max(logits, axis=0, keepdims=True))
        self.probs = terms / jnp.sum(terms, axis=0, keepdims=True)
        self.gate = jnp.sum(self.probs * self.own, axis=0, keepdims=True)
        self.acc[...] = jnp.zeros_like(self.acc)

    def blocks(self, body):
        def block(j, carry):
            body(pl.ds(pl.multiple_of(j * 512, 512), 512))
            return carry

        lax.fori_loop(0, self.width // 512, block, 0)

    def forward(self):
        units, rows, w_ref = self.units, self.rows, self.w_ref

        def piece(i, carry):
            gate_part = mm(w_ref[i, 0:units], self.flat(self.x_ref), NT)
            up_part = mm(w_ref[i, units : 2 * units], self.flat(self.x_ref), NT)
            sig = sigmoid(gate_part)
            act = gate_part * sig
            gated = (act * up_part * self.gate).astype(bf16)
            slope = self.gate * up_part * sig * (1.0 + gate_part * (1.0 - sig))
            self.slope_ref[i, 0] = slope.astype(bf16)
            self.slope_ref[i, 1] = (self.gate * act).astype(bf16)
            self.unit_ref[i] = gated

            def add(cols):
                self.acc[0:rows, cols] += mm(gated, w_ref[i, 2 * units : 3 * units, cols], TN)

            self.blocks(add)
            return carry

        lax.fori_loop(0, GROUPS, piece, 0)

    def backward(self):
        units, rows, w_ref = self.units, self.rows, self.w_ref

        def piece(i, gated_d_gate):
            raw = mm(w_ref[i, 2 * units : 3 * units], self.flat(self.up_ref), NT)
            d_gate = (raw * self.slope_ref[i, 0].astype(f32)).astype(bf16)
            d_up = (raw * self.slope_ref[i, 1].astype(f32)).astype(bf16)
            self.dgu_ref[i, 0:units] = d_gate
            self.dgu_ref[i, units : 2 * units] = d_up

            def add(cols):
                self.acc[rows : 2 * rows, cols] += mm(d_gate, w_ref[i, 0:units, cols], TN) + mm(
                    d_up, w_ref[i, units : 2 * units, cols], TN
                )

            self.blocks(add)
            return gated_d_gate + jnp.sum(self.unit_ref[i].astype(f32) * raw, axis=0, keepdims=True)

        gated_d_gate = lax.fori_loop(0, GROUPS, piece, jnp.zeros((1, rows), f32))
        d_logits = (gated_d_gate * (self.own - self.probs)).astype(bf16)
        self.router_grad_ref[...] = mm(d_logits, self.flat(self.x_ref))
        self.acc[rows : 2 * rows] += mm(d_logits, self.router_ref[...], TN)


def experts(places, below, above, far_rows, in_rows, out_rows, tokens, upstream, w_in, w_out, vec, router, own, number):
    slots = places.shape[1]
    tok, width = tokens.shape
    hidden, units = w_out.shape[0], out_rows.shape[0]
    n_rows = GROUPS * slots

    def kernel(*refs):
        (below_ref, above_ref, far_ref, in_ref, out_ref, w_in_ref, w_out_ref), refs = refs[:7], refs[7:]
        (places_ref, x_ref, up_ref, vec_ref, router_ref, own_ref), refs = refs[:6], refs[6:]
        (back_d, back_out, part_ref, d_ref, by_z_ref, row_ref, router_grad_ref, mine_ref, *sent_refs), refs = (
            refs[:11],
            refs[11:],
        )
        (weights, low, grads, xs, us, w, acc, dgu, unit, slope, far, send_d, send_out), refs = refs[:13], refs[13:]
        row_sems, refs = [refs[3 * i : 3 * i + 3] for i in range(4)], refs[12:]
        csend, crecv, loaded, stored = refs
        d = lax.axis_index("dp")
        core = lax.rem(d, 2)
        out_x = Rows(send_d, xs, *row_sems[0])
        out_u = Rows(send_out, us, *row_sems[1])
        in_d = Rows(send_d, back_d, *row_sems[2], back=True)
        in_out = Rows(send_out, back_out, *row_sems[3], back=True)
        greet([{"dp": d ^ 1}], out_x, in_d)
        for j in range(GROUPS):
            send_d[j] = mm(places_ref[j], x_ref[...]).astype(bf16)
            out_x.start_one(j)
        for j in range(GROUPS):
            send_out[j] = mm(places_ref[j], up_ref[...]).astype(bf16)
            out_u.start_one(j)
        loads = [
            pltpu.make_async_copy(src, dst, loaded.at[i])
            for i, (src, dst) in enumerate(
                (
                    (w_in_ref, weights.at[pl.ds(0, 2 * hidden)]),
                    (w_out_ref, weights.at[pl.ds(2 * hidden, hidden)]),
                    (in_ref, w.at[0, pl.ds(0, 2 * units)]),
                    (out_ref, w.at[0, pl.ds(2 * units, units)]),
                    (above_ref, w.at[1]),
                    (far_ref, w.at[2]),
                    (below_ref, w.at[3]),
                )
            )
        ]
        for load in loads:
            load.start()
        for load in loads[:2]:
            load.wait()
        shared_expert(x_ref, up_ref, weights, vec_ref, part_ref, d_ref, grads, row_ref, low)
        cores = Sends(
            [(grads.at[chip, 1 - core], far.at[chip], {"dp": d ^ 1}) for chip in range(8)], csend, crecv
        )
        cores.start()
        for load in loads[2:]:
            load.wait()
        out_x.wait()
        routed = Routed(xs, us, w, router_ref, own_ref[:, 0:1], acc, dgu, unit, slope, router_grad_ref)
        routed.start()

        routed.forward()
        out_u.wait()
        send_out[...] = acc[0:n_rows].astype(bf16).reshape(GROUPS, slots, width)
        in_out.start()
        routed.backward()
        send_d[...] = acc[n_rows : 2 * n_rows].astype(bf16).reshape(GROUPS, slots, width)
        in_d.start()

        def block(j, carry):
            cols = pl.ds(pl.multiple_of(j * 256, 256), 256)
            x, up = xs[:, :, cols].reshape(n_rows, 256), us[:, :, cols].reshape(n_rows, 256)
            acc[0 : 2 * units, cols] = mm(dgu[0], x)
            acc[2 * units : 3 * units, cols] = mm(unit[0], up)
            for i in range(1, GROUPS):
                at = 3 * units * (i - 1)
                weights[at : at + 2 * units, cols] = mm(dgu[i], x).astype(bf16)
                weights[at + 2 * units : at + 3 * units, cols] = mm(unit[i], up).astype(bf16)
            return carry

        lax.fori_loop(0, width // 256, block, 0)
        stores = [pltpu.make_async_copy(acc.at[pl.ds(0, 3 * units)], mine_ref, stored.at[0])] + [
            pltpu.make_async_copy(weights.at[pl.ds(3 * units * i, 3 * units)], ref, stored.at[i + 1])
            for i, ref in enumerate(sent_refs)
        ]
        for store in stores:
            store.start()
        for chip in range(8):
            cores.copies[chip].wait_recv()
            far[chip] = (far[chip].astype(f32) + grads[chip, core].astype(f32)).astype(bf16)
            stores.append(pltpu.make_async_copy(far.at[chip], by_z_ref.at[chip], stored.at[4 + chip]))
            stores[-1].start()
        for copy in cores.copies:
            copy.wait_send()
        in_out.wait()
        in_d.wait()
        for store in stores:
            store.wait()

    row = struct((GROUPS, slots, width), bf16)
    return pl.pallas_call(
        kernel,
        out_shape=(
            row,
            row,
            struct((tok, width), f32),
            struct((tok, width), f32),
            struct((8, 3 * hidden, 128), bf16),
            struct((1, width), f32),
            struct((router.shape[0], width), f32),
            struct((3 * units, width), f32),
        )
        + (struct((3 * units, width), bf16),) * 3,
        in_specs=[HBM] * 7 + [VMEM] * 6,
        out_specs=(HBM, HBM, VMEM, VMEM, HBM, VMEM, VMEM) + (HBM,) * 4,
        scratch_shapes=[
            pltpu.VMEM((3 * hidden, width), bf16),
            pltpu.VMEM((tok, width), bf16),
            pltpu.VMEM((8, 2, 3 * hidden, 128), bf16),
            pltpu.VMEM(row.shape, bf16),
            pltpu.VMEM(row.shape, bf16),
            pltpu.VMEM((GROUPS, 3 * units, width), bf16),
            pltpu.VMEM((2 * n_rows, width), f32),
            pltpu.VMEM((GROUPS, 2 * units, n_rows), bf16),
            pltpu.VMEM((GROUPS, units, n_rows), bf16),
            pltpu.VMEM((GROUPS, 2, units, n_rows), bf16),
            pltpu.VMEM((8, 3 * hidden, 128), bf16),
            pltpu.VMEM(row.shape, bf16),
            pltpu.VMEM(row.shape, bf16),
        ]
        + ROW_SEMS * 4
        + sems(8, 8, 7, 12),
        compiler_params=comm_params(number, 61 * 1024 * 1024),
        name="experts",
        cost_estimate=cost(115),
    )(below, above, far_rows, in_rows, out_rows, w_in, w_out, places, tokens, upstream, vec, router, own)


def backward(
    part, moe_part, cotangent, middle, gain, out_weight, heads, q, keys, values, wide, logs, lengths, weights, sent, number
):
    _, rows, width = part.shape
    tok, size = q.shape[1:]
    stream, count = N_DP * tok, 2 * tok
    scale = size ** (-0.5)
    factor = scale * math.log2(math.e)
    n_sent = sent[0].shape[0]
    half, rest = pl.ds(0, HALF), pl.ds(HALF, n_sent - HALF)
    now, later = pl.ds(0, NOW), pl.ds(NOW, n_sent - NOW)

    def kernel(*refs):
        (part_ref, moe_ref, up_in_ref, middle_ref, gain_ref, w_ref, heads_ref, q_ref, k_ref, v_ref), refs = (
            refs[:10],
            refs[10:],
        )
        (wide_ref, log_ref, lengths_ref, by_z_ref, one_up, two_up, one_down), refs = refs[:7], refs[7:]
        (d_middle_ref, stats_ref, sums_ref, pair_ref, out_ref, by_x), refs = refs[:6], refs[6:]
        (full_ref, below_ref, above_ref, up_ref, down_ref), refs = refs[:5], refs[5:]
        (full, d_attn, out_slice, d_heads, d_pair, made, got, d_query, out_part, out_got), refs = refs[:10], refs[10:]
        (z_got, up, down, far), refs = refs[:4], refs[4:]
        direct, refs = refs[:N_DIRECT], refs[N_DIRECT:]
        moe_scratch, refs = refs[:5], refs[5:]
        send, recv, osend, orecv, small_send, small_recv, fsend, frecv, wsend, wrecv, loaded = refs[:11]
        zsend, zrecv, gather_sems = refs[11], refs[12], refs[13:]
        me, z, _, _ = coordinates()
        t = lax.axis_index("tensor")
        core = lax.rem(me, 2)
        greet(dp_peers() + tensor_peers())
        scatter, gather = direct_parts(part_ref, full, direct)
        scatter.start()
        scatter_moe = Scatter(moe_ref, *moe_scratch)
        scatter_moe.start()
        over_z = Sends(
            [(by_z_ref.at[z ^ k], z_got.at[k], {"dp": me ^ (4 * k)}) for k in (1, 3, 2)], zsend, zrecv
        )
        over_z.start()
        loads = [
            pltpu.make_async_copy(one_up, up, loaded.at[0]),
            pltpu.make_async_copy(one_down, down, loaded.at[1]),
            pltpu.make_async_copy(by_z_ref.at[z], z_got.at[0], loaded.at[2]),
        ]
        for load in loads:
            load.start()
        middle = middle_ref[...]
        inv = second_moment(middle)
        d_normed = scatter.total()
        scaled = d_normed * gain_ref[...]
        d_middle = (
            up_in_ref[t].astype(f32)
            + inv * scaled
            - middle * (inv * inv * inv) * jnp.mean(scaled * middle, axis=1, keepdims=True)
        )
        gather.start(d_middle)
        first = Sends(
            [
                (two_up.at[half], far.at[half], along_y(1)),
                (two_up.at[rest], far.at[rest], along_y(3)),
            ],
            fsend,
            frecv,
        )
        first.start()
        d_middle_ref[...] = d_middle
        stats_ref[0:1] = column_sum(d_normed * middle * inv)
        scatter_moe.middle()
        gather.wait()
        d_attn[...] = full[...].astype(f32).reshape(tok, width).astype(bf16)
        value = mm(d_attn[...], w_ref[...], NT).astype(bf16)
        d_heads[0] = value[:, 0:size]
        d_heads[1] = value[:, size : 2 * size]
        swap = remote(
            d_heads.at[1 - core], d_pair.at[core], small_send.at[1], small_recv.at[1], {"dp": me ^ 1}
        )
        swap.start()
        d_pair[core] = d_heads[core]
        for d in range(N_DP):
            out_part[d] = mm(d_attn[:, d * 128 : (d + 1) * 128], heads_ref[...], TN).astype(bf16)
        outs = [
            remote(out_part.at[me ^ k], out_got.at[k], osend.at[k], orecv.at[k], {"dp": me ^ k})
            for k in range(1, N_DP)
        ]
        for copy in outs:
            copy.start()
        moe_out = scatter_moe.total()
        output = middle_ref[...] + moe_out
        out_slice[...] = output.astype(bf16)
        gather_out = YGather(out_slice, full_ref, *gather_sems)
        gather_out.start()
        stats_ref[1:2] = column_sum(moe_out * moe_out)
        stats_ref[2:3] = column_sum(output * output)

        swap.wait_recv()
        q, d_out = q_ref[...].reshape(count, size), d_pair[...].reshape(count, size)
        lowest, highest = codes_of_queries(me // 2, count, lengths_ref)
        log = log_ref[0:1]
        delta = jnp.sum((wide_ref[...] * d_out.astype(f32)).T, axis=0, keepdims=True)

        def send_to(step):
            return remote(
                made.at[me ^ step], got.at[step], send.at[step], recv.at[step], {"dp": me ^ step}
            )

        def block(group, acc):
            at = pl.ds(pl.multiple_of(group * tok, tok), tok)
            k = k_ref[at]
            scores = mm(k, q, NT) * factor
            code = codes_of_keys(group, tok, lengths_ref)
            seen = (code >= lowest) & (code <= highest)
            probs = jnp.where(seen, jnp.exp2(scores - log), 0.0)
            d_probs = mm(v_ref[at], d_out, NT)
            d_scores = (probs * (d_probs - delta)).astype(bf16)
            made[group, 0:tok] = (mm(d_scores, q) * scale).astype(bf16)
            made[group, tok : 2 * tok] = mm(probs.astype(bf16), d_out).astype(bf16)
            return acc + mm(k, d_scores, TN)

        def other(step, acc):
            acc = block(me ^ step, acc)
            send_to(step).start()
            return acc

        acc = lax.fori_loop(1, N_DP, other, jnp.zeros((size, count), f32))
        acc = block(me, acc)
        d_query[...] = (acc.T * scale).astype(bf16).reshape(2, tok, size)
        back = remote(
            d_query.at[1 - core], pair_ref.at[core], small_send.at[2], small_recv.at[2], {"dp": me ^ 1}
        )
        back.start()
        pair_ref[core] = d_query[core]

        loads[2].wait()
        over_z.wait()
        for side in range(2):
            total = z_got[0, side].astype(f32)
            for k in (1, 2, 3):
                total = total + z_got[k, side].astype(f32)
            by_x[side] = total.astype(bf16)

        for load in loads[:2]:
            load.wait()
        for copy in first.copies:
            copy.wait_recv()

        def add(rows, target):
            def step(j, carry):
                cols = pl.ds(pl.multiple_of(j * 512, 512), 512)
                target[rows, cols] = (target[rows, cols].astype(f32) + far[rows, cols].astype(f32)).astype(bf16)
                return carry

            lax.fori_loop(0, width // 512, step, 0)

        add(half, up)
        add(rest, down)
        second = Sends(
            [(up.at[now], below_ref, along_y(1)), (down.at[now], above_ref, along_y(3))], wsend, wrecv
        )
        second.start()
        stores = [
            pltpu.make_async_copy(up.at[later], up_ref, loaded.at[3]),
            pltpu.make_async_copy(down.at[later], down_ref, loaded.at[4]),
        ]
        for store in stores:
            store.start()
        gather_out.relay()
        got[0] = made[me]
        for k in range(1, N_DP):
            send_to(k).wait_recv()
        for head in range(2):
            total = jnp.zeros((2 * tok, size), f32)
            for k in range(N_DP // 2):
                total = total + got[2 * k + (core + head) % 2].astype(f32)
            sums_ref[head] = total
        total = out_part[me].astype(f32)
        for k, copy in enumerate(outs):
            copy.wait_recv()
            total = total + out_got[k + 1].astype(f32)
        out_ref[...] = total
        back.wait_recv()
        for copy in [swap, back] + outs + first.copies:
            copy.wait_send()
        scatter.wait_send()
        scatter_moe.wait_send()
        for store in stores:
            store.wait()
        gather_out.wait()
        second.wait()
        for k in range(1, N_DP):
            send_to(k).wait_send()

    return pl.pallas_call(
        kernel,
        out_shape=(
            struct((rows, width), f32),
            struct((8, width), f32),
            struct((2, 2 * tok, size), f32),
            struct(q.shape, bf16),
            struct((width // N_DP, 2 * size), f32),
            struct(weights.shape[1:], bf16),
            struct(part.shape, bf16),
            struct((NOW, width), bf16),
            struct((NOW, width), bf16),
            struct((n_sent - NOW, width), bf16),
            struct((n_sent - NOW, width), bf16),
        ),
        in_specs=[VMEM] * 12 + [SMEM] + [HBM] * 4,
        out_specs=(VMEM,) * 6 + (HBM,) * 5,
        scratch_shapes=[
            pltpu.VMEM(part.shape, bf16),
            pltpu.VMEM((tok, width), bf16),
            pltpu.VMEM((rows, width), bf16),
            pltpu.VMEM(q.shape, bf16),
            pltpu.VMEM(q.shape, bf16),
            pltpu.VMEM((N_DP, 2 * tok, size), bf16),
            pltpu.VMEM((N_DP, 2 * tok, size), bf16),
            pltpu.VMEM(q.shape, bf16),
            pltpu.VMEM((N_DP, 128, 2 * size), bf16),
            pltpu.VMEM((N_DP, 128, 2 * size), bf16),
            pltpu.VMEM(weights.shape, bf16),
        ]
        + [pltpu.VMEM((n_sent, width), bf16)] * 3
        + direct_scratch(rows, width)
        + [pltpu.VMEM((2, 4, rows, width), bf16)]
        + [pltpu.VMEM((rows, width), bf16)] * 2
        + sems((2, 4), (2, 4))
        + sems(N_DP, N_DP, N_DP, N_DP, 3, 3, 2, 2, 2, 2, 5, 3, 3, (2, 4), (2, 4), 1),
        compiler_params=comm_params(number, LIMIT),
        name="backward",
        cost_estimate=cost(110),
    )(
        part, moe_part, cotangent, middle, gain, out_weight, heads, q, keys, values, wide, logs, lengths, weights, *sent
    )


def join_tail(part, layer_input, d_middle, gain, normed, d_proj, smalls, own_grads, received, waiting, by_x, number):
    _, rows, width = part.shape
    small = 32
    wide = d_proj.shape[1]
    n_in, n_out = 14 + len(received), 8
    n_hidden = by_x.shape[1] // 3
    n_expert = own_grads.shape[0]
    n_late = n_expert - NOW - SOON
    first = pl.ds(0, NOW)
    parts = ((0, SOON), (SOON, n_late))
    units = n_expert // 3

    def kernel(*refs):
        part_ref, x_ref, d_ref, gain_ref, n_ref, proj_ref = refs[:6]
        router_ref, vec_ref, one_stats, two_stats, own_grads_ref = refs[6:11]
        received_refs, (up_ref, down_ref, by_x_ref) = refs[11 : n_in - 3], refs[n_in - 3 : n_in]
        full_ref, qkv_ref, one_ref, both_ref, shared_in_ref, shared_out_ref, in_ref, out_ref = refs[n_in : n_in + n_out]
        scratch = refs[n_in + n_out :]
        join, scratch = scratch[:N_DIRECT], scratch[N_DIRECT:]
        own, few, summed, more, send, recv, tsend, trecv = scratch[:8]
        qbuf, qgot, qsum, qin, csend, crecv, ksend, krecv = scratch[8:16]
        acc, others, lsem, osem, esend, erecv, x_near, x_far, xsend, xrecv = scratch[16:]
        me, t = lax.axis_index("dp"), lax.axis_index("tensor")
        core, chip = me % 2, me // 2
        greet(tensor_peers() + dp_peers())
        got, mine, jsend, jrecv, asend, arecv, alocal = join
        scatter = DirectScatter(part_ref, got, jsend, jrecv)
        gather = YGather(mine, full_ref, asend, arecv, alocal)
        scatter.start()
        rest = Sends(
            [
                (ref.at[pl.ds(at, n)], others.at[i, pl.ds(NOW + at, n)], along_y(shift))
                for at, n in parts
                for i, (ref, shift) in enumerate(((up_ref, 1), (down_ref, 3)))
            ],
            esend,
            erecv,
        )
        for copy in rest.copies[:2]:
            copy.start()
        loads = [pltpu.make_async_copy(own_grads_ref, acc, lsem.at[0])] + [
            pltpu.make_async_copy(r, others.at[i, first], lsem.at[i + 1])
            for i, r in enumerate(received_refs)
        ]
        for load in loads:
            load.start()
        x_index = chip % 2
        along_x = remote(by_x_ref.at[1 - x_index], x_far, xsend.at[0], xrecv.at[0], {"dp": me ^ 2})
        along_x.start()
        near = pltpu.make_async_copy(by_x_ref.at[x_index], x_near, xsend.at[1])
        near.start()
        across = []
        for c in range(8):
            for side in range(2):
                cols = slice((2 * c + side) * 128, (2 * c + side + 1) * 128)
                qbuf[c, side] = mm(n_ref[:, cols], proj_ref[...], TN).astype(bf16)
            across.append(
                remote(qbuf.at[c, 1 - core], qgot.at[c], csend.at[c], crecv.at[c], {"dp": me ^ 1})
            )
            across[-1].start()
        for c in range(8):
            across[c].wait_recv()
            qsum[c] = (qbuf[c, core].astype(f32) + qgot[c].astype(f32)).astype(bf16)
        chips = [
            remote(
                qsum.at[chip ^ k], qin.at[k], ksend.at[k], krecv.at[k], {"dp": me ^ (2 * k)}
            )
            for k in range(1, 8)
        ]
        for copy in chips:
            copy.start()
        bias = column_sum(proj_ref[...].astype(f32))
        stats = [one_stats[k : k + 1] for k in range(3)] + [two_stats[k : k + 1] for k in (1, 2)]
        rows_all = [sum(row[:, i * 128 : (i + 1) * 128] for i in range(N_DP)) for row in stats] + [
            bias[:, i * 128 : (i + 1) * 128] for i in range(wide // 128)
        ]
        for i in range(N_DP):
            cols = slice(i * 128, (i + 1) * 128)
            own[i, 0:16] = router_ref[:, cols]
            own[i, 16:17] = vec_ref[:, cols]
            own[i, 17:18] = two_stats[0:1, cols]
            for k, row in enumerate(rows_all):
                own[i, 19 + k : 20 + k] = row
            own[i, 19 + len(rows_all) : small] = jnp.zeros((small - 19 - len(rows_all), 128), f32)
        resid = x_ref[t].astype(f32)
        inv = second_moment(resid)
        d_normed = scatter.total()
        scaled = d_normed * gain_ref[...]
        mine[...] = (
            d_ref[...]
            + inv * scaled
            - resid * (inv * inv * inv) * jnp.mean(scaled * resid, axis=1, keepdims=True)
        ).astype(bf16)
        gather.start()
        gain_grad = column_sum(d_normed * resid * inv)
        for i in range(N_DP):
            own[i, 18:19] = gain_grad[:, i * 128 : (i + 1) * 128]
        firsts = [
            remote(own.at[me ^ k], few.at[k], send.at[k], recv.at[k], {"dp": me ^ k})
            for k in range(1, N_DP)
        ]
        for copy in firsts:
            copy.start()
        for copy in rest.copies[2:]:
            copy.start()
        value = own[me]
        for k in range(1, N_DP):
            firsts[k - 1].wait_recv()
            value = value + few[k]
        one_ref[...] = value
        summed[...] = value
        seconds = [
            remote(summed, more.at[k], tsend.at[k], trecv.at[k], {"tensor": t ^ k}) for k in range(1, N_T)
        ]
        for copy in seconds:
            copy.start()
        gather.relay()
        for load in loads:
            load.wait()
        for copy in rest.copies:
            copy.wait_recv()

        def add(j, carry):
            cols = pl.ds(pl.multiple_of(j * 256, 256), 256)
            total = acc[:, cols]
            for i in range(len(received)):
                total = total + others[i, :, cols].astype(f32)
            acc[:, cols] = total
            return carry

        lax.fori_loop(0, width // 256, add, 0)
        stores = [
            pltpu.make_async_copy(acc.at[pl.ds(0, 2 * units)], in_ref, osem.at[0]),
            pltpu.make_async_copy(acc.at[pl.ds(2 * units, units)], out_ref, osem.at[1]),
        ]
        for store in stores:
            store.start()
        near.wait()
        along_x.wait_recv()
        total = x_near[...].astype(f32) + x_far[...].astype(f32)
        shared_in_ref[...] = total[0 : 2 * n_hidden]
        shared_out_ref[...] = total[2 * n_hidden :]
        total = qsum[chip].astype(f32)
        for k in range(1, 8):
            chips[k - 1].wait_recv()
            total = total + qin[k].astype(f32)
        qkv_ref[...] = total
        for k in range(1, N_T):
            seconds[k - 1].wait_recv()
            value = value + more[k]
        both_ref[...] = value
        for copy in firsts + seconds + across + chips + rest.copies + [along_x]:
            copy.wait_send()
        scatter.wait_send()
        gather.wait()
        for store in stores:
            store.wait()

    return pl.pallas_call(
        kernel,
        out_shape=(
            struct(part.shape, bf16),
            struct((width // N_DP, wide), f32),
            struct((small, 128), f32),
            struct((small, 128), f32),
            struct((2 * n_hidden, 128), f32),
            struct((n_hidden, 128), f32),
            struct((2 * units, width), f32),
            struct((units, width), f32),
        ),
        in_specs=[VMEM] * 10 + [HBM] * (n_in - 10),
        out_specs=(HBM,) + (VMEM,) * 5 + (HBM,) * 2,
        scratch_shapes=[
            pltpu.VMEM(part.shape, bf16),
            pltpu.VMEM((rows, width), bf16),
        ]
        + sems(N_T, N_T, (2, 4), (2, 4), 1)
        + [
            pltpu.VMEM((N_DP, small, 128), f32),
            pltpu.VMEM((N_DP, small, 128), f32),
            pltpu.VMEM((small, 128), f32),
            pltpu.VMEM((N_T, small, 128), f32),
        ]
        + sems(N_DP, N_DP, N_T, N_T)
        + [
            pltpu.VMEM((8, 2, 128, wide), bf16),
            pltpu.VMEM((8, 128, wide), bf16),
            pltpu.VMEM((8, 128, wide), bf16),
            pltpu.VMEM((8, 128, wide), bf16),
        ]
        + sems(8, 8, 8, 8)
        + [
            pltpu.VMEM((n_expert, width), f32),
            pltpu.VMEM((len(received), n_expert, width), bf16),
        ]
        + sems(1 + len(received), 2, 4, 4)
        + [pltpu.VMEM(by_x.shape[1:], bf16)] * 2
        + sems(2, 1),
        compiler_params=comm_params(number, LIMIT),
        name="join_tail",
        cost_estimate=cost(55),
    )(part, layer_input, d_middle, gain, normed, d_proj, *smalls, own_grads, *received, *waiting, by_x)


def doc_layout(lengths, token_index):
    doc_ends = jnp.cumsum(lengths)
    starts = doc_ends - lengths
    seq_ids = jnp.sum((token_index[:, None] >= doc_ends[None, :]).astype(jnp.int32), axis=1)
    member = seq_ids[:, None] == jnp.arange(lengths.shape[0], dtype=jnp.int32)[None, :]
    begins = jnp.sum(jnp.where(member, starts[None, :], 0), axis=1)
    offsets = token_index - begins
    return (seq_ids, offsets, offsets // DBLOCK)


def rope_tables(offsets, head_dim):
    half_dim = head_dim // 2
    frequencies = jnp.exp(
        jnp.arange(half_dim, dtype=f32) * (-2.0 * math.log(THETA) / head_dim)
    )
    angles = offsets.astype(f32)[:, None] * frequencies[None, :]
    return (jnp.cos(angles)[:, None, :], jnp.sin(angles)[:, None, :])


def rotate(vectors, cosine, sine):
    half_dim = vectors.shape[-1] // 2
    front, back = vectors[..., :half_dim], vectors[..., half_dim:]
    return jnp.concatenate([front * cosine - back * sine, back * cosine + front * sine], axis=-1)


def dot(pattern, a, b):
    return jnp.einsum(pattern, a, b, preferred_element_type=f32)


def on_device(
    layer_input,
    doc_lengths,
    expert_ids,
    attn_gain,
    qkv_weight,
    qkv_bias,
    out_weight,
    ffn_gain,
    router_weight,
    shared_gate,
    shared_in,
    shared_out,
    expert_in,
    expert_out,
    cotangent,
):
    tok, width = layer_input.shape
    dp, tn = lax.axis_index("dp"), lax.axis_index("tensor")
    experts_n = router_weight.shape[1]
    head_dim = qkv_weight.shape[3]
    stream = tok * N_DP
    part_rows = tok // N_T
    score_scale = head_dim ** (-0.5)
    eff = expert_out.shape[1]

    in_rows = expert_in[0].transpose(1, 2, 0).reshape(2 * eff, width)

    hot = jnp.sum(
        (expert_ids[:, :, None] == jnp.arange(experts_n, dtype=jnp.int32)[None, None, :]).astype(f32),
        axis=1,
    )
    before = (jnp.arange(tok)[:, None] > jnp.arange(tok)[None, :]).astype(bf16)
    rank = dot("ts,se->te", before, hot.astype(bf16))
    place = jnp.where(hot > 0, rank, -1.0).astype(jnp.int32).T
    _, offset = route_plane()
    served = lax.dynamic_slice_in_dim(place, GROUPS * ((dp // 4) ^ offset), GROUPS, 0)
    places = (served[:, None, :] == jnp.arange(SLOTS, dtype=jnp.int32)[None, :, None]).astype(bf16)
    returned = lax.dynamic_index_in_dim(place.reshape(GROUPS, 4, tok), offset, 1, keepdims=False)
    places_back = (
        (returned[:, None, :] == jnp.arange(SLOTS, dtype=jnp.int32)[None, :, None])
        .astype(bf16)
        .reshape(GROUPS * SLOTS, tok)
    )

    local_index = dp * tok + jnp.arange(tok, dtype=jnp.int32)
    _, pos_local, _ = doc_layout(doc_lengths, local_index)
    cosine, sine = rope_tables(pos_local, head_dim)
    residual = layer_input.astype(f32)
    inv_first = lax.rsqrt(jnp.mean(residual * residual, axis=1, keepdims=True) + EPSILON)
    normed_one = (residual * inv_first * attn_gain).astype(bf16)
    projected = dot("td,dshe->tshe", normed_one, qkv_weight) + qkv_bias.astype(f32)[None]
    q_own = rotate(projected[:, 0], cosine, sine).astype(bf16).transpose(1, 0, 2)
    k_own = rotate(projected[:, 1], cosine, sine).astype(bf16).transpose(1, 0, 2)
    v_own = projected[:, 2].astype(bf16).transpose(1, 0, 2)
    by_slice = (N_T, part_rows, width)
    out_flat = out_weight.reshape(2 * head_dim, width)
    keys, values, queries, wide, logs, heads_out, normed_two, middle, stats_one, *neighbours = attend_forward(
        k_own,
        v_own,
        q_own,
        doc_lengths,
        out_flat,
        layer_input.reshape(by_slice),
        ffn_gain.reshape(1, width),
        [in_rows, expert_out[0]],
        1,
    )
    normed_two = normed_two.reshape(tok, width)

    own_expert = jnp.broadcast_to(
        (jnp.arange(experts_n, dtype=jnp.int32) == dp).astype(f32)[:, None], (experts_n, 128)
    )
    back_grads, back_out, mixed, shared_d_normed, got, gate_vec_part, router_part, own_grads, *sent = experts(
        places,
        *neighbours,
        in_rows,
        expert_out[0],
        normed_two,
        cotangent,
        shared_in.transpose(1, 2, 0).reshape(-1, width),
        shared_out,
        shared_gate.astype(f32).reshape(1, width),
        router_weight.T,
        own_expert,
        5,
    )

    by_z = got.reshape((4, 2) + got.shape[1:])

    def combine(rows):
        return dot("rt,rd->td", places_back, rows.reshape(-1, width))

    d_normed_part = (shared_d_normed + combine(back_grads)).astype(bf16)
    moe_part = (mixed + combine(back_out)).astype(bf16)
    d_middle, stats_two, d_keys, d_queries, outproj_grad, by_x, output, *moved = backward(
        d_normed_part.reshape(by_slice),
        moe_part.reshape(by_slice),
        cotangent.reshape(by_slice),
        middle,
        ffn_gain.reshape(1, width),
        out_flat,
        heads_out,
        queries,
        keys,
        values,
        wide,
        logs,
        doc_lengths,
        by_z,
        sent,
        7,
    )

    cosine, sine = cosine[:, 0], sine[:, 0]
    d_proj = jnp.concatenate(
        [rotate(d_queries[h].astype(f32), cosine, -sine) for h in range(2)]
        + [rotate(d_keys[h, :tok], cosine, -sine) for h in range(2)]
        + [d_keys[h, tok:] for h in range(2)],
        axis=1,
    ).astype(bf16)
    d_normed_one = dot(
        "tshe,dshe->td", d_proj.reshape(tok, 3, 2, head_dim), qkv_weight
    ).astype(bf16)
    input_grad, qkv_grad, over_dp, over_both, shared_in_grad, shared_out_grad, expert_in_grad, expert_out_grad = join_tail(
        d_normed_one.reshape(by_slice),
        layer_input.reshape(by_slice),
        d_middle,
        attn_gain.reshape(1, width),
        normed_one,
        d_proj,
        [router_part, gate_vec_part, stats_one, stats_two],
        own_grads,
        moved[:2],
        moved[2:],
        by_x,
        10,
    )
    bias_grad = lax.dynamic_slice_in_dim(over_dp[24:30], 8 * dp, 8, 1).reshape(3, 2, 8)
    rms_stats = jnp.sqrt(jnp.sum(over_both[19:24], axis=1) / (stream * width))

    return (
        output.reshape(tok, width),
        input_grad.reshape(tok, width).astype(f32),
        qkv_grad.reshape(width // N_DP, 3, 2, head_dim),
        bias_grad,
        outproj_grad.T.reshape(2, head_dim, width // N_DP),
        over_both[18],
        over_both[17],
        over_both[:16].T,
        over_both[16],
        shared_in_grad.reshape(2, shared_in.shape[2], -1).transpose(2, 0, 1),
        shared_out_grad,
        expert_in_grad.reshape(2, eff, width).transpose(2, 0, 1)[None],
        expert_out_grad[None],
        rms_stats,
    )


def solution(mesh):
    in_specs = (
        P("dp", None),
        P(),
        P("dp", None),
        P(),
        P(None, None, "tensor", None),
        P(None, "tensor", None),
        P("tensor", None, None),
        P(),
        P(),
        P(),
        P(None, None, "tensor"),
        P("tensor", None),
        P("dp", None, None, "tensor"),
        P("dp", "tensor", None),
        P("dp", None),
    )
    out_specs = (
        P("dp", None),
        P("dp", None),
        P("dp", None, "tensor", None),
        P(None, "tensor", "dp"),
        P("tensor", None, "dp"),
        P("dp"),
        P("dp"),
        P("dp", None),
        P("dp"),
        P("dp", None, "tensor"),
        P("tensor", "dp"),
        P("dp", None, None, "tensor"),
        P("dp", "tensor", None),
        P(),
    )
    return jax.shard_map(
        on_device, mesh=mesh, in_specs=in_specs, out_specs=out_specs, check_vma=False
    )
```

```python
import math

import jax
import jax.numpy as jnp
from jax import lax
from jax.experimental import pallas as pl
from jax.experimental.pallas import tpu as pltpu
from jax.sharding import PartitionSpec as P

DBLOCK = 256
EPSILON = 1e-06
THETA = 1000000.0
NEG_FILL = -1e30
MESH = pl.DeviceIdType.MESH
f32 = jnp.float32
bf16 = jnp.bfloat16
N_DP = 16
N_T = 8
SLOTS = 112
LIMIT = 48 * 1024 * 1024
CODE = 1 << 16

HBM = pl.BlockSpec(memory_space=pl.ANY)
VMEM = pl.BlockSpec(memory_space=pltpu.VMEM)
SMEM = pl.BlockSpec(memory_space=pltpu.SMEM)


def greet(peers, *more):
    barrier = pltpu.get_barrier_semaphore()
    for peer in peers:
        pl.semaphore_signal(barrier, inc=1, device_id=peer, device_id_type=MESH)
    count = len(peers)
    for rows in more:
        count = count + rows.greet()
    pl.semaphore_wait(barrier, count)


def remote(src, dst, send, recv, device):
    return pltpu.make_async_remote_copy(
        src_ref=src,
        dst_ref=dst,
        send_sem=send,
        recv_sem=recv,
        device_id=device,
        device_id_type=MESH,
    )


def dma(*shape):
    return pltpu.SemaphoreType.DMA(shape)


def cost(micros):
    return pl.CostEstimate(flops=0, bytes_accessed=int(micros * 3e6), transcendentals=0)


def comm_params(number, limit=None):
    return pltpu.CompilerParams(
        collective_id=number, has_side_effects=True, vmem_limit_bytes=limit
    )


NT = (((1,), (1,)), ((), ()))
TN = (((0,), (0,)), ((), ()))


def mm(a, b, dims=(((1,), (0,)), ((), ()))):
    return lax.dot_general(a, b, dims, preferred_element_type=f32)


GROUPS = 4
HALF = 256
SOON = 96
ORDER = (4, 12, 2, 5, 13, 3, 8, 6, 14, 9, 7, 15, 10, 11, 1)
STEPS = (1, 3, 2, 4, 5, 7, 6)
CHUNKS = ((0, 48), (48, 64))


def sems(*counts):
    return [dma(*c) if isinstance(c, tuple) else dma(c) for c in counts]


def dp_peers():
    me = lax.axis_index("dp")
    return [{"dp": me ^ k} for k in range(1, N_DP)]


def tensor_peers():
    me = lax.axis_index("tensor")
    return [{"tensor": me ^ k} for k in range(1, N_T)]


def coordinates():
    d, t = lax.axis_index("dp"), lax.axis_index("tensor")
    return d, d // 4, t // 4, t % 4


def route_plane():
    d, z, _, y = coordinates()
    plane = 2 * ((z + d // 2) % 2) + d % 2
    return plane, y ^ plane


class Rows:
    def __init__(self, x_ref, out_ref, send, recv, local, back=False):
        self.x, self.out, self.send, self.recv, self.local, self.back = x_ref, out_ref, send, recv, local, back
        d, z, half, y = coordinates()
        plane, offset = route_plane()
        if back:
            experts = [{"dp": 4 * k + offset, "tensor": 4 * half + plane} for k in range(GROUPS)]
            target = y ^ (d % 4)
        else:
            experts = [{"dp": 4 * (z ^ offset) + j, "tensor": 4 * half + plane} for j in range(GROUPS)]
        groups = [
            {
                "dp": 4 * g + 2 * ((y // 2 + g) % 2) + y % 2,
                "tensor": 4 * half + (target if back else y ^ g ^ z),
            }
            for g in range(GROUPS)
        ]
        self.peers, self.sources = (groups, experts) if back else (experts, groups)
        self.slot = z
        self.mine = z if back else d % 4
        self.own = offset == 0
        if back:
            self.own = jnp.logical_and(self.own, d % 4 == 0)
        self.d = d

    def is_own(self, j):
        return jnp.logical_and(self.own, self.mine == j)

    def greet(self):
        barrier = pltpu.get_barrier_semaphore()
        for j in range(GROUPS):
            source = self.sources[j]

            @pl.when(jnp.logical_not(jnp.logical_and(self.own, self.slot == j)))
            def _():
                pl.semaphore_signal(barrier, inc=1, device_id=source, device_id_type=MESH)

        return GROUPS - self.own.astype(jnp.int32)

    def copy(self, j, c):
        rows = pl.ds(*CHUNKS[c])
        return remote(
            self.x.at[j, rows],
            self.out.at[self.slot, rows],
            self.send.at[c, j],
            self.recv.at[c, self.slot],
            self.peers[j],
        )

    def arrival(self, j, c):
        rows = pl.ds(*CHUNKS[c])
        return remote(
            self.x.at[j, rows],
            self.out.at[j, rows],
            self.send.at[c, j],
            self.recv.at[c, j],
            self.peers[j],
        )

    def inside(self):
        return pltpu.make_async_copy(self.x.at[self.mine], self.out.at[self.slot], self.local.at[0])

    def start_one(self, j):
        @pl.when(jnp.logical_not(self.is_own(j)))
        def _():
            for c in range(len(CHUNKS)):
                self.copy(j, c).start()

        @pl.when(self.is_own(j))
        def _():
            self.inside().start()

    def start(self):
        for j in range(GROUPS):
            self.start_one(j)

    def wait(self):
        @pl.when(self.own)
        def _():
            self.inside().wait()

        for c in range(len(CHUNKS)):
            for j in range(GROUPS):

                @pl.when(jnp.logical_not(self.is_own(j)))
                def _():
                    self.copy(j, c).wait_send()

                @pl.when(jnp.logical_not(jnp.logical_and(self.own, self.slot == j)))
                def _():
                    self.arrival(j, c).wait_recv()


ROW_SEMS = sems((len(CHUNKS), GROUPS), (len(CHUNKS), GROUPS), 1)


class Exchange:
    def __init__(self, x_ref, out_ref, send, recv, local):
        me = lax.axis_index("dp")
        self.copies = [
            remote(x_ref.at[me ^ k], out_ref.at[me], send.at[k], recv.at[k], {"dp": me ^ k})
            for k in ORDER
        ]
        self.copies.append(pltpu.make_async_copy(x_ref.at[me], out_ref.at[me], local.at[0]))

    def start(self):
        for copy in self.copies:
            copy.start()

    def wait(self):
        for copy in self.copies:
            copy.wait()


DP_SEMS = sems(N_DP, N_DP, 1)


class Swap:
    def __init__(self, x_ref, out_ref, send, recv, local):
        me = lax.axis_index("dp")
        core = lax.rem(me, 2)
        self.copies = [
            remote(x_ref.at[1 - core], out_ref.at[core], send.at[0], recv.at[0], {"dp": me ^ 1}),
            pltpu.make_async_copy(x_ref.at[core], out_ref.at[core], local.at[0]),
        ]

    start = Exchange.start
    wait = Exchange.wait


SWAP_SEMS = sems(1, 1, 1)


class DirectScatter:
    def __init__(self, part_ref, got, send, recv):
        self.me = lax.axis_index("tensor")
        self.part, self.got = part_ref, got
        self.copies = [
            remote(
                part_ref.at[self.me ^ k], got.at[k], send.at[k], recv.at[k], {"tensor": self.me ^ k}
            )
            for k in STEPS
        ]

    def start(self):
        for copy in self.copies:
            copy.start()

    def total(self):
        value = self.part[self.me].astype(f32)
        for k, copy in zip(STEPS, self.copies):
            copy.wait_recv()
            value = value + self.got[k].astype(f32)
        return value

    def wait_send(self):
        for copy in self.copies:
            copy.wait_send()


class DirectGather:
    def __init__(self, mine, full_ref, send, recv, local):
        me = lax.axis_index("tensor")
        self.mine = mine
        self.copies = [
            remote(mine, full_ref.at[me], send.at[k], recv.at[k], {"tensor": me ^ k}) for k in STEPS
        ]
        self.copies.append(pltpu.make_async_copy(mine, full_ref.at[me], local.at[0]))

    def start(self, value):
        self.mine[...] = value.astype(bf16)
        for copy in self.copies:
            copy.start()

    def wait(self):
        for copy in self.copies:
            copy.wait()


def direct_scratch(rows, width):
    return [
        pltpu.VMEM((N_T, rows, width), bf16),
        pltpu.VMEM((rows, width), bf16),
    ] + sems(N_T, N_T, N_T, N_T, 1)


N_DIRECT = 7


def direct_parts(part_ref, full_ref, scratch):
    got, mine, send, recv, asend, arecv, local = scratch
    return DirectScatter(part_ref, got, send, recv), DirectGather(mine, full_ref, asend, arecv, local)


class Scatter:
    def __init__(self, part_ref, got, mid, last, send, recv):
        t = lax.axis_index("tensor")
        y, half = t % 4, t // 4
        self.part, self.got, self.mid, self.last = part_ref, got, mid, last
        self.slots = (4 * (1 - half) + y, t)
        self.copies = [
            [
                remote(
                    part_ref.at[slot ^ k],
                    got.at[a, k],
                    send.at[a, k],
                    recv.at[a, k],
                    {"tensor": t ^ k},
                )
                for k in (1, 3, 2)
            ]
            for a, slot in enumerate(self.slots)
        ]
        self.across = remote(mid, last, send.at[0, 0], recv.at[0, 0], {"tensor": t ^ 4})

    def start(self):
        for copies in self.copies:
            for copy in copies:
                copy.start()

    def over_y(self, a):
        value = self.part[self.slots[a]].astype(f32)
        for k, copy in zip((1, 3, 2), self.copies[a]):
            copy.wait_recv()
            value = value + self.got[a, k].astype(f32)
        return value

    def middle(self):
        self.mid[...] = self.over_y(0).astype(bf16)
        self.across.start()

    def total(self):
        value = self.over_y(1)
        self.across.wait_recv()
        return value + self.last[...].astype(f32)

    def wait_send(self):
        for copies in self.copies:
            for copy in copies:
                copy.wait_send()
        self.across.wait_send()


class Gather:
    def __init__(self, mine, full_ref, send, recv, local):
        t = lax.axis_index("tensor")
        self.mine = mine
        self.across = remote(
            mine, full_ref.at[t], send.at[0, 0], recv.at[0, 0], {"tensor": t ^ 4}
        )
        self.first = [
            remote(mine, full_ref.at[t], send.at[0, k], recv.at[0, k], {"tensor": t ^ k})
            for k in (1, 3, 2)
        ]
        self.second = [
            remote(
                full_ref.at[t ^ 4],
                full_ref.at[t ^ 4],
                send.at[1, k],
                recv.at[1, k],
                {"tensor": t ^ k},
            )
            for k in (1, 3, 2)
        ]
        self.own = pltpu.make_async_copy(mine, full_ref.at[t], local.at[0])

    def start(self, value):
        self.mine[...] = value.astype(bf16)
        for copy in [self.across] + self.first + [self.own]:
            copy.start()

    def relay(self):
        self.across.wait_recv()
        for copy in self.second:
            copy.start()

    def wait(self):
        self.across.wait_send()
        for copy in self.first + self.second + [self.own]:
            copy.wait()


class YGather:
    def __init__(self, mine, full_ref, send, recv, local):
        t = lax.axis_index("tensor")
        self.first = [
            remote(mine, full_ref.at[t], send.at[0, k], recv.at[0, k], {"tensor": t ^ k})
            for k in (1, 3, 2)
        ]
        self.second = [
            remote(full_ref.at[t ^ k], full_ref.at[t ^ k], send.at[1, k], recv.at[1, k], {"tensor": t ^ 4})
            for k in (1, 3, 2)
        ]
        self.across = remote(mine, full_ref.at[t], send.at[1, 0], recv.at[1, 0], {"tensor": t ^ 4})
        self.own = pltpu.make_async_copy(mine, full_ref.at[t], local.at[0])

    def start(self):
        for copy in self.first + [self.across, self.own]:
            copy.start()

    def relay(self):
        for first, second in zip(self.first, self.second):
            first.wait_recv()
            second.start()

    def wait(self):
        for copy in self.first:
            copy.wait_send()
        for copy in self.second + [self.across, self.own]:
            copy.wait()


class Sends:
    def __init__(self, messages, send, recv):
        self.copies = [
            remote(src, dst, send.at[i], recv.at[i], peer) for i, (src, dst, peer) in enumerate(messages)
        ]

    start = Exchange.start
    wait = Exchange.wait


def struct(shape, dtype):
    return jax.ShapeDtypeStruct(shape, dtype)


def column_sum(value):
    return jnp.sum(value, axis=0, keepdims=True)


def second_moment(value):
    return lax.rsqrt(jnp.mean(value * value, axis=1, keepdims=True) + EPSILON)


def codes_of(index, lengths_ref):
    end, seq, begin = 0, 0, 0
    for j in range(lengths_ref.shape[0]):
        end = end + lengths_ref[j]
        past = index >= end
        seq = seq + past.astype(jnp.int32)
        begin = jnp.where(past, end, begin)
    return seq * CODE, seq * CODE + lax.shift_right_arithmetic(index - begin, DBLOCK.bit_length() - 1)


def codes_of_keys(group, count, lengths_ref):
    index = group * count + lax.broadcasted_iota(jnp.int32, (count, 1), 0)
    return codes_of(index, lengths_ref)[1]


def codes_of_queries(chip, count, lengths_ref):
    index = chip * count + lax.broadcasted_iota(jnp.int32, (1, count), 1)
    return codes_of(index, lengths_ref)


def attend(q, state, k, v, code, bounds, factor):
    peak, total, acc = state
    scores = mm(k, q, NT) * factor
    seen = (code >= bounds[0]) & (code <= bounds[1])
    scores = jnp.where(seen, scores, NEG_FILL)
    new_peak = jnp.maximum(peak, jnp.max(scores, axis=0, keepdims=True))
    terms = jnp.exp2(scores - new_peak)
    shrink = jnp.exp2(peak - new_peak)
    total = total * shrink + jnp.sum(terms, axis=0, keepdims=True)
    acc = acc * shrink + mm(v, terms.astype(bf16), TN)
    return new_peak, total, acc


def along_y(shift):
    t = lax.axis_index("tensor")
    return {"tensor": 4 * (t // 4) + (t + shift) % 4}


def weights_along_y(weight_refs, n_rows, results, send, recv):
    messages = []
    for result, shift in zip(results, (1, 3)):
        at = 0
        for ref, count in zip(weight_refs, n_rows):
            messages.append((ref, result.at[pl.ds(at, count)], along_y(shift)))
            at += count
    return Sends(messages, send, recv)


def attend_forward(k, v, q, lengths, out_weight, layer_input, gain, weights, number):
    _, tok, size = q.shape
    n_rows = [w.shape[0] for w in weights]
    stream, count = N_DP * tok, 2 * tok
    _, rows, width = layer_input.shape
    factor = size ** (-0.5) * math.log2(math.e)

    def kernel(k_ref, v_ref, q_ref, lengths_ref, w_ref, x_ref, gain_ref, *refs):
        weight_refs, outs, scratch = refs[:2], refs[2:14], refs[14:]
        keys_ref, values_ref, pair_ref, wide_ref, log_ref, heads_ref, full_ref, middle_ref, stats_ref = outs[:9]
        keys, values, pair, own_out, heads, part = scratch[:6]
        send, recv, local = scratch[6:9]
        swap_sems, out_sems, store_sems, weight_sems = scratch[9:12], scratch[12:14], scratch[14], scratch[15:17]
        relay_sems, join = scratch[17:19], scratch[19:]
        me = lax.axis_index("dp")
        core = lax.rem(me, 2)
        greet(tensor_peers() + dp_peers())
        both = weights_along_y(weight_refs, n_rows, outs[9:11], *weight_sems)
        both.start()
        swap = Swap(q_ref, pair, *swap_sems)
        swap.start()

        def place(group):
            return pl.ds(pl.multiple_of(group * tok, tok), tok)

        def copies(step, head):
            return [
                remote(
                    own.at[head],
                    full.at[place(me)],
                    send.at[i, step],
                    recv.at[i, step],
                    {"dp": me ^ step},
                )
                for i, (own, full) in enumerate(((k_ref, keys), (v_ref, values)))
            ]

        for step in ORDER:
            for copy in copies(step, core if step % 2 == 0 else 1 - core):
                copy.start()
        locals_ = [
            pltpu.make_async_copy(own.at[core], full.at[place(me)], local.at[i])
            for i, (own, full) in enumerate(((k_ref, keys), (v_ref, values)))
        ]
        for copy in locals_:
            copy.start()
        swap.wait()
        for copy in locals_:
            copy.wait()
        queries = pair[...].reshape(count, size)
        limits = codes_of_queries(me // 2, count, lengths_ref)

        def block(group, state):
            at = place(group)
            code = codes_of_keys(group, tok, lengths_ref)
            return attend(queries, state, keys[at], values[at], code, limits, factor)

        def arrived(step, state):
            group = me ^ step
            for i, (own, full) in enumerate(((k_ref, keys), (v_ref, values))):
                remote(
                    own.at[core], full.at[place(group)], send.at[i, step], recv.at[i, step], {"dp": group}
                ).wait_recv()
            return block(group, state)

        state = block(
            me,
            (
                jnp.full((1, count), NEG_FILL, f32),
                jnp.zeros((1, count), f32),
                jnp.zeros((size, count), f32),
            ),
        )
        peak, total, acc = lax.fori_loop(1, N_DP, arrived, state)
        out = (acc / total).T
        wide_ref[...] = out
        log_ref[...] = jnp.broadcast_to(peak + jnp.log2(total), (8, count))
        own_out[...] = out.astype(bf16).reshape(2, tok, size)
        across = remote(
            own_out.at[1 - core], heads.at[core], out_sems[0].at[0], out_sems[1].at[0], {"dp": me ^ 1}
        )
        across.start()
        heads[core] = own_out[core]
        stores = [
            pltpu.make_async_copy(keys, keys_ref, store_sems.at[0]),
            pltpu.make_async_copy(values, values_ref, store_sems.at[1]),
            pltpu.make_async_copy(pair, pair_ref, store_sems.at[2]),
        ]
        for store in stores:
            store.start()
        across.wait_recv()
        heads_ref[:, 0:size] = heads[0]
        heads_ref[:, size : 2 * size] = heads[1]

        def project(j, carry):
            cols = pl.ds(pl.multiple_of(j * 512, 512), 512)
            value = mm(heads_ref[...], w_ref[:, cols])
            part[:, :, cols] = value.reshape(N_T, rows, 512).astype(bf16)
            return carry

        lax.fori_loop(0, width // 512, project, 0)
        scatter = DirectScatter(part, join[0], *join[2:4])
        mine = join[1]
        gather = YGather(mine, full_ref, *join[4:])
        scatter.start()
        for copy in both.copies:
            copy.wait_recv()
        below_ref, above_ref, far_ref = outs[9:]
        relay = Sends(
            [
                (ref.at[pl.ds(at, n)], far_ref.at[pl.ds(at, n)], along_y(shift))
                for ref, shift, at, n in (
                    (below_ref, 1, 0, SOON),
                    (above_ref, 3, HALF, SOON),
                    (below_ref, 1, SOON, HALF - SOON),
                    (above_ref, 3, HALF + SOON, sum(n_rows) - HALF - SOON),
                )
            ],
            *relay_sems,
        )
        for copy in relay.copies[:2]:
            copy.start()
        resid = x_ref[lax.axis_index("tensor")].astype(f32)
        attn_out = scatter.total()
        middle = resid + attn_out
        mine[...] = (middle * second_moment(middle) * gain_ref[...]).astype(bf16)
        gather.start()
        for copy in relay.copies[2:]:
            copy.start()
        middle_ref[...] = middle
        stats_ref[0:1] = column_sum(resid * resid)
        stats_ref[1:2] = column_sum(attn_out * attn_out)
        stats_ref[2:3] = column_sum(middle * middle)
        gather.relay()
        for step in ORDER:
            for copy in copies(step, core):
                copy.wait_send()
        across.wait_send()
        scatter.wait_send()
        for store in stores:
            store.wait()
        gather.wait()
        for copy in both.copies:
            copy.wait_send()
        relay.wait()

    return pl.pallas_call(
        kernel,
        out_shape=(
            struct((stream, size), bf16),
            struct((stream, size), bf16),
            struct(q.shape, bf16),
            struct((count, size), f32),
            struct((8, count), f32),
            struct((tok, 2 * size), bf16),
            struct(layer_input.shape, bf16),
            struct((rows, width), f32),
            struct((8, width), f32),
        )
        + (struct((sum(n_rows), width), bf16),) * 3,
        in_specs=[HBM] * 3 + [SMEM] + [VMEM] * 3 + [HBM] * 2,
        out_specs=(HBM,) * 3 + (VMEM,) * 3 + (HBM,) + (VMEM,) * 2 + (HBM,) * 3,
        scratch_shapes=[
            pltpu.VMEM((stream, size), bf16),
            pltpu.VMEM((stream, size), bf16),
            pltpu.VMEM(q.shape, bf16),
            pltpu.VMEM(q.shape, bf16),
            pltpu.VMEM(q.shape, bf16),
            pltpu.VMEM(layer_input.shape, bf16),
        ]
        + sems((2, N_DP), (2, N_DP), 2)
        + SWAP_SEMS
        + sems(1, 1, 3, 4, 4, 4, 4)
        + [
            pltpu.VMEM(layer_input.shape, bf16),
            pltpu.VMEM((rows, width), bf16),
        ]
        + sems(N_T, N_T, (2, 4), (2, 4), 1),
        compiler_params=comm_params(number, LIMIT),
        name="attend_forward",
        cost_estimate=cost(85),
    )(k, v, q, lengths, out_weight, layer_input, gain, *weights)


def sigmoid(x):
    return 1.0 / (1.0 + jnp.exp(-x))


TILE = 176
NOW = 96


def shared_expert(x_ref, up_ref, w_ref, vec_ref, part_ref, d_ref, grads_ref, row_ref, low_ref):
    hidden = w_ref.shape[0] // 3
    vec = vec_ref[...]
    gate = sigmoid(jnp.sum(x_ref[...].astype(f32) * vec, axis=1, keepdims=True))
    low_ref[...] = (gate * up_ref[...].astype(f32)).astype(bf16)
    part_ref[...] = jnp.zeros_like(part_ref)
    d_ref[...] = jnp.zeros_like(d_ref)

    def tile(i, carry):
        rows = [pl.ds(pl.multiple_of(i * TILE + k * hidden, 16), TILE) for k in range(3)]
        x, d_out = x_ref[...], low_ref[...]
        gate_part = mm(w_ref[rows[0]], x, NT)
        up_part = mm(w_ref[rows[1]], x, NT)
        sig = sigmoid(gate_part)
        act = gate_part * sig
        unit = (act * up_part).astype(bf16)
        d_unit = mm(w_ref[rows[2]], d_out, NT)
        d_gate = (d_unit * up_part * sig * (1.0 + gate_part * (1.0 - sig))).astype(bf16)
        d_up = (d_unit * act).astype(bf16)

        def block(j, carry):
            cols = pl.ds(pl.multiple_of(j * 256, 256), 256)
            xs, ds = x_ref[:, cols], low_ref[:, cols]
            part_ref[:, cols] += mm(unit, w_ref[rows[2], cols], TN)
            d_ref[:, cols] += mm(d_gate, w_ref[rows[0], cols], TN) + mm(d_up, w_ref[rows[1], cols], TN)
            for k, grad in enumerate((mm(d_gate, xs), mm(d_up, xs), mm(unit, ds))):
                grad = grad.astype(bf16)
                grads_ref[j, 0, rows[k]] = grad[:, :128]
                grads_ref[j, 1, rows[k]] = grad[:, 128:]
            return carry

        return lax.fori_loop(0, x.shape[1] // 256, block, carry)

    lax.fori_loop(0, hidden // TILE, tile, 0)
    total = part_ref[...]
    d_logit = jnp.sum(up_ref[...].astype(f32) * total, axis=1, keepdims=True) * gate * (1.0 - gate)
    part_ref[...] = gate * total
    d_ref[...] += d_logit * vec
    row_ref[...] = column_sum(d_logit * x_ref[...].astype(f32))


class Routed:
    def __init__(self, x_ref, up_ref, w_ref, router_ref, own, acc, dgu_ref, unit_ref, slope_ref, router_grad_ref):
        groups, slots, self.width = x_ref.shape
        self.rows, self.units = groups * slots, w_ref.shape[1] // 3
        self.x_ref, self.up_ref, self.w_ref, self.router_ref, self.own = x_ref, up_ref, w_ref, router_ref, own
        self.acc, self.dgu_ref, self.unit_ref, self.slope_ref = acc, dgu_ref, unit_ref, slope_ref
        self.router_grad_ref = router_grad_ref

    def flat(self, ref):
        return ref[...].reshape(self.rows, self.width)

    def start(self):
        logits = mm(self.router_ref[...], self.flat(self.x_ref), NT)
        terms = jnp.exp(logits - jnp.max(logits, axis=0, keepdims=True))
        self.probs = terms / jnp.sum(terms, axis=0, keepdims=True)
        self.gate = jnp.sum(self.probs * self.own, axis=0, keepdims=True)
        self.acc[...] = jnp.zeros_like(self.acc)

    def blocks(self, body):
        def block(j, carry):
            body(pl.ds(pl.multiple_of(j * 512, 512), 512))
            return carry

        lax.fori_loop(0, self.width // 512, block, 0)

    def forward(self):
        units, rows, w_ref = self.units, self.rows, self.w_ref

        def piece(i, carry):
            gate_part = mm(w_ref[i, 0:units], self.flat(self.x_ref), NT)
            up_part = mm(w_ref[i, units : 2 * units], self.flat(self.x_ref), NT)
            sig = sigmoid(gate_part)
            act = gate_part * sig
            gated = (act * up_part * self.gate).astype(bf16)
            slope = self.gate * up_part * sig * (1.0 + gate_part * (1.0 - sig))
            self.slope_ref[i, 0] = slope.astype(bf16)
            self.slope_ref[i, 1] = (self.gate * act).astype(bf16)
            self.unit_ref[i] = gated

            def add(cols):
                self.acc[0:rows, cols] += mm(gated, w_ref[i, 2 * units : 3 * units, cols], TN)

            self.blocks(add)
            return carry

        lax.fori_loop(0, GROUPS, piece, 0)

    def backward(self):
        units, rows, w_ref = self.units, self.rows, self.w_ref

        def piece(i, gated_d_gate):
            raw = mm(w_ref[i, 2 * units : 3 * units], self.flat(self.up_ref), NT)
            d_gate = (raw * self.slope_ref[i, 0].astype(f32)).astype(bf16)
            d_up = (raw * self.slope_ref[i, 1].astype(f32)).astype(bf16)
            self.dgu_ref[i, 0:units] = d_gate
            self.dgu_ref[i, units : 2 * units] = d_up

            def add(cols):
                self.acc[rows : 2 * rows, cols] += mm(d_gate, w_ref[i, 0:units, cols], TN) + mm(
                    d_up, w_ref[i, units : 2 * units, cols], TN
                )

            self.blocks(add)
            return gated_d_gate + jnp.sum(self.unit_ref[i].astype(f32) * raw, axis=0, keepdims=True)

        gated_d_gate = lax.fori_loop(0, GROUPS, piece, jnp.zeros((1, rows), f32))
        d_logits = (gated_d_gate * (self.own - self.probs)).astype(bf16)
        self.router_grad_ref[...] = mm(d_logits, self.flat(self.x_ref))
        self.acc[rows : 2 * rows] += mm(d_logits, self.router_ref[...], TN)


def experts(places, below, above, far_rows, in_rows, out_rows, tokens, upstream, w_in, w_out, vec, router, own, number):
    slots = places.shape[1]
    tok, width = tokens.shape
    hidden, units = w_out.shape[0], out_rows.shape[0]
    n_rows = GROUPS * slots

    def kernel(*refs):
        (below_ref, above_ref, far_ref, in_ref, out_ref, w_in_ref, w_out_ref), refs = refs[:7], refs[7:]
        (places_ref, x_ref, up_ref, vec_ref, router_ref, own_ref), refs = refs[:6], refs[6:]
        (back_d, back_out, part_ref, d_ref, by_z_ref, row_ref, router_grad_ref, mine_ref, *sent_refs), refs = (
            refs[:11],
            refs[11:],
        )
        (weights, low, grads, xs, us, w, acc, dgu, unit, slope, far, send_d, send_out), refs = refs[:13], refs[13:]
        row_sems, refs = [refs[3 * i : 3 * i + 3] for i in range(4)], refs[12:]
        csend, crecv, loaded, stored = refs
        d = lax.axis_index("dp")
        core = lax.rem(d, 2)
        out_x = Rows(send_d, xs, *row_sems[0])
        out_u = Rows(send_out, us, *row_sems[1])
        in_d = Rows(send_d, back_d, *row_sems[2], back=True)
        in_out = Rows(send_out, back_out, *row_sems[3], back=True)
        greet([{"dp": d ^ 1}], out_x, in_d)
        for j in range(GROUPS):
            send_d[j] = mm(places_ref[j], x_ref[...]).astype(bf16)
            out_x.start_one(j)
        for j in range(GROUPS):
            send_out[j] = mm(places_ref[j], up_ref[...]).astype(bf16)
            out_u.start_one(j)
        loads = [
            pltpu.make_async_copy(src, dst, loaded.at[i])
            for i, (src, dst) in enumerate(
                (
                    (w_in_ref, weights.at[pl.ds(0, 2 * hidden)]),
                    (w_out_ref, weights.at[pl.ds(2 * hidden, hidden)]),
                    (in_ref, w.at[0, pl.ds(0, 2 * units)]),
                    (out_ref, w.at[0, pl.ds(2 * units, units)]),
                    (above_ref, w.at[1]),
                    (far_ref, w.at[2]),
                    (below_ref, w.at[3]),
                )
            )
        ]
        for load in loads:
            load.start()
        for load in loads[:2]:
            load.wait()
        shared_expert(x_ref, up_ref, weights, vec_ref, part_ref, d_ref, grads, row_ref, low)
        cores = Sends(
            [(grads.at[chip, 1 - core], far.at[chip], {"dp": d ^ 1}) for chip in range(8)], csend, crecv
        )
        cores.start()
        for load in loads[2:]:
            load.wait()
        out_x.wait()
        routed = Routed(xs, us, w, router_ref, own_ref[:, 0:1], acc, dgu, unit, slope, router_grad_ref)
        routed.start()

        routed.forward()
        out_u.wait()
        send_out[...] = acc[0:n_rows].astype(bf16).reshape(GROUPS, slots, width)
        in_out.start()
        routed.backward()
        send_d[...] = acc[n_rows : 2 * n_rows].astype(bf16).reshape(GROUPS, slots, width)
        in_d.start()

        def block(j, carry):
            cols = pl.ds(pl.multiple_of(j * 256, 256), 256)
            x, up = xs[:, :, cols].reshape(n_rows, 256), us[:, :, cols].reshape(n_rows, 256)
            acc[0 : 2 * units, cols] = mm(dgu[0], x)
            acc[2 * units : 3 * units, cols] = mm(unit[0], up)
            for i in range(1, GROUPS):
                at = 3 * units * (i - 1)
                weights[at : at + 2 * units, cols] = mm(dgu[i], x).astype(bf16)
                weights[at + 2 * units : at + 3 * units, cols] = mm(unit[i], up).astype(bf16)
            return carry

        lax.fori_loop(0, width // 256, block, 0)
        stores = [pltpu.make_async_copy(acc.at[pl.ds(0, 3 * units)], mine_ref, stored.at[0])] + [
            pltpu.make_async_copy(weights.at[pl.ds(3 * units * i, 3 * units)], ref, stored.at[i + 1])
            for i, ref in enumerate(sent_refs)
        ]
        for store in stores:
            store.start()
        for chip in range(8):
            cores.copies[chip].wait_recv()
            far[chip] = (far[chip].astype(f32) + grads[chip, core].astype(f32)).astype(bf16)
            stores.append(pltpu.make_async_copy(far.at[chip], by_z_ref.at[chip], stored.at[4 + chip]))
            stores[-1].start()
        for copy in cores.copies:
            copy.wait_send()
        in_out.wait()
        in_d.wait()
        for store in stores:
            store.wait()

    row = struct((GROUPS, slots, width), bf16)
    return pl.pallas_call(
        kernel,
        out_shape=(
            row,
            row,
            struct((tok, width), f32),
            struct((tok, width), f32),
            struct((8, 3 * hidden, 128), bf16),
            struct((1, width), f32),
            struct((router.shape[0], width), f32),
            struct((3 * units, width), f32),
        )
        + (struct((3 * units, width), bf16),) * 3,
        in_specs=[HBM] * 7 + [VMEM] * 6,
        out_specs=(HBM, HBM, VMEM, VMEM, HBM, VMEM, VMEM) + (HBM,) * 4,
        scratch_shapes=[
            pltpu.VMEM((3 * hidden, width), bf16),
            pltpu.VMEM((tok, width), bf16),
            pltpu.VMEM((8, 2, 3 * hidden, 128), bf16),
            pltpu.VMEM(row.shape, bf16),
            pltpu.VMEM(row.shape, bf16),
            pltpu.VMEM((GROUPS, 3 * units, width), bf16),
            pltpu.VMEM((2 * n_rows, width), f32),
            pltpu.VMEM((GROUPS, 2 * units, n_rows), bf16),
            pltpu.VMEM((GROUPS, units, n_rows), bf16),
            pltpu.VMEM((GROUPS, 2, units, n_rows), bf16),
            pltpu.VMEM((8, 3 * hidden, 128), bf16),
            pltpu.VMEM(row.shape, bf16),
            pltpu.VMEM(row.shape, bf16),
        ]
        + ROW_SEMS * 4
        + sems(8, 8, 7, 12),
        compiler_params=comm_params(number, 61 * 1024 * 1024),
        name="experts",
        cost_estimate=cost(115),
    )(below, above, far_rows, in_rows, out_rows, w_in, w_out, places, tokens, upstream, vec, router, own)


def backward(
    part, moe_part, cotangent, middle, gain, out_weight, heads, q, keys, values, wide, logs, lengths, weights, sent, number
):
    _, rows, width = part.shape
    tok, size = q.shape[1:]
    stream, count = N_DP * tok, 2 * tok
    scale = size ** (-0.5)
    factor = scale * math.log2(math.e)
    n_sent, n_hidden = sent[0].shape[0], weights.shape[2] // 3
    half, rest = pl.ds(0, HALF), pl.ds(HALF, n_sent - HALF)
    now, later = pl.ds(0, NOW), pl.ds(NOW, n_sent - NOW)

    def kernel(*refs):
        (part_ref, moe_ref, up_in_ref, middle_ref, gain_ref, w_ref, heads_ref, q_ref, k_ref, v_ref), refs = (
            refs[:10],
            refs[10:],
        )
        (wide_ref, log_ref, lengths_ref, by_z_ref, one_up, two_up, one_down), refs = refs[:7], refs[7:]
        (d_middle_ref, stats_ref, sums_ref, pair_ref, out_ref, shared_in_ref, shared_out_ref), refs = refs[:7], refs[7:]
        (full_ref, below_ref, above_ref, up_ref, down_ref), refs = refs[:5], refs[5:]
        (full, d_attn, out_slice, d_heads, d_pair, made, got, d_query, out_part, out_got), refs = refs[:10], refs[10:]
        (z_got, by_x, x_got, up, down, far), refs = refs[:6], refs[6:]
        direct, refs = refs[:N_DIRECT], refs[N_DIRECT:]
        moe_scratch, refs = refs[:5], refs[5:]
        send, recv, osend, orecv, small_send, small_recv, fsend, frecv, wsend, wrecv, loaded = refs[:11]
        zsend, zrecv, gather_sems = refs[11], refs[12], refs[13:]
        me, z, _, _ = coordinates()
        t = lax.axis_index("tensor")
        core, x_index = lax.rem(me, 2), lax.rem(me // 2, 2)
        greet(dp_peers() + tensor_peers())
        scatter, gather = direct_parts(part_ref, full, direct)
        scatter.start()
        scatter_moe = Scatter(moe_ref, *moe_scratch)
        scatter_moe.start()
        over_z = Sends(
            [(by_z_ref.at[z ^ k], z_got.at[k], {"dp": me ^ (4 * k)}) for k in (1, 3, 2)], zsend, zrecv
        )
        over_z.start()
        loads = [
            pltpu.make_async_copy(one_up, up, loaded.at[0]),
            pltpu.make_async_copy(one_down, down, loaded.at[1]),
            pltpu.make_async_copy(by_z_ref.at[z], z_got.at[0], loaded.at[2]),
        ]
        for load in loads:
            load.start()
        middle = middle_ref[...]
        inv = second_moment(middle)
        d_normed = scatter.total()
        scaled = d_normed * gain_ref[...]
        d_middle = (
            up_in_ref[t].astype(f32)
            + inv * scaled
            - middle * (inv * inv * inv) * jnp.mean(scaled * middle, axis=1, keepdims=True)
        )
        gather.start(d_middle)
        first = Sends(
            [
                (two_up.at[half], far.at[half], along_y(1)),
                (two_up.at[rest], far.at[rest], along_y(3)),
            ],
            fsend,
            frecv,
        )
        first.start()
        d_middle_ref[...] = d_middle
        stats_ref[0:1] = column_sum(d_normed * middle * inv)
        scatter_moe.middle()
        gather.wait()
        d_attn[...] = full[...].astype(f32).reshape(tok, width).astype(bf16)
        value = mm(d_attn[...], w_ref[...], NT).astype(bf16)
        d_heads[0] = value[:, 0:size]
        d_heads[1] = value[:, size : 2 * size]
        swap = remote(
            d_heads.at[1 - core], d_pair.at[core], small_send.at[1], small_recv.at[1], {"dp": me ^ 1}
        )
        swap.start()
        d_pair[core] = d_heads[core]
        for d in range(N_DP):
            out_part[d] = mm(d_attn[:, d * 128 : (d + 1) * 128], heads_ref[...], TN).astype(bf16)
        outs = [
            remote(out_part.at[me ^ k], out_got.at[k], osend.at[k], orecv.at[k], {"dp": me ^ k})
            for k in range(1, N_DP)
        ]
        for copy in outs:
            copy.start()
        moe_out = scatter_moe.total()
        output = middle_ref[...] + moe_out
        gather_out = Gather(out_slice, full_ref, *gather_sems)
        gather_out.start(output)
        stats_ref[1:2] = column_sum(moe_out * moe_out)
        stats_ref[2:3] = column_sum(output * output)

        swap.wait_recv()
        q, d_out = q_ref[...].reshape(count, size), d_pair[...].reshape(count, size)
        lowest, highest = codes_of_queries(me // 2, count, lengths_ref)
        log = log_ref[0:1]
        delta = jnp.sum((wide_ref[...] * d_out.astype(f32)).T, axis=0, keepdims=True)

        def send_to(step):
            return remote(
                made.at[me ^ step], got.at[step], send.at[step], recv.at[step], {"dp": me ^ step}
            )

        def block(group, acc):
            at = pl.ds(pl.multiple_of(group * tok, tok), tok)
            k = k_ref[at]
            scores = mm(k, q, NT) * factor
            code = codes_of_keys(group, tok, lengths_ref)
            seen = (code >= lowest) & (code <= highest)
            probs = jnp.where(seen, jnp.exp2(scores - log), 0.0)
            d_probs = mm(v_ref[at], d_out, NT)
            d_scores = (probs * (d_probs - delta)).astype(bf16)
            made[group, 0:tok] = (mm(d_scores, q) * scale).astype(bf16)
            made[group, tok : 2 * tok] = mm(probs.astype(bf16), d_out).astype(bf16)
            return acc + mm(k, d_scores, TN)

        def other(step, acc):
            acc = block(me ^ step, acc)
            send_to(step).start()
            return acc

        acc = lax.fori_loop(1, N_DP, other, jnp.zeros((size, count), f32))
        gather_out.relay()
        acc = block(me, acc)
        d_query[...] = (acc.T * scale).astype(bf16).reshape(2, tok, size)
        back = remote(
            d_query.at[1 - core], pair_ref.at[core], small_send.at[2], small_recv.at[2], {"dp": me ^ 1}
        )
        back.start()
        pair_ref[core] = d_query[core]

        loads[2].wait()
        over_z.wait()
        for side in range(2):
            total = z_got[0, side].astype(f32)
            for k in (1, 2, 3):
                total = total + z_got[k, side].astype(f32)
            by_x[side] = total.astype(bf16)
        along_x = remote(
            by_x.at[1 - x_index], x_got, small_send.at[0], small_recv.at[0], {"dp": me ^ 2}
        )
        along_x.start()

        for load in loads[:2]:
            load.wait()
        for copy in first.copies:
            copy.wait_recv()

        def add(rows, target):
            def step(j, carry):
                cols = pl.ds(pl.multiple_of(j * 512, 512), 512)
                target[rows, cols] = (target[rows, cols].astype(f32) + far[rows, cols].astype(f32)).astype(bf16)
                return carry

            lax.fori_loop(0, width // 512, step, 0)

        add(half, up)
        add(rest, down)
        second = Sends(
            [(up.at[now], below_ref, along_y(1)), (down.at[now], above_ref, along_y(3))], wsend, wrecv
        )
        second.start()
        stores = [
            pltpu.make_async_copy(up.at[later], up_ref, loaded.at[3]),
            pltpu.make_async_copy(down.at[later], down_ref, loaded.at[4]),
        ]
        for store in stores:
            store.start()
        got[0] = made[me]
        for k in range(1, N_DP):
            send_to(k).wait_recv()
        for head in range(2):
            total = jnp.zeros((2 * tok, size), f32)
            for k in range(N_DP // 2):
                total = total + got[2 * k + (core + head) % 2].astype(f32)
            sums_ref[head] = total
        total = out_part[me].astype(f32)
        for k, copy in enumerate(outs):
            copy.wait_recv()
            total = total + out_got[k + 1].astype(f32)
        out_ref[...] = total
        along_x.wait_recv()
        total = by_x[x_index].astype(f32) + x_got[...].astype(f32)
        shared_in_ref[...] = total[0 : 2 * n_hidden]
        shared_out_ref[...] = total[2 * n_hidden :]
        back.wait_recv()
        for copy in [along_x, swap, back] + outs + first.copies:
            copy.wait_send()
        scatter.wait_send()
        scatter_moe.wait_send()
        for store in stores:
            store.wait()
        gather_out.wait()
        second.wait()
        for k in range(1, N_DP):
            send_to(k).wait_send()

    return pl.pallas_call(
        kernel,
        out_shape=(
            struct((rows, width), f32),
            struct((8, width), f32),
            struct((2, 2 * tok, size), f32),
            struct(q.shape, bf16),
            struct((width // N_DP, 2 * size), f32),
            struct((2 * n_hidden, 128), f32),
            struct((n_hidden, 128), f32),
            struct(part.shape, bf16),
            struct((NOW, width), bf16),
            struct((NOW, width), bf16),
            struct((n_sent - NOW, width), bf16),
            struct((n_sent - NOW, width), bf16),
        ),
        in_specs=[VMEM] * 12 + [SMEM] + [HBM] * 4,
        out_specs=(VMEM,) * 7 + (HBM,) * 5,
        scratch_shapes=[
            pltpu.VMEM(part.shape, bf16),
            pltpu.VMEM((tok, width), bf16),
            pltpu.VMEM((rows, width), bf16),
            pltpu.VMEM(q.shape, bf16),
            pltpu.VMEM(q.shape, bf16),
            pltpu.VMEM((N_DP, 2 * tok, size), bf16),
            pltpu.VMEM((N_DP, 2 * tok, size), bf16),
            pltpu.VMEM(q.shape, bf16),
            pltpu.VMEM((N_DP, 128, 2 * size), bf16),
            pltpu.VMEM((N_DP, 128, 2 * size), bf16),
            pltpu.VMEM(weights.shape, bf16),
            pltpu.VMEM(weights.shape[1:], bf16),
            pltpu.VMEM(weights.shape[2:], bf16),
        ]
        + [pltpu.VMEM((n_sent, width), bf16)] * 3
        + direct_scratch(rows, width)
        + [pltpu.VMEM((2, 4, rows, width), bf16)]
        + [pltpu.VMEM((rows, width), bf16)] * 2
        + sems((2, 4), (2, 4))
        + sems(N_DP, N_DP, N_DP, N_DP, 3, 3, 2, 2, 2, 2, 5, 3, 3, (2, 4), (2, 4), 1),
        compiler_params=comm_params(number, LIMIT),
        name="backward",
        cost_estimate=cost(110),
    )(
        part, moe_part, cotangent, middle, gain, out_weight, heads, q, keys, values, wide, logs, lengths, weights, *sent
    )


def join_tail(part, layer_input, d_middle, gain, normed, d_proj, smalls, own_grads, received, waiting, number):
    _, rows, width = part.shape
    small = 32
    wide = d_proj.shape[1]
    n_in, n_out = 13 + len(received), 6
    n_expert = own_grads.shape[0]
    n_late = n_expert - NOW - SOON
    first = pl.ds(0, NOW)
    parts = ((0, SOON), (SOON, n_late))
    units = n_expert // 3

    def kernel(*refs):
        part_ref, x_ref, d_ref, gain_ref, n_ref, proj_ref = refs[:6]
        router_ref, vec_ref, one_stats, two_stats, own_grads_ref = refs[6:11]
        received_refs, (up_ref, down_ref) = refs[11 : n_in - 2], refs[n_in - 2 : n_in]
        grad_ref, qkv_ref, one_ref, both_ref, in_ref, out_ref = refs[n_in : n_in + n_out]
        scratch = refs[n_in + n_out :]
        join, scratch = scratch[:N_DIRECT], scratch[N_DIRECT:]
        own, few, summed, more, send, recv, tsend, trecv = scratch[:8]
        qbuf, qgot, qsum, qin, csend, crecv, ksend, krecv = scratch[8:16]
        acc, others, lsem, osem, esend, erecv, full = scratch[16:]
        me, t = lax.axis_index("dp"), lax.axis_index("tensor")
        core, chip = me % 2, me // 2
        greet(tensor_peers() + dp_peers())
        got, mine, jsend, jrecv, asend, arecv, alocal = join
        scatter = DirectScatter(part_ref, got, jsend, jrecv)
        gather = YGather(mine, full, asend, arecv, alocal)
        scatter.start()
        rest = Sends(
            [
                (ref.at[pl.ds(at, n)], others.at[i, pl.ds(NOW + at, n)], along_y(shift))
                for at, n in parts
                for i, (ref, shift) in enumerate(((up_ref, 1), (down_ref, 3)))
            ],
            esend,
            erecv,
        )
        for copy in rest.copies[:2]:
            copy.start()
        loads = [pltpu.make_async_copy(own_grads_ref, acc, lsem.at[0])] + [
            pltpu.make_async_copy(r, others.at[i, first], lsem.at[i + 1])
            for i, r in enumerate(received_refs)
        ]
        for load in loads:
            load.start()
        across = []
        for c in range(8):
            for side in range(2):
                cols = slice((2 * c + side) * 128, (2 * c + side + 1) * 128)
                qbuf[c, side] = mm(n_ref[:, cols], proj_ref[...], TN).astype(bf16)
            across.append(
                remote(qbuf.at[c, 1 - core], qgot.at[c], csend.at[c], crecv.at[c], {"dp": me ^ 1})
            )
            across[-1].start()
        for c in range(8):
            across[c].wait_recv()
            qsum[c] = (qbuf[c, core].astype(f32) + qgot[c].astype(f32)).astype(bf16)
        chips = [
            remote(
                qsum.at[chip ^ k], qin.at[k], ksend.at[k], krecv.at[k], {"dp": me ^ (2 * k)}
            )
            for k in range(1, 8)
        ]
        for copy in chips:
            copy.start()
        bias = column_sum(proj_ref[...].astype(f32))
        stats = [one_stats[k : k + 1] for k in range(3)] + [two_stats[k : k + 1] for k in (1, 2)]
        rows_all = [sum(row[:, i * 128 : (i + 1) * 128] for i in range(N_DP)) for row in stats] + [
            bias[:, i * 128 : (i + 1) * 128] for i in range(wide // 128)
        ]
        for i in range(N_DP):
            cols = slice(i * 128, (i + 1) * 128)
            own[i, 0:16] = router_ref[:, cols]
            own[i, 16:17] = vec_ref[:, cols]
            own[i, 17:18] = two_stats[0:1, cols]
            for k, row in enumerate(rows_all):
                own[i, 19 + k : 20 + k] = row
            own[i, 19 + len(rows_all) : small] = jnp.zeros((small - 19 - len(rows_all), 128), f32)
        resid = x_ref[t].astype(f32)
        inv = second_moment(resid)
        d_normed = scatter.total()
        scaled = d_normed * gain_ref[...]
        mine[...] = (
            d_ref[...]
            + inv * scaled
            - resid * (inv * inv * inv) * jnp.mean(scaled * resid, axis=1, keepdims=True)
        ).astype(bf16)
        gather.start()
        gain_grad = column_sum(d_normed * resid * inv)
        for i in range(N_DP):
            own[i, 18:19] = gain_grad[:, i * 128 : (i + 1) * 128]
        firsts = [
            remote(own.at[me ^ k], few.at[k], send.at[k], recv.at[k], {"dp": me ^ k})
            for k in range(1, N_DP)
        ]
        for copy in firsts:
            copy.start()
        for copy in rest.copies[2:]:
            copy.start()
        value = own[me]
        for k in range(1, N_DP):
            firsts[k - 1].wait_recv()
            value = value + few[k]
        one_ref[...] = value
        summed[...] = value
        seconds = [
            remote(summed, more.at[k], tsend.at[k], trecv.at[k], {"tensor": t ^ k}) for k in range(1, N_T)
        ]
        for copy in seconds:
            copy.start()
        gather.relay()
        for load in loads:
            load.wait()
        for copy in rest.copies:
            copy.wait_recv()

        def add(j, carry):
            cols = pl.ds(pl.multiple_of(j * 256, 256), 256)
            total = acc[:, cols]
            for i in range(len(received)):
                total = total + others[i, :, cols].astype(f32)
            acc[:, cols] = total
            return carry

        lax.fori_loop(0, width // 256, add, 0)
        stores = [
            pltpu.make_async_copy(acc.at[pl.ds(0, 2 * units)], in_ref, osem.at[0]),
            pltpu.make_async_copy(acc.at[pl.ds(2 * units, units)], out_ref, osem.at[1]),
        ]
        for store in stores:
            store.start()
        total = qsum[chip].astype(f32)
        for k in range(1, 8):
            chips[k - 1].wait_recv()
            total = total + qin[k].astype(f32)
        qkv_ref[...] = total
        for k in range(1, N_T):
            seconds[k - 1].wait_recv()
            value = value + more[k]
        both_ref[...] = value
        for copy in firsts + seconds + across + chips + rest.copies:
            copy.wait_send()
        scatter.wait_send()
        gather.wait()
        grad_ref[...] = full[...].astype(f32)
        for store in stores:
            store.wait()

    return pl.pallas_call(
        kernel,
        out_shape=(
            struct(part.shape, f32),
            struct((width // N_DP, wide), f32),
            struct((small, 128), f32),
            struct((small, 128), f32),
            struct((2 * units, width), f32),
            struct((units, width), f32),
        ),
        in_specs=[VMEM] * 10 + [HBM] * (n_in - 10),
        out_specs=(VMEM,) * 4 + (HBM,) * 2,
        scratch_shapes=[
            pltpu.VMEM(part.shape, bf16),
            pltpu.VMEM((rows, width), bf16),
        ]
        + sems(N_T, N_T, (2, 4), (2, 4), 1)
        + [
            pltpu.VMEM((N_DP, small, 128), f32),
            pltpu.VMEM((N_DP, small, 128), f32),
            pltpu.VMEM((small, 128), f32),
            pltpu.VMEM((N_T, small, 128), f32),
        ]
        + sems(N_DP, N_DP, N_T, N_T)
        + [
            pltpu.VMEM((8, 2, 128, wide), bf16),
            pltpu.VMEM((8, 128, wide), bf16),
            pltpu.VMEM((8, 128, wide), bf16),
            pltpu.VMEM((8, 128, wide), bf16),
        ]
        + sems(8, 8, 8, 8)
        + [
            pltpu.VMEM((n_expert, width), f32),
            pltpu.VMEM((len(received), n_expert, width), bf16),
        ]
        + sems(1 + len(received), 2, 4, 4)
        + [pltpu.VMEM(part.shape, bf16)],
        compiler_params=comm_params(number, LIMIT),
        name="join_tail",
        cost_estimate=cost(55),
    )(part, layer_input, d_middle, gain, normed, d_proj, *smalls, own_grads, *received, *waiting)


def doc_layout(lengths, token_index):
    doc_ends = jnp.cumsum(lengths)
    starts = doc_ends - lengths
    seq_ids = jnp.sum((token_index[:, None] >= doc_ends[None, :]).astype(jnp.int32), axis=1)
    member = seq_ids[:, None] == jnp.arange(lengths.shape[0], dtype=jnp.int32)[None, :]
    begins = jnp.sum(jnp.where(member, starts[None, :], 0), axis=1)
    offsets = token_index - begins
    return (seq_ids, offsets, offsets // DBLOCK)


def rope_tables(offsets, head_dim):
    half_dim = head_dim // 2
    frequencies = jnp.exp(
        jnp.arange(half_dim, dtype=f32) * (-2.0 * math.log(THETA) / head_dim)
    )
    angles = offsets.astype(f32)[:, None] * frequencies[None, :]
    return (jnp.cos(angles)[:, None, :], jnp.sin(angles)[:, None, :])


def rotate(vectors, cosine, sine):
    half_dim = vectors.shape[-1] // 2
    front, back = vectors[..., :half_dim], vectors[..., half_dim:]
    return jnp.concatenate([front * cosine - back * sine, back * cosine + front * sine], axis=-1)


def dot(pattern, a, b):
    return jnp.einsum(pattern, a, b, preferred_element_type=f32)


def on_device(
    layer_input,
    doc_lengths,
    expert_ids,
    attn_gain,
    qkv_weight,
    qkv_bias,
    out_weight,
    ffn_gain,
    router_weight,
    shared_gate,
    shared_in,
    shared_out,
    expert_in,
    expert_out,
    cotangent,
):
    tok, width = layer_input.shape
    dp, tn = lax.axis_index("dp"), lax.axis_index("tensor")
    experts_n = router_weight.shape[1]
    head_dim = qkv_weight.shape[3]
    stream = tok * N_DP
    part_rows = tok // N_T
    score_scale = head_dim ** (-0.5)
    eff = expert_out.shape[1]

    in_rows = expert_in[0].transpose(1, 2, 0).reshape(2 * eff, width)

    hot = jnp.sum(
        (expert_ids[:, :, None] == jnp.arange(experts_n, dtype=jnp.int32)[None, None, :]).astype(f32),
        axis=1,
    )
    before = (jnp.arange(tok)[:, None] > jnp.arange(tok)[None, :]).astype(bf16)
    rank = dot("ts,se->te", before, hot.astype(bf16))
    place = jnp.where(hot > 0, rank, -1.0).astype(jnp.int32).T
    _, offset = route_plane()
    served = lax.dynamic_slice_in_dim(place, GROUPS * ((dp // 4) ^ offset), GROUPS, 0)
    places = (served[:, None, :] == jnp.arange(SLOTS, dtype=jnp.int32)[None, :, None]).astype(bf16)
    returned = lax.dynamic_index_in_dim(place.reshape(GROUPS, 4, tok), offset, 1, keepdims=False)
    places_back = (
        (returned[:, None, :] == jnp.arange(SLOTS, dtype=jnp.int32)[None, :, None])
        .astype(bf16)
        .reshape(GROUPS * SLOTS, tok)
    )

    local_index = dp * tok + jnp.arange(tok, dtype=jnp.int32)
    _, pos_local, _ = doc_layout(doc_lengths, local_index)
    cosine, sine = rope_tables(pos_local, head_dim)
    residual = layer_input.astype(f32)
    inv_first = lax.rsqrt(jnp.mean(residual * residual, axis=1, keepdims=True) + EPSILON)
    normed_one = (residual * inv_first * attn_gain).astype(bf16)
    projected = dot("td,dshe->tshe", normed_one, qkv_weight) + qkv_bias.astype(f32)[None]
    q_own = rotate(projected[:, 0], cosine, sine).astype(bf16).transpose(1, 0, 2)
    k_own = rotate(projected[:, 1], cosine, sine).astype(bf16).transpose(1, 0, 2)
    v_own = projected[:, 2].astype(bf16).transpose(1, 0, 2)
    by_slice = (N_T, part_rows, width)
    out_flat = out_weight.reshape(2 * head_dim, width)
    keys, values, queries, wide, logs, heads_out, normed_two, middle, stats_one, *neighbours = attend_forward(
        k_own,
        v_own,
        q_own,
        doc_lengths,
        out_flat,
        layer_input.reshape(by_slice),
        ffn_gain.reshape(1, width),
        [in_rows, expert_out[0]],
        1,
    )
    normed_two = normed_two.reshape(tok, width)

    own_expert = jnp.broadcast_to(
        (jnp.arange(experts_n, dtype=jnp.int32) == dp).astype(f32)[:, None], (experts_n, 128)
    )
    back_grads, back_out, mixed, shared_d_normed, got, gate_vec_part, router_part, own_grads, *sent = experts(
        places,
        *neighbours,
        in_rows,
        expert_out[0],
        normed_two,
        cotangent,
        shared_in.transpose(1, 2, 0).reshape(-1, width),
        shared_out,
        shared_gate.astype(f32).reshape(1, width),
        router_weight.T,
        own_expert,
        5,
    )

    by_z = got.reshape((4, 2) + got.shape[1:])

    def combine(rows):
        return dot("rt,rd->td", places_back, rows.reshape(-1, width))

    d_normed_part = (shared_d_normed + combine(back_grads)).astype(bf16)
    moe_part = (mixed + combine(back_out)).astype(bf16)
    d_middle, stats_two, d_keys, d_queries, outproj_grad, shared_in_grad, shared_out_grad, output, *moved = backward(
        d_normed_part.reshape(by_slice),
        moe_part.reshape(by_slice),
        cotangent.reshape(by_slice),
        middle,
        ffn_gain.reshape(1, width),
        out_flat,
        heads_out,
        queries,
        keys,
        values,
        wide,
        logs,
        doc_lengths,
        by_z,
        sent,
        7,
    )

    cosine, sine = cosine[:, 0], sine[:, 0]
    d_proj = jnp.concatenate(
        [rotate(d_queries[h].astype(f32), cosine, -sine) for h in range(2)]
        + [rotate(d_keys[h, :tok], cosine, -sine) for h in range(2)]
        + [d_keys[h, tok:] for h in range(2)],
        axis=1,
    ).astype(bf16)
    d_normed_one = dot(
        "tshe,dshe->td", d_proj.reshape(tok, 3, 2, head_dim), qkv_weight
    ).astype(bf16)
    input_grad, qkv_grad, over_dp, over_both, expert_in_grad, expert_out_grad = join_tail(
        d_normed_one.reshape(by_slice),
        layer_input.reshape(by_slice),
        d_middle,
        attn_gain.reshape(1, width),
        normed_one,
        d_proj,
        [router_part, gate_vec_part, stats_one, stats_two],
        own_grads,
        moved[:2],
        moved[2:],
        10,
    )
    bias_grad = lax.dynamic_slice_in_dim(over_dp[24:30], 8 * dp, 8, 1).reshape(3, 2, 8)
    rms_stats = jnp.sqrt(jnp.sum(over_both[19:24], axis=1) / (stream * width))

    return (
        output.reshape(tok, width),
        input_grad.reshape(tok, width),
        qkv_grad.reshape(width // N_DP, 3, 2, head_dim),
        bias_grad,
        outproj_grad.T.reshape(2, head_dim, width // N_DP),
        over_both[18],
        over_both[17],
        over_both[:16].T,
        over_both[16],
        shared_in_grad.reshape(2, shared_in.shape[2], -1).transpose(2, 0, 1),
        shared_out_grad,
        expert_in_grad.reshape(2, eff, width).transpose(2, 0, 1)[None],
        expert_out_grad[None],
        rms_stats,
    )


def solution(mesh):
    in_specs = (
        P("dp", None),
        P(),
        P("dp", None),
        P(),
        P(None, None, "tensor", None),
        P(None, "tensor", None),
        P("tensor", None, None),
        P(),
        P(),
        P(),
        P(None, None, "tensor"),
        P("tensor", None),
        P("dp", None, None, "tensor"),
        P("dp", "tensor", None),
        P("dp", None),
    )
    out_specs = (
        P("dp", None),
        P("dp", None),
        P("dp", None, "tensor", None),
        P(None, "tensor", "dp"),
        P("tensor", None, "dp"),
        P("dp"),
        P("dp"),
        P("dp", None),
        P("dp"),
        P("dp", None, "tensor"),
        P("tensor", "dp"),
        P("dp", None, None, "tensor"),
        P("dp", "tensor", None),
        P(),
    )
    return jax.shard_map(
        on_device, mesh=mesh, in_specs=in_specs, out_specs=out_specs, check_vma=False
    )
```

```python
import math

import jax
import jax.numpy as jnp
from jax import lax
from jax.experimental import pallas as pl
from jax.experimental.pallas import tpu as pltpu
from jax.sharding import PartitionSpec as P

DBLOCK = 256
EPSILON = 1e-06
THETA = 1000000.0
NEG_FILL = -1e30
MESH = pl.DeviceIdType.MESH
f32 = jnp.float32
bf16 = jnp.bfloat16
N_DP = 16
N_T = 8
SLOTS = 112
LIMIT = 48 * 1024 * 1024
CODE = 1 << 16

HBM = pl.BlockSpec(memory_space=pl.ANY)
VMEM = pl.BlockSpec(memory_space=pltpu.VMEM)
SMEM = pl.BlockSpec(memory_space=pltpu.SMEM)


def greet(peers, *more):
    barrier = pltpu.get_barrier_semaphore()
    for peer in peers:
        pl.semaphore_signal(barrier, inc=1, device_id=peer, device_id_type=MESH)
    count = len(peers)
    for rows in more:
        count = count + rows.greet()
    pl.semaphore_wait(barrier, count)


def remote(src, dst, send, recv, device):
    return pltpu.make_async_remote_copy(
        src_ref=src,
        dst_ref=dst,
        send_sem=send,
        recv_sem=recv,
        device_id=device,
        device_id_type=MESH,
    )


def dma(*shape):
    return pltpu.SemaphoreType.DMA(shape)


def cost(micros):
    return pl.CostEstimate(flops=0, bytes_accessed=int(micros * 3e6), transcendentals=0)


def comm_params(number, limit=None):
    return pltpu.CompilerParams(
        collective_id=number, has_side_effects=True, vmem_limit_bytes=limit
    )


NT = (((1,), (1,)), ((), ()))
TN = (((0,), (0,)), ((), ()))


def mm(a, b, dims=(((1,), (0,)), ((), ()))):
    return lax.dot_general(a, b, dims, preferred_element_type=f32)


GROUPS = 4
HALF = 256
SOON = 96
ORDER = (4, 12, 2, 5, 13, 3, 8, 6, 14, 9, 7, 15, 10, 11, 1)
STEPS = (1, 3, 2, 4, 5, 7, 6)
CHUNKS = ((0, 48), (48, 64))


def sems(*counts):
    return [dma(*c) if isinstance(c, tuple) else dma(c) for c in counts]


def dp_peers():
    me = lax.axis_index("dp")
    return [{"dp": me ^ k} for k in range(1, N_DP)]


def tensor_peers():
    me = lax.axis_index("tensor")
    return [{"tensor": me ^ k} for k in range(1, N_T)]


def coordinates():
    d, t = lax.axis_index("dp"), lax.axis_index("tensor")
    return d, d // 4, t // 4, t % 4


def route_plane():
    d, z, _, y = coordinates()
    plane = 2 * ((z + d // 2) % 2) + d % 2
    return plane, y ^ plane


class Rows:
    def __init__(self, x_ref, out_ref, send, recv, local, back=False):
        self.x, self.out, self.send, self.recv, self.local, self.back = x_ref, out_ref, send, recv, local, back
        d, z, half, y = coordinates()
        plane, offset = route_plane()
        if back:
            experts = [{"dp": 4 * k + offset, "tensor": 4 * half + plane} for k in range(GROUPS)]
            target = y ^ (d % 4)
        else:
            experts = [{"dp": 4 * (z ^ offset) + j, "tensor": 4 * half + plane} for j in range(GROUPS)]
        groups = [
            {
                "dp": 4 * g + 2 * ((y // 2 + g) % 2) + y % 2,
                "tensor": 4 * half + (target if back else y ^ g ^ z),
            }
            for g in range(GROUPS)
        ]
        self.peers, self.sources = (groups, experts) if back else (experts, groups)
        self.slot = z
        self.mine = z if back else d % 4
        self.own = offset == 0
        if back:
            self.own = jnp.logical_and(self.own, d % 4 == 0)
        self.d = d

    def is_own(self, j):
        return jnp.logical_and(self.own, self.mine == j)

    def greet(self):
        barrier = pltpu.get_barrier_semaphore()
        for j in range(GROUPS):
            source = self.sources[j]

            @pl.when(jnp.logical_not(jnp.logical_and(self.own, self.slot == j)))
            def _():
                pl.semaphore_signal(barrier, inc=1, device_id=source, device_id_type=MESH)

        return GROUPS - self.own.astype(jnp.int32)

    def copy(self, j, c):
        rows = pl.ds(*CHUNKS[c])
        return remote(
            self.x.at[j, rows],
            self.out.at[self.slot, rows],
            self.send.at[c, j],
            self.recv.at[c, self.slot],
            self.peers[j],
        )

    def arrival(self, j, c):
        rows = pl.ds(*CHUNKS[c])
        return remote(
            self.x.at[j, rows],
            self.out.at[j, rows],
            self.send.at[c, j],
            self.recv.at[c, j],
            self.peers[j],
        )

    def inside(self):
        return pltpu.make_async_copy(self.x.at[self.mine], self.out.at[self.slot], self.local.at[0])

    def start_one(self, j):
        @pl.when(jnp.logical_not(self.is_own(j)))
        def _():
            for c in range(len(CHUNKS)):
                self.copy(j, c).start()

        @pl.when(self.is_own(j))
        def _():
            self.inside().start()

    def start(self):
        for j in range(GROUPS):
            self.start_one(j)

    def wait(self):
        @pl.when(self.own)
        def _():
            self.inside().wait()

        for c in range(len(CHUNKS)):
            for j in range(GROUPS):

                @pl.when(jnp.logical_not(self.is_own(j)))
                def _():
                    self.copy(j, c).wait_send()

                @pl.when(jnp.logical_not(jnp.logical_and(self.own, self.slot == j)))
                def _():
                    self.arrival(j, c).wait_recv()


ROW_SEMS = sems((len(CHUNKS), GROUPS), (len(CHUNKS), GROUPS), 1)


class Exchange:
    def __init__(self, x_ref, out_ref, send, recv, local):
        me = lax.axis_index("dp")
        self.copies = [
            remote(x_ref.at[me ^ k], out_ref.at[me], send.at[k], recv.at[k], {"dp": me ^ k})
            for k in ORDER
        ]
        self.copies.append(pltpu.make_async_copy(x_ref.at[me], out_ref.at[me], local.at[0]))

    def start(self):
        for copy in self.copies:
            copy.start()

    def wait(self):
        for copy in self.copies:
            copy.wait()


DP_SEMS = sems(N_DP, N_DP, 1)


class Swap:
    def __init__(self, x_ref, out_ref, send, recv, local):
        me = lax.axis_index("dp")
        core = lax.rem(me, 2)
        self.copies = [
            remote(x_ref.at[1 - core], out_ref.at[core], send.at[0], recv.at[0], {"dp": me ^ 1}),
            pltpu.make_async_copy(x_ref.at[core], out_ref.at[core], local.at[0]),
        ]

    start = Exchange.start
    wait = Exchange.wait


SWAP_SEMS = sems(1, 1, 1)


class DirectScatter:
    def __init__(self, part_ref, got, send, recv):
        self.me = lax.axis_index("tensor")
        self.part, self.got = part_ref, got
        self.copies = [
            remote(
                part_ref.at[self.me ^ k], got.at[k], send.at[k], recv.at[k], {"tensor": self.me ^ k}
            )
            for k in STEPS
        ]

    def start(self):
        for copy in self.copies:
            copy.start()

    def total(self):
        value = self.part[self.me].astype(f32)
        for k, copy in zip(STEPS, self.copies):
            copy.wait_recv()
            value = value + self.got[k].astype(f32)
        return value

    def wait_send(self):
        for copy in self.copies:
            copy.wait_send()


class DirectGather:
    def __init__(self, mine, full_ref, send, recv, local):
        me = lax.axis_index("tensor")
        self.mine = mine
        self.copies = [
            remote(mine, full_ref.at[me], send.at[k], recv.at[k], {"tensor": me ^ k}) for k in STEPS
        ]
        self.copies.append(pltpu.make_async_copy(mine, full_ref.at[me], local.at[0]))

    def start(self, value):
        self.mine[...] = value.astype(bf16)
        for copy in self.copies:
            copy.start()

    def wait(self):
        for copy in self.copies:
            copy.wait()


def direct_scratch(rows, width):
    return [
        pltpu.VMEM((N_T, rows, width), bf16),
        pltpu.VMEM((rows, width), bf16),
    ] + sems(N_T, N_T, N_T, N_T, 1)


N_DIRECT = 7


def direct_parts(part_ref, full_ref, scratch):
    got, mine, send, recv, asend, arecv, local = scratch
    return DirectScatter(part_ref, got, send, recv), DirectGather(mine, full_ref, asend, arecv, local)


class Scatter:
    def __init__(self, part_ref, got, mid, last, send, recv):
        t = lax.axis_index("tensor")
        y, half = t % 4, t // 4
        self.part, self.got, self.mid, self.last = part_ref, got, mid, last
        self.slots = (4 * (1 - half) + y, t)
        self.copies = [
            [
                remote(
                    part_ref.at[slot ^ k],
                    got.at[a, k],
                    send.at[a, k],
                    recv.at[a, k],
                    {"tensor": t ^ k},
                )
                for k in (1, 3, 2)
            ]
            for a, slot in enumerate(self.slots)
        ]
        self.across = remote(mid, last, send.at[0, 0], recv.at[0, 0], {"tensor": t ^ 4})

    def start(self):
        for copies in self.copies:
            for copy in copies:
                copy.start()

    def over_y(self, a):
        value = self.part[self.slots[a]].astype(f32)
        for k, copy in zip((1, 3, 2), self.copies[a]):
            copy.wait_recv()
            value = value + self.got[a, k].astype(f32)
        return value

    def middle(self):
        self.mid[...] = self.over_y(0).astype(bf16)
        self.across.start()

    def total(self):
        value = self.over_y(1)
        self.across.wait_recv()
        return value + self.last[...].astype(f32)

    def wait_send(self):
        for copies in self.copies:
            for copy in copies:
                copy.wait_send()
        self.across.wait_send()


class Gather:
    def __init__(self, mine, full_ref, send, recv, local):
        t = lax.axis_index("tensor")
        self.mine = mine
        self.across = remote(
            mine, full_ref.at[t], send.at[0, 0], recv.at[0, 0], {"tensor": t ^ 4}
        )
        self.first = [
            remote(mine, full_ref.at[t], send.at[0, k], recv.at[0, k], {"tensor": t ^ k})
            for k in (1, 3, 2)
        ]
        self.second = [
            remote(
                full_ref.at[t ^ 4],
                full_ref.at[t ^ 4],
                send.at[1, k],
                recv.at[1, k],
                {"tensor": t ^ k},
            )
            for k in (1, 3, 2)
        ]
        self.own = pltpu.make_async_copy(mine, full_ref.at[t], local.at[0])

    def start(self, value):
        self.mine[...] = value.astype(bf16)
        for copy in [self.across] + self.first + [self.own]:
            copy.start()

    def relay(self):
        self.across.wait_recv()
        for copy in self.second:
            copy.start()

    def wait(self):
        self.across.wait_send()
        for copy in self.first + self.second + [self.own]:
            copy.wait()


class YGather:
    def __init__(self, mine, full_ref, send, recv, local):
        t = lax.axis_index("tensor")
        self.first = [
            remote(mine, full_ref.at[t], send.at[0, k], recv.at[0, k], {"tensor": t ^ k})
            for k in (1, 3, 2)
        ]
        self.second = [
            remote(full_ref.at[t ^ k], full_ref.at[t ^ k], send.at[1, k], recv.at[1, k], {"tensor": t ^ 4})
            for k in (1, 3, 2)
        ]
        self.across = remote(mine, full_ref.at[t], send.at[1, 0], recv.at[1, 0], {"tensor": t ^ 4})
        self.own = pltpu.make_async_copy(mine, full_ref.at[t], local.at[0])

    def start(self):
        for copy in self.first + [self.across, self.own]:
            copy.start()

    def relay(self):
        for first, second in zip(self.first, self.second):
            first.wait_recv()
            second.start()

    def wait(self):
        for copy in self.first:
            copy.wait_send()
        for copy in self.second + [self.across, self.own]:
            copy.wait()


class Sends:
    def __init__(self, messages, send, recv):
        self.copies = [
            remote(src, dst, send.at[i], recv.at[i], peer) for i, (src, dst, peer) in enumerate(messages)
        ]

    start = Exchange.start
    wait = Exchange.wait


def struct(shape, dtype):
    return jax.ShapeDtypeStruct(shape, dtype)


def column_sum(value):
    return jnp.sum(value, axis=0, keepdims=True)


def second_moment(value):
    return lax.rsqrt(jnp.mean(value * value, axis=1, keepdims=True) + EPSILON)


def codes_of(index, lengths_ref):
    end, seq, begin = 0, 0, 0
    for j in range(lengths_ref.shape[0]):
        end = end + lengths_ref[j]
        past = index >= end
        seq = seq + past.astype(jnp.int32)
        begin = jnp.where(past, end, begin)
    return seq * CODE, seq * CODE + lax.shift_right_arithmetic(index - begin, DBLOCK.bit_length() - 1)


def codes_of_keys(group, count, lengths_ref):
    index = group * count + lax.broadcasted_iota(jnp.int32, (count, 1), 0)
    return codes_of(index, lengths_ref)[1]


def codes_of_queries(chip, count, lengths_ref):
    index = chip * count + lax.broadcasted_iota(jnp.int32, (1, count), 1)
    return codes_of(index, lengths_ref)


def attend(q, state, k, v, code, bounds, factor):
    peak, total, acc = state
    scores = mm(k, q, NT) * factor
    seen = (code >= bounds[0]) & (code <= bounds[1])
    scores = jnp.where(seen, scores, NEG_FILL)
    new_peak = jnp.maximum(peak, jnp.max(scores, axis=0, keepdims=True))
    terms = jnp.exp2(scores - new_peak)
    shrink = jnp.exp2(peak - new_peak)
    total = total * shrink + jnp.sum(terms, axis=0, keepdims=True)
    acc = acc * shrink + mm(v, terms.astype(bf16), TN)
    return new_peak, total, acc


def along_y(shift):
    t = lax.axis_index("tensor")
    return {"tensor": 4 * (t // 4) + (t + shift) % 4}


def weights_along_y(weight_refs, n_rows, results, send, recv):
    messages = []
    for result, shift in zip(results, (1, 3)):
        at = 0
        for ref, count in zip(weight_refs, n_rows):
            messages.append((ref, result.at[pl.ds(at, count)], along_y(shift)))
            at += count
    return Sends(messages, send, recv)


def attend_forward(k, v, q, lengths, out_weight, layer_input, gain, weights, number):
    _, tok, size = q.shape
    n_rows = [w.shape[0] for w in weights]
    stream, count = N_DP * tok, 2 * tok
    _, rows, width = layer_input.shape
    factor = size ** (-0.5) * math.log2(math.e)

    def kernel(k_ref, v_ref, q_ref, lengths_ref, w_ref, x_ref, gain_ref, *refs):
        weight_refs, outs, scratch = refs[:2], refs[2:14], refs[14:]
        keys_ref, values_ref, pair_ref, wide_ref, log_ref, heads_ref, full_ref, middle_ref, stats_ref = outs[:9]
        keys, values, pair, own_out, heads, part = scratch[:6]
        send, recv, local = scratch[6:9]
        swap_sems, out_sems, store_sems, weight_sems = scratch[9:12], scratch[12:14], scratch[14], scratch[15:17]
        relay_sems, join = scratch[17:19], scratch[19:]
        me = lax.axis_index("dp")
        core = lax.rem(me, 2)
        greet(tensor_peers() + dp_peers())
        both = weights_along_y(weight_refs, n_rows, outs[9:11], *weight_sems)
        both.start()
        swap = Swap(q_ref, pair, *swap_sems)
        swap.start()

        def place(group):
            return pl.ds(pl.multiple_of(group * tok, tok), tok)

        def copies(step, head):
            return [
                remote(
                    own.at[head],
                    full.at[place(me)],
                    send.at[i, step],
                    recv.at[i, step],
                    {"dp": me ^ step},
                )
                for i, (own, full) in enumerate(((k_ref, keys), (v_ref, values)))
            ]

        for step in ORDER:
            for copy in copies(step, core if step % 2 == 0 else 1 - core):
                copy.start()
        locals_ = [
            pltpu.make_async_copy(own.at[core], full.at[place(me)], local.at[i])
            for i, (own, full) in enumerate(((k_ref, keys), (v_ref, values)))
        ]
        for copy in locals_:
            copy.start()
        swap.wait()
        for copy in locals_:
            copy.wait()
        queries = pair[...].reshape(count, size)
        limits = codes_of_queries(me // 2, count, lengths_ref)

        def block(group, state):
            at = place(group)
            code = codes_of_keys(group, tok, lengths_ref)
            return attend(queries, state, keys[at], values[at], code, limits, factor)

        def arrived(step, state):
            group = me ^ step
            for i, (own, full) in enumerate(((k_ref, keys), (v_ref, values))):
                remote(
                    own.at[core], full.at[place(group)], send.at[i, step], recv.at[i, step], {"dp": group}
                ).wait_recv()
            return block(group, state)

        state = block(
            me,
            (
                jnp.full((1, count), NEG_FILL, f32),
                jnp.zeros((1, count), f32),
                jnp.zeros((size, count), f32),
            ),
        )
        peak, total, acc = lax.fori_loop(1, N_DP, arrived, state)
        out = (acc / total).T
        wide_ref[...] = out
        log_ref[...] = jnp.broadcast_to(peak + jnp.log2(total), (8, count))
        own_out[...] = out.astype(bf16).reshape(2, tok, size)
        across = remote(
            own_out.at[1 - core], heads.at[core], out_sems[0].at[0], out_sems[1].at[0], {"dp": me ^ 1}
        )
        across.start()
        heads[core] = own_out[core]
        stores = [
            pltpu.make_async_copy(keys, keys_ref, store_sems.at[0]),
            pltpu.make_async_copy(values, values_ref, store_sems.at[1]),
            pltpu.make_async_copy(pair, pair_ref, store_sems.at[2]),
        ]
        for store in stores:
            store.start()
        across.wait_recv()
        heads_ref[:, 0:size] = heads[0]
        heads_ref[:, size : 2 * size] = heads[1]

        def project(j, carry):
            cols = pl.ds(pl.multiple_of(j * 512, 512), 512)
            value = mm(heads_ref[...], w_ref[:, cols])
            part[:, :, cols] = value.reshape(N_T, rows, 512).astype(bf16)
            return carry

        lax.fori_loop(0, width // 512, project, 0)
        scatter = DirectScatter(part, join[0], *join[2:4])
        mine = join[1]
        gather = YGather(mine, full_ref, *join[4:])
        scatter.start()
        for copy in both.copies:
            copy.wait_recv()
        below_ref, above_ref, far_ref = outs[9:]
        relay = Sends(
            [
                (ref.at[pl.ds(at, n)], far_ref.at[pl.ds(at, n)], along_y(shift))
                for ref, shift, at, n in (
                    (below_ref, 1, 0, SOON),
                    (above_ref, 3, HALF, SOON),
                    (below_ref, 1, SOON, HALF - SOON),
                    (above_ref, 3, HALF + SOON, sum(n_rows) - HALF - SOON),
                )
            ],
            *relay_sems,
        )
        for copy in relay.copies[:2]:
            copy.start()
        resid = x_ref[lax.axis_index("tensor")].astype(f32)
        attn_out = scatter.total()
        middle = resid + attn_out
        mine[...] = (middle * second_moment(middle) * gain_ref[...]).astype(bf16)
        gather.start()
        for copy in relay.copies[2:]:
            copy.start()
        middle_ref[...] = middle
        stats_ref[0:1] = column_sum(resid * resid)
        stats_ref[1:2] = column_sum(attn_out * attn_out)
        stats_ref[2:3] = column_sum(middle * middle)
        gather.relay()
        for step in ORDER:
            for copy in copies(step, core):
                copy.wait_send()
        across.wait_send()
        scatter.wait_send()
        for store in stores:
            store.wait()
        gather.wait()
        for copy in both.copies:
            copy.wait_send()
        relay.wait()

    return pl.pallas_call(
        kernel,
        out_shape=(
            struct((stream, size), bf16),
            struct((stream, size), bf16),
            struct(q.shape, bf16),
            struct((count, size), f32),
            struct((8, count), f32),
            struct((tok, 2 * size), bf16),
            struct(layer_input.shape, bf16),
            struct((rows, width), f32),
            struct((8, width), f32),
        )
        + (struct((sum(n_rows), width), bf16),) * 3,
        in_specs=[HBM] * 3 + [SMEM] + [VMEM] * 3 + [HBM] * 2,
        out_specs=(HBM,) * 3 + (VMEM,) * 3 + (HBM,) + (VMEM,) * 2 + (HBM,) * 3,
        scratch_shapes=[
            pltpu.VMEM((stream, size), bf16),
            pltpu.VMEM((stream, size), bf16),
            pltpu.VMEM(q.shape, bf16),
            pltpu.VMEM(q.shape, bf16),
            pltpu.VMEM(q.shape, bf16),
            pltpu.VMEM(layer_input.shape, bf16),
        ]
        + sems((2, N_DP), (2, N_DP), 2)
        + SWAP_SEMS
        + sems(1, 1, 3, 4, 4, 4, 4)
        + [
            pltpu.VMEM(layer_input.shape, bf16),
            pltpu.VMEM((rows, width), bf16),
        ]
        + sems(N_T, N_T, (2, 4), (2, 4), 1),
        compiler_params=comm_params(number, LIMIT),
        name="attend_forward",
        cost_estimate=cost(85),
    )(k, v, q, lengths, out_weight, layer_input, gain, *weights)


def sigmoid(x):
    return 1.0 / (1.0 + jnp.exp(-x))


TILE = 176
NOW = 208


def shared_expert(x_ref, up_ref, w_ref, vec_ref, part_ref, d_ref, grads_ref, row_ref, low_ref):
    hidden = w_ref.shape[0] // 3
    vec = vec_ref[...]
    gate = sigmoid(jnp.sum(x_ref[...].astype(f32) * vec, axis=1, keepdims=True))
    low_ref[...] = (gate * up_ref[...].astype(f32)).astype(bf16)
    part_ref[...] = jnp.zeros_like(part_ref)
    d_ref[...] = jnp.zeros_like(d_ref)

    def tile(i, carry):
        rows = [pl.ds(pl.multiple_of(i * TILE + k * hidden, 16), TILE) for k in range(3)]
        x, d_out = x_ref[...], low_ref[...]
        gate_part = mm(w_ref[rows[0]], x, NT)
        up_part = mm(w_ref[rows[1]], x, NT)
        sig = sigmoid(gate_part)
        act = gate_part * sig
        unit = (act * up_part).astype(bf16)
        d_unit = mm(w_ref[rows[2]], d_out, NT)
        d_gate = (d_unit * up_part * sig * (1.0 + gate_part * (1.0 - sig))).astype(bf16)
        d_up = (d_unit * act).astype(bf16)

        def block(j, carry):
            cols = pl.ds(pl.multiple_of(j * 256, 256), 256)
            xs, ds = x_ref[:, cols], low_ref[:, cols]
            part_ref[:, cols] += mm(unit, w_ref[rows[2], cols], TN)
            d_ref[:, cols] += mm(d_gate, w_ref[rows[0], cols], TN) + mm(d_up, w_ref[rows[1], cols], TN)
            for k, grad in enumerate((mm(d_gate, xs), mm(d_up, xs), mm(unit, ds))):
                grad = grad.astype(bf16)
                grads_ref[j, 0, rows[k]] = grad[:, :128]
                grads_ref[j, 1, rows[k]] = grad[:, 128:]
            return carry

        return lax.fori_loop(0, x.shape[1] // 256, block, carry)

    lax.fori_loop(0, hidden // TILE, tile, 0)
    total = part_ref[...]
    d_logit = jnp.sum(up_ref[...].astype(f32) * total, axis=1, keepdims=True) * gate * (1.0 - gate)
    part_ref[...] = gate * total
    d_ref[...] += d_logit * vec
    row_ref[...] = column_sum(d_logit * x_ref[...].astype(f32))


class Routed:
    def __init__(self, x_ref, up_ref, w_ref, router_ref, own, acc, dgu_ref, unit_ref, slope_ref, router_grad_ref):
        groups, slots, self.width = x_ref.shape
        self.rows, self.units = groups * slots, w_ref.shape[1] // 3
        self.x_ref, self.up_ref, self.w_ref, self.router_ref, self.own = x_ref, up_ref, w_ref, router_ref, own
        self.acc, self.dgu_ref, self.unit_ref, self.slope_ref = acc, dgu_ref, unit_ref, slope_ref
        self.router_grad_ref = router_grad_ref

    def flat(self, ref):
        return ref[...].reshape(self.rows, self.width)

    def start(self):
        logits = mm(self.router_ref[...], self.flat(self.x_ref), NT)
        terms = jnp.exp(logits - jnp.max(logits, axis=0, keepdims=True))
        self.probs = terms / jnp.sum(terms, axis=0, keepdims=True)
        self.gate = jnp.sum(self.probs * self.own, axis=0, keepdims=True)
        self.acc[...] = jnp.zeros_like(self.acc)

    def blocks(self, body):
        def block(j, carry):
            body(pl.ds(pl.multiple_of(j * 512, 512), 512))
            return carry

        lax.fori_loop(0, self.width // 512, block, 0)

    def forward(self):
        units, rows, w_ref = self.units, self.rows, self.w_ref

        def piece(i, carry):
            gate_part = mm(w_ref[i, 0:units], self.flat(self.x_ref), NT)
            up_part = mm(w_ref[i, units : 2 * units], self.flat(self.x_ref), NT)
            sig = sigmoid(gate_part)
            act = gate_part * sig
            gated = (act * up_part * self.gate).astype(bf16)
            slope = self.gate * up_part * sig * (1.0 + gate_part * (1.0 - sig))
            self.slope_ref[i, 0] = slope.astype(bf16)
            self.slope_ref[i, 1] = (self.gate * act).astype(bf16)
            self.unit_ref[i] = gated

            def add(cols):
                self.acc[0:rows, cols] += mm(gated, w_ref[i, 2 * units : 3 * units, cols], TN)

            self.blocks(add)
            return carry

        lax.fori_loop(0, GROUPS, piece, 0)

    def backward(self):
        units, rows, w_ref = self.units, self.rows, self.w_ref

        def piece(i, gated_d_gate):
            raw = mm(w_ref[i, 2 * units : 3 * units], self.flat(self.up_ref), NT)
            d_gate = (raw * self.slope_ref[i, 0].astype(f32)).astype(bf16)
            d_up = (raw * self.slope_ref[i, 1].astype(f32)).astype(bf16)
            self.dgu_ref[i, 0:units] = d_gate
            self.dgu_ref[i, units : 2 * units] = d_up

            def add(cols):
                self.acc[rows : 2 * rows, cols] += mm(d_gate, w_ref[i, 0:units, cols], TN) + mm(
                    d_up, w_ref[i, units : 2 * units, cols], TN
                )

            self.blocks(add)
            return gated_d_gate + jnp.sum(self.unit_ref[i].astype(f32) * raw, axis=0, keepdims=True)

        gated_d_gate = lax.fori_loop(0, GROUPS, piece, jnp.zeros((1, rows), f32))
        d_logits = (gated_d_gate * (self.own - self.probs)).astype(bf16)
        self.router_grad_ref[...] = mm(d_logits, self.flat(self.x_ref))
        self.acc[rows : 2 * rows] += mm(d_logits, self.router_ref[...], TN)


def experts(places, below, above, far_rows, in_rows, out_rows, tokens, upstream, w_in, w_out, vec, router, own, number):
    slots = places.shape[1]
    tok, width = tokens.shape
    hidden, units = w_out.shape[0], out_rows.shape[0]
    n_rows = GROUPS * slots

    def kernel(*refs):
        (below_ref, above_ref, far_ref, in_ref, out_ref, w_in_ref, w_out_ref), refs = refs[:7], refs[7:]
        (places_ref, x_ref, up_ref, vec_ref, router_ref, own_ref), refs = refs[:6], refs[6:]
        (back_d, back_out, part_ref, d_ref, by_z_ref, row_ref, router_grad_ref, mine_ref, *sent_refs), refs = (
            refs[:11],
            refs[11:],
        )
        (weights, low, grads, xs, us, w, acc, dgu, unit, slope, far, send_d, send_out), refs = refs[:13], refs[13:]
        row_sems, refs = [refs[3 * i : 3 * i + 3] for i in range(4)], refs[12:]
        csend, crecv, loaded, stored = refs
        d = lax.axis_index("dp")
        core = lax.rem(d, 2)
        out_x = Rows(send_d, xs, *row_sems[0])
        out_u = Rows(send_out, us, *row_sems[1])
        in_d = Rows(send_d, back_d, *row_sems[2], back=True)
        in_out = Rows(send_out, back_out, *row_sems[3], back=True)
        greet([{"dp": d ^ 1}], out_x, in_d)
        for j in range(GROUPS):
            send_d[j] = mm(places_ref[j], x_ref[...]).astype(bf16)
            out_x.start_one(j)
        for j in range(GROUPS):
            send_out[j] = mm(places_ref[j], up_ref[...]).astype(bf16)
            out_u.start_one(j)
        loads = [
            pltpu.make_async_copy(src, dst, loaded.at[i])
            for i, (src, dst) in enumerate(
                (
                    (w_in_ref, weights.at[pl.ds(0, 2 * hidden)]),
                    (w_out_ref, weights.at[pl.ds(2 * hidden, hidden)]),
                    (in_ref, w.at[0, pl.ds(0, 2 * units)]),
                    (out_ref, w.at[0, pl.ds(2 * units, units)]),
                    (above_ref, w.at[1]),
                    (far_ref, w.at[2]),
                    (below_ref, w.at[3]),
                )
            )
        ]
        for load in loads:
            load.start()
        for load in loads[:2]:
            load.wait()
        shared_expert(x_ref, up_ref, weights, vec_ref, part_ref, d_ref, grads, row_ref, low)
        cores = Sends(
            [(grads.at[chip, 1 - core], far.at[chip], {"dp": d ^ 1}) for chip in range(8)], csend, crecv
        )
        cores.start()
        for load in loads[2:]:
            load.wait()
        out_x.wait()
        routed = Routed(xs, us, w, router_ref, own_ref[:, 0:1], acc, dgu, unit, slope, router_grad_ref)
        routed.start()

        routed.forward()
        out_u.wait()
        send_out[...] = acc[0:n_rows].astype(bf16).reshape(GROUPS, slots, width)
        in_out.start()
        routed.backward()
        send_d[...] = acc[n_rows : 2 * n_rows].astype(bf16).reshape(GROUPS, slots, width)
        in_d.start()

        def block(j, carry):
            cols = pl.ds(pl.multiple_of(j * 256, 256), 256)
            x, up = xs[:, :, cols].reshape(n_rows, 256), us[:, :, cols].reshape(n_rows, 256)
            acc[0 : 2 * units, cols] = mm(dgu[0], x)
            acc[2 * units : 3 * units, cols] = mm(unit[0], up)
            for i in range(1, GROUPS):
                at = 3 * units * (i - 1)
                weights[at : at + 2 * units, cols] = mm(dgu[i], x).astype(bf16)
                weights[at + 2 * units : at + 3 * units, cols] = mm(unit[i], up).astype(bf16)
            return carry

        lax.fori_loop(0, width // 256, block, 0)
        stores = [pltpu.make_async_copy(acc.at[pl.ds(0, 3 * units)], mine_ref, stored.at[0])] + [
            pltpu.make_async_copy(weights.at[pl.ds(3 * units * i, 3 * units)], ref, stored.at[i + 1])
            for i, ref in enumerate(sent_refs)
        ]
        for store in stores:
            store.start()
        for chip in range(8):
            cores.copies[chip].wait_recv()
            far[chip] = (far[chip].astype(f32) + grads[chip, core].astype(f32)).astype(bf16)
            stores.append(pltpu.make_async_copy(far.at[chip], by_z_ref.at[chip], stored.at[4 + chip]))
            stores[-1].start()
        for copy in cores.copies:
            copy.wait_send()
        in_out.wait()
        in_d.wait()
        for store in stores:
            store.wait()

    row = struct((GROUPS, slots, width), bf16)
    return pl.pallas_call(
        kernel,
        out_shape=(
            row,
            row,
            struct((tok, width), f32),
            struct((tok, width), f32),
            struct((8, 3 * hidden, 128), bf16),
            struct((1, width), f32),
            struct((router.shape[0], width), f32),
            struct((3 * units, width), f32),
        )
        + (struct((3 * units, width), bf16),) * 3,
        in_specs=[HBM] * 7 + [VMEM] * 6,
        out_specs=(HBM, HBM, VMEM, VMEM, HBM, VMEM, VMEM) + (HBM,) * 4,
        scratch_shapes=[
            pltpu.VMEM((3 * hidden, width), bf16),
            pltpu.VMEM((tok, width), bf16),
            pltpu.VMEM((8, 2, 3 * hidden, 128), bf16),
            pltpu.VMEM(row.shape, bf16),
            pltpu.VMEM(row.shape, bf16),
            pltpu.VMEM((GROUPS, 3 * units, width), bf16),
            pltpu.VMEM((2 * n_rows, width), f32),
            pltpu.VMEM((GROUPS, 2 * units, n_rows), bf16),
            pltpu.VMEM((GROUPS, units, n_rows), bf16),
            pltpu.VMEM((GROUPS, 2, units, n_rows), bf16),
            pltpu.VMEM((8, 3 * hidden, 128), bf16),
            pltpu.VMEM(row.shape, bf16),
            pltpu.VMEM(row.shape, bf16),
        ]
        + ROW_SEMS * 4
        + sems(8, 8, 7, 12),
        compiler_params=comm_params(number, 61 * 1024 * 1024),
        name="experts",
        cost_estimate=cost(115),
    )(below, above, far_rows, in_rows, out_rows, w_in, w_out, places, tokens, upstream, vec, router, own)


def backward(
    part, moe_part, cotangent, middle, gain, out_weight, heads, q, keys, values, wide, logs, lengths, weights, sent, number
):
    _, rows, width = part.shape
    tok, size = q.shape[1:]
    stream, count = N_DP * tok, 2 * tok
    scale = size ** (-0.5)
    factor = scale * math.log2(math.e)
    n_sent, n_hidden = sent[0].shape[0], weights.shape[2] // 3
    half, rest = pl.ds(0, HALF), pl.ds(HALF, n_sent - HALF)
    now, later = pl.ds(0, NOW), pl.ds(NOW, n_sent - NOW)

    def kernel(*refs):
        (part_ref, moe_ref, up_in_ref, middle_ref, gain_ref, w_ref, heads_ref, q_ref, k_ref, v_ref), refs = (
            refs[:10],
            refs[10:],
        )
        (wide_ref, log_ref, lengths_ref, by_z_ref, one_up, two_up, one_down), refs = refs[:7], refs[7:]
        (d_middle_ref, stats_ref, sums_ref, pair_ref, out_ref, shared_in_ref, shared_out_ref), refs = refs[:7], refs[7:]
        (full_ref, below_ref, above_ref, up_ref, down_ref), refs = refs[:5], refs[5:]
        (full, d_attn, out_slice, d_heads, d_pair, made, got, d_query, out_part, out_got), refs = refs[:10], refs[10:]
        (z_got, by_x, x_got, up, down, far), refs = refs[:6], refs[6:]
        direct, refs = refs[:N_DIRECT], refs[N_DIRECT:]
        moe_scratch, refs = refs[:5], refs[5:]
        send, recv, osend, orecv, small_send, small_recv, fsend, frecv, wsend, wrecv, loaded = refs[:11]
        zsend, zrecv, gather_sems = refs[11], refs[12], refs[13:]
        me, z, _, _ = coordinates()
        t = lax.axis_index("tensor")
        core, x_index = lax.rem(me, 2), lax.rem(me // 2, 2)
        greet(dp_peers() + tensor_peers())
        scatter, gather = direct_parts(part_ref, full, direct)
        scatter.start()
        scatter_moe = Scatter(moe_ref, *moe_scratch)
        scatter_moe.start()
        over_z = Sends(
            [(by_z_ref.at[z ^ k], z_got.at[k], {"dp": me ^ (4 * k)}) for k in (1, 3, 2)], zsend, zrecv
        )
        over_z.start()
        loads = [
            pltpu.make_async_copy(one_up, up, loaded.at[0]),
            pltpu.make_async_copy(one_down, down, loaded.at[1]),
            pltpu.make_async_copy(by_z_ref.at[z], z_got.at[0], loaded.at[2]),
        ]
        for load in loads:
            load.start()
        middle = middle_ref[...]
        inv = second_moment(middle)
        d_normed = scatter.total()
        scaled = d_normed * gain_ref[...]
        d_middle = (
            up_in_ref[t].astype(f32)
            + inv * scaled
            - middle * (inv * inv * inv) * jnp.mean(scaled * middle, axis=1, keepdims=True)
        )
        gather.start(d_middle)
        first = Sends(
            [
                (two_up.at[half], far.at[half], along_y(1)),
                (two_up.at[rest], far.at[rest], along_y(3)),
            ],
            fsend,
            frecv,
        )
        first.start()
        d_middle_ref[...] = d_middle
        stats_ref[0:1] = column_sum(d_normed * middle * inv)
        scatter_moe.middle()
        gather.wait()
        d_attn[...] = full[...].astype(f32).reshape(tok, width).astype(bf16)
        value = mm(d_attn[...], w_ref[...], NT).astype(bf16)
        d_heads[0] = value[:, 0:size]
        d_heads[1] = value[:, size : 2 * size]
        swap = remote(
            d_heads.at[1 - core], d_pair.at[core], small_send.at[1], small_recv.at[1], {"dp": me ^ 1}
        )
        swap.start()
        d_pair[core] = d_heads[core]
        for d in range(N_DP):
            out_part[d] = mm(d_attn[:, d * 128 : (d + 1) * 128], heads_ref[...], TN).astype(bf16)
        outs = [
            remote(out_part.at[me ^ k], out_got.at[k], osend.at[k], orecv.at[k], {"dp": me ^ k})
            for k in range(1, N_DP)
        ]
        for copy in outs:
            copy.start()
        moe_out = scatter_moe.total()
        output = middle_ref[...] + moe_out
        gather_out = Gather(out_slice, full_ref, *gather_sems)
        gather_out.start(output)
        stats_ref[1:2] = column_sum(moe_out * moe_out)
        stats_ref[2:3] = column_sum(output * output)

        swap.wait_recv()
        q, d_out = q_ref[...].reshape(count, size), d_pair[...].reshape(count, size)
        lowest, highest = codes_of_queries(me // 2, count, lengths_ref)
        log = log_ref[0:1]
        delta = jnp.sum((wide_ref[...] * d_out.astype(f32)).T, axis=0, keepdims=True)

        def send_to(step):
            return remote(
                made.at[me ^ step], got.at[step], send.at[step], recv.at[step], {"dp": me ^ step}
            )

        def block(group, acc):
            at = pl.ds(pl.multiple_of(group * tok, tok), tok)
            k = k_ref[at]
            scores = mm(k, q, NT) * factor
            code = codes_of_keys(group, tok, lengths_ref)
            seen = (code >= lowest) & (code <= highest)
            probs = jnp.where(seen, jnp.exp2(scores - log), 0.0)
            d_probs = mm(v_ref[at], d_out, NT)
            d_scores = (probs * (d_probs - delta)).astype(bf16)
            made[group, 0:tok] = (mm(d_scores, q) * scale).astype(bf16)
            made[group, tok : 2 * tok] = mm(probs.astype(bf16), d_out).astype(bf16)
            return acc + mm(k, d_scores, TN)

        def other(step, acc):
            acc = block(me ^ step, acc)
            send_to(step).start()
            return acc

        acc = lax.fori_loop(1, N_DP, other, jnp.zeros((size, count), f32))
        gather_out.relay()
        acc = block(me, acc)
        d_query[...] = (acc.T * scale).astype(bf16).reshape(2, tok, size)
        back = remote(
            d_query.at[1 - core], pair_ref.at[core], small_send.at[2], small_recv.at[2], {"dp": me ^ 1}
        )
        back.start()
        pair_ref[core] = d_query[core]

        loads[2].wait()
        over_z.wait()
        for side in range(2):
            total = z_got[0, side].astype(f32)
            for k in (1, 2, 3):
                total = total + z_got[k, side].astype(f32)
            by_x[side] = total.astype(bf16)
        along_x = remote(
            by_x.at[1 - x_index], x_got, small_send.at[0], small_recv.at[0], {"dp": me ^ 2}
        )
        along_x.start()

        for load in loads[:2]:
            load.wait()
        for copy in first.copies:
            copy.wait_recv()

        def add(rows, target):
            def step(j, carry):
                cols = pl.ds(pl.multiple_of(j * 512, 512), 512)
                target[rows, cols] = (target[rows, cols].astype(f32) + far[rows, cols].astype(f32)).astype(bf16)
                return carry

            lax.fori_loop(0, width // 512, step, 0)

        add(half, up)
        add(rest, down)
        second = Sends(
            [(up.at[now], below_ref, along_y(1)), (down.at[now], above_ref, along_y(3))], wsend, wrecv
        )
        second.start()
        stores = [
            pltpu.make_async_copy(up.at[later], up_ref, loaded.at[3]),
            pltpu.make_async_copy(down.at[later], down_ref, loaded.at[4]),
        ]
        for store in stores:
            store.start()
        got[0] = made[me]
        for k in range(1, N_DP):
            send_to(k).wait_recv()
        for head in range(2):
            total = jnp.zeros((2 * tok, size), f32)
            for k in range(N_DP // 2):
                total = total + got[2 * k + (core + head) % 2].astype(f32)
            sums_ref[head] = total
        total = out_part[me].astype(f32)
        for k, copy in enumerate(outs):
            copy.wait_recv()
            total = total + out_got[k + 1].astype(f32)
        out_ref[...] = total
        along_x.wait_recv()
        total = by_x[x_index].astype(f32) + x_got[...].astype(f32)
        shared_in_ref[...] = total[0 : 2 * n_hidden]
        shared_out_ref[...] = total[2 * n_hidden :]
        back.wait_recv()
        for copy in [along_x, swap, back] + outs + first.copies:
            copy.wait_send()
        scatter.wait_send()
        scatter_moe.wait_send()
        for store in stores:
            store.wait()
        gather_out.wait()
        second.wait()
        for k in range(1, N_DP):
            send_to(k).wait_send()

    return pl.pallas_call(
        kernel,
        out_shape=(
            struct((rows, width), f32),
            struct((8, width), f32),
            struct((2, 2 * tok, size), f32),
            struct(q.shape, bf16),
            struct((width // N_DP, 2 * size), f32),
            struct((2 * n_hidden, 128), f32),
            struct((n_hidden, 128), f32),
            struct(part.shape, bf16),
            struct((NOW, width), bf16),
            struct((NOW, width), bf16),
            struct((n_sent - NOW, width), bf16),
            struct((n_sent - NOW, width), bf16),
        ),
        in_specs=[VMEM] * 12 + [SMEM] + [HBM] * 4,
        out_specs=(VMEM,) * 7 + (HBM,) * 5,
        scratch_shapes=[
            pltpu.VMEM(part.shape, bf16),
            pltpu.VMEM((tok, width), bf16),
            pltpu.VMEM((rows, width), bf16),
            pltpu.VMEM(q.shape, bf16),
            pltpu.VMEM(q.shape, bf16),
            pltpu.VMEM((N_DP, 2 * tok, size), bf16),
            pltpu.VMEM((N_DP, 2 * tok, size), bf16),
            pltpu.VMEM(q.shape, bf16),
            pltpu.VMEM((N_DP, 128, 2 * size), bf16),
            pltpu.VMEM((N_DP, 128, 2 * size), bf16),
            pltpu.VMEM(weights.shape, bf16),
            pltpu.VMEM(weights.shape[1:], bf16),
            pltpu.VMEM(weights.shape[2:], bf16),
        ]
        + [pltpu.VMEM((n_sent, width), bf16)] * 3
        + direct_scratch(rows, width)
        + [pltpu.VMEM((2, 4, rows, width), bf16)]
        + [pltpu.VMEM((rows, width), bf16)] * 2
        + sems((2, 4), (2, 4))
        + sems(N_DP, N_DP, N_DP, N_DP, 3, 3, 2, 2, 2, 2, 5, 3, 3, (2, 4), (2, 4), 1),
        compiler_params=comm_params(number, LIMIT),
        name="backward",
        cost_estimate=cost(110),
    )(
        part, moe_part, cotangent, middle, gain, out_weight, heads, q, keys, values, wide, logs, lengths, weights, *sent
    )


def join_tail(part, layer_input, d_middle, gain, normed, d_proj, smalls, own_grads, received, waiting, number):
    _, rows, width = part.shape
    small = 32
    wide = d_proj.shape[1]
    n_in, n_out = 13 + len(received), 6
    n_expert = own_grads.shape[0]
    n_late = n_expert - NOW - SOON
    first = pl.ds(0, NOW)
    parts = ((0, SOON), (SOON, n_late))
    units = n_expert // 3

    def kernel(*refs):
        part_ref, x_ref, d_ref, gain_ref, n_ref, proj_ref = refs[:6]
        router_ref, vec_ref, one_stats, two_stats, own_grads_ref = refs[6:11]
        received_refs, (up_ref, down_ref) = refs[11 : n_in - 2], refs[n_in - 2 : n_in]
        grad_ref, qkv_ref, one_ref, both_ref, in_ref, out_ref = refs[n_in : n_in + n_out]
        scratch = refs[n_in + n_out :]
        join, scratch = scratch[:N_DIRECT], scratch[N_DIRECT:]
        own, few, summed, more, send, recv, tsend, trecv = scratch[:8]
        qbuf, qgot, qsum, qin, csend, crecv, ksend, krecv = scratch[8:16]
        acc, others, lsem, osem, esend, erecv, full = scratch[16:]
        me, t = lax.axis_index("dp"), lax.axis_index("tensor")
        core, chip = me % 2, me // 2
        greet(tensor_peers() + dp_peers())
        got, mine, jsend, jrecv, asend, arecv, alocal = join
        scatter = DirectScatter(part_ref, got, jsend, jrecv)
        gather = YGather(mine, full, asend, arecv, alocal)
        scatter.start()
        rest = Sends(
            [
                (ref.at[pl.ds(at, n)], others.at[i, pl.ds(NOW + at, n)], along_y(shift))
                for at, n in parts
                for i, (ref, shift) in enumerate(((up_ref, 1), (down_ref, 3)))
            ],
            esend,
            erecv,
        )
        for copy in rest.copies[:2]:
            copy.start()
        loads = [pltpu.make_async_copy(own_grads_ref, acc, lsem.at[0])] + [
            pltpu.make_async_copy(r, others.at[i, first], lsem.at[i + 1])
            for i, r in enumerate(received_refs)
        ]
        for load in loads:
            load.start()
        across = []
        for c in range(8):
            for side in range(2):
                cols = slice((2 * c + side) * 128, (2 * c + side + 1) * 128)
                qbuf[c, side] = mm(n_ref[:, cols], proj_ref[...], TN).astype(bf16)
            across.append(
                remote(qbuf.at[c, 1 - core], qgot.at[c], csend.at[c], crecv.at[c], {"dp": me ^ 1})
            )
            across[-1].start()
        for c in range(8):
            across[c].wait_recv()
            qsum[c] = (qbuf[c, core].astype(f32) + qgot[c].astype(f32)).astype(bf16)
        chips = [
            remote(
                qsum.at[chip ^ k], qin.at[k], ksend.at[k], krecv.at[k], {"dp": me ^ (2 * k)}
            )
            for k in range(1, 8)
        ]
        for copy in chips:
            copy.start()
        bias = column_sum(proj_ref[...].astype(f32))
        stats = [one_stats[k : k + 1] for k in range(3)] + [two_stats[k : k + 1] for k in (1, 2)]
        rows_all = [sum(row[:, i * 128 : (i + 1) * 128] for i in range(N_DP)) for row in stats] + [
            bias[:, i * 128 : (i + 1) * 128] for i in range(wide // 128)
        ]
        for i in range(N_DP):
            cols = slice(i * 128, (i + 1) * 128)
            own[i, 0:16] = router_ref[:, cols]
            own[i, 16:17] = vec_ref[:, cols]
            own[i, 17:18] = two_stats[0:1, cols]
            for k, row in enumerate(rows_all):
                own[i, 19 + k : 20 + k] = row
            own[i, 19 + len(rows_all) : small] = jnp.zeros((small - 19 - len(rows_all), 128), f32)
        resid = x_ref[t].astype(f32)
        inv = second_moment(resid)
        d_normed = scatter.total()
        scaled = d_normed * gain_ref[...]
        mine[...] = (
            d_ref[...]
            + inv * scaled
            - resid * (inv * inv * inv) * jnp.mean(scaled * resid, axis=1, keepdims=True)
        ).astype(bf16)
        gather.start()
        gain_grad = column_sum(d_normed * resid * inv)
        for i in range(N_DP):
            own[i, 18:19] = gain_grad[:, i * 128 : (i + 1) * 128]
        firsts = [
            remote(own.at[me ^ k], few.at[k], send.at[k], recv.at[k], {"dp": me ^ k})
            for k in range(1, N_DP)
        ]
        for copy in firsts:
            copy.start()
        for copy in rest.copies[2:]:
            copy.start()
        value = own[me]
        for k in range(1, N_DP):
            firsts[k - 1].wait_recv()
            value = value + few[k]
        one_ref[...] = value
        summed[...] = value
        seconds = [
            remote(summed, more.at[k], tsend.at[k], trecv.at[k], {"tensor": t ^ k}) for k in range(1, N_T)
        ]
        for copy in seconds:
            copy.start()
        gather.relay()
        for load in loads:
            load.wait()
        for copy in rest.copies:
            copy.wait_recv()

        def add(j, carry):
            cols = pl.ds(pl.multiple_of(j * 256, 256), 256)
            total = acc[:, cols]
            for i in range(len(received)):
                total = total + others[i, :, cols].astype(f32)
            acc[:, cols] = total
            return carry

        lax.fori_loop(0, width // 256, add, 0)
        stores = [
            pltpu.make_async_copy(acc.at[pl.ds(0, 2 * units)], in_ref, osem.at[0]),
            pltpu.make_async_copy(acc.at[pl.ds(2 * units, units)], out_ref, osem.at[1]),
        ]
        for store in stores:
            store.start()
        total = qsum[chip].astype(f32)
        for k in range(1, 8):
            chips[k - 1].wait_recv()
            total = total + qin[k].astype(f32)
        qkv_ref[...] = total
        for k in range(1, N_T):
            seconds[k - 1].wait_recv()
            value = value + more[k]
        both_ref[...] = value
        for copy in firsts + seconds + across + chips + rest.copies:
            copy.wait_send()
        scatter.wait_send()
        gather.wait()
        grad_ref[...] = full[...].astype(f32)
        for store in stores:
            store.wait()

    return pl.pallas_call(
        kernel,
        out_shape=(
            struct(part.shape, f32),
            struct((width // N_DP, wide), f32),
            struct((small, 128), f32),
            struct((small, 128), f32),
            struct((2 * units, width), f32),
            struct((units, width), f32),
        ),
        in_specs=[VMEM] * 10 + [HBM] * (n_in - 10),
        out_specs=(VMEM,) * 4 + (HBM,) * 2,
        scratch_shapes=[
            pltpu.VMEM(part.shape, bf16),
            pltpu.VMEM((rows, width), bf16),
        ]
        + sems(N_T, N_T, (2, 4), (2, 4), 1)
        + [
            pltpu.VMEM((N_DP, small, 128), f32),
            pltpu.VMEM((N_DP, small, 128), f32),
            pltpu.VMEM((small, 128), f32),
            pltpu.VMEM((N_T, small, 128), f32),
        ]
        + sems(N_DP, N_DP, N_T, N_T)
        + [
            pltpu.VMEM((8, 2, 128, wide), bf16),
            pltpu.VMEM((8, 128, wide), bf16),
            pltpu.VMEM((8, 128, wide), bf16),
            pltpu.VMEM((8, 128, wide), bf16),
        ]
        + sems(8, 8, 8, 8)
        + [
            pltpu.VMEM((n_expert, width), f32),
            pltpu.VMEM((len(received), n_expert, width), bf16),
        ]
        + sems(1 + len(received), 2, 4, 4)
        + [pltpu.VMEM(part.shape, bf16)],
        compiler_params=comm_params(number, LIMIT),
        name="join_tail",
        cost_estimate=cost(55),
    )(part, layer_input, d_middle, gain, normed, d_proj, *smalls, own_grads, *received, *waiting)


def doc_layout(lengths, token_index):
    doc_ends = jnp.cumsum(lengths)
    starts = doc_ends - lengths
    seq_ids = jnp.sum((token_index[:, None] >= doc_ends[None, :]).astype(jnp.int32), axis=1)
    member = seq_ids[:, None] == jnp.arange(lengths.shape[0], dtype=jnp.int32)[None, :]
    begins = jnp.sum(jnp.where(member, starts[None, :], 0), axis=1)
    offsets = token_index - begins
    return (seq_ids, offsets, offsets // DBLOCK)


def rope_tables(offsets, head_dim):
    half_dim = head_dim // 2
    frequencies = jnp.exp(
        jnp.arange(half_dim, dtype=f32) * (-2.0 * math.log(THETA) / head_dim)
    )
    angles = offsets.astype(f32)[:, None] * frequencies[None, :]
    return (jnp.cos(angles)[:, None, :], jnp.sin(angles)[:, None, :])


def rotate(vectors, cosine, sine):
    half_dim = vectors.shape[-1] // 2
    front, back = vectors[..., :half_dim], vectors[..., half_dim:]
    return jnp.concatenate([front * cosine - back * sine, back * cosine + front * sine], axis=-1)


def dot(pattern, a, b):
    return jnp.einsum(pattern, a, b, preferred_element_type=f32)


def on_device(
    layer_input,
    doc_lengths,
    expert_ids,
    attn_gain,
    qkv_weight,
    qkv_bias,
    out_weight,
    ffn_gain,
    router_weight,
    shared_gate,
    shared_in,
    shared_out,
    expert_in,
    expert_out,
    cotangent,
):
    tok, width = layer_input.shape
    dp, tn = lax.axis_index("dp"), lax.axis_index("tensor")
    experts_n = router_weight.shape[1]
    head_dim = qkv_weight.shape[3]
    stream = tok * N_DP
    part_rows = tok // N_T
    score_scale = head_dim ** (-0.5)
    eff = expert_out.shape[1]

    in_rows = expert_in[0].transpose(1, 2, 0).reshape(2 * eff, width)

    hot = jnp.sum(
        (expert_ids[:, :, None] == jnp.arange(experts_n, dtype=jnp.int32)[None, None, :]).astype(f32),
        axis=1,
    )
    before = (jnp.arange(tok)[:, None] > jnp.arange(tok)[None, :]).astype(bf16)
    rank = dot("ts,se->te", before, hot.astype(bf16))
    place = jnp.where(hot > 0, rank, -1.0).astype(jnp.int32).T
    _, offset = route_plane()
    served = lax.dynamic_slice_in_dim(place, GROUPS * ((dp // 4) ^ offset), GROUPS, 0)
    places = (served[:, None, :] == jnp.arange(SLOTS, dtype=jnp.int32)[None, :, None]).astype(bf16)
    returned = lax.dynamic_index_in_dim(place.reshape(GROUPS, 4, tok), offset, 1, keepdims=False)
    places_back = (
        (returned[:, None, :] == jnp.arange(SLOTS, dtype=jnp.int32)[None, :, None])
        .astype(bf16)
        .reshape(GROUPS * SLOTS, tok)
    )

    local_index = dp * tok + jnp.arange(tok, dtype=jnp.int32)
    _, pos_local, _ = doc_layout(doc_lengths, local_index)
    cosine, sine = rope_tables(pos_local, head_dim)
    residual = layer_input.astype(f32)
    inv_first = lax.rsqrt(jnp.mean(residual * residual, axis=1, keepdims=True) + EPSILON)
    normed_one = (residual * inv_first * attn_gain).astype(bf16)
    projected = dot("td,dshe->tshe", normed_one, qkv_weight) + qkv_bias.astype(f32)[None]
    q_own = rotate(projected[:, 0], cosine, sine).astype(bf16).transpose(1, 0, 2)
    k_own = rotate(projected[:, 1], cosine, sine).astype(bf16).transpose(1, 0, 2)
    v_own = projected[:, 2].astype(bf16).transpose(1, 0, 2)
    by_slice = (N_T, part_rows, width)
    out_flat = out_weight.reshape(2 * head_dim, width)
    keys, values, queries, wide, logs, heads_out, normed_two, middle, stats_one, *neighbours = attend_forward(
        k_own,
        v_own,
        q_own,
        doc_lengths,
        out_flat,
        layer_input.reshape(by_slice),
        ffn_gain.reshape(1, width),
        [in_rows, expert_out[0]],
        1,
    )
    normed_two = normed_two.reshape(tok, width)

    own_expert = jnp.broadcast_to(
        (jnp.arange(experts_n, dtype=jnp.int32) == dp).astype(f32)[:, None], (experts_n, 128)
    )
    back_grads, back_out, mixed, shared_d_normed, got, gate_vec_part, router_part, own_grads, *sent = experts(
        places,
        *neighbours,
        in_rows,
        expert_out[0],
        normed_two,
        cotangent,
        shared_in.transpose(1, 2, 0).reshape(-1, width),
        shared_out,
        shared_gate.astype(f32).reshape(1, width),
        router_weight.T,
        own_expert,
        5,
    )

    by_z = got.reshape((4, 2) + got.shape[1:])

    def combine(rows):
        return dot("rt,rd->td", places_back, rows.reshape(-1, width))

    d_normed_part = (shared_d_normed + combine(back_grads)).astype(bf16)
    moe_part = (mixed + combine(back_out)).astype(bf16)
    d_middle, stats_two, d_keys, d_queries, outproj_grad, shared_in_grad, shared_out_grad, output, *moved = backward(
        d_normed_part.reshape(by_slice),
        moe_part.reshape(by_slice),
        cotangent.reshape(by_slice),
        middle,
        ffn_gain.reshape(1, width),
        out_flat,
        heads_out,
        queries,
        keys,
        values,
        wide,
        logs,
        doc_lengths,
        by_z,
        sent,
        7,
    )

    cosine, sine = cosine[:, 0], sine[:, 0]
    d_proj = jnp.concatenate(
        [rotate(d_queries[h].astype(f32), cosine, -sine) for h in range(2)]
        + [rotate(d_keys[h, :tok], cosine, -sine) for h in range(2)]
        + [d_keys[h, tok:] for h in range(2)],
        axis=1,
    ).astype(bf16)
    d_normed_one = dot(
        "tshe,dshe->td", d_proj.reshape(tok, 3, 2, head_dim), qkv_weight
    ).astype(bf16)
    input_grad, qkv_grad, over_dp, over_both, expert_in_grad, expert_out_grad = join_tail(
        d_normed_one.reshape(by_slice),
        layer_input.reshape(by_slice),
        d_middle,
        attn_gain.reshape(1, width),
        normed_one,
        d_proj,
        [router_part, gate_vec_part, stats_one, stats_two],
        own_grads,
        moved[:2],
        moved[2:],
        10,
    )
    bias_grad = lax.dynamic_slice_in_dim(over_dp[24:30], 8 * dp, 8, 1).reshape(3, 2, 8)
    rms_stats = jnp.sqrt(jnp.sum(over_both[19:24], axis=1) / (stream * width))

    return (
        output.reshape(tok, width),
        input_grad.reshape(tok, width),
        qkv_grad.reshape(width // N_DP, 3, 2, head_dim),
        bias_grad,
        outproj_grad.T.reshape(2, head_dim, width // N_DP),
        over_both[18],
        over_both[17],
        over_both[:16].T,
        over_both[16],
        shared_in_grad.reshape(2, shared_in.shape[2], -1).transpose(2, 0, 1),
        shared_out_grad,
        expert_in_grad.reshape(2, eff, width).transpose(2, 0, 1)[None],
        expert_out_grad[None],
        rms_stats,
    )


def solution(mesh):
    in_specs = (
        P("dp", None),
        P(),
        P("dp", None),
        P(),
        P(None, None, "tensor", None),
        P(None, "tensor", None),
        P("tensor", None, None),
        P(),
        P(),
        P(),
        P(None, None, "tensor"),
        P("tensor", None),
        P("dp", None, None, "tensor"),
        P("dp", "tensor", None),
        P("dp", None),
    )
    out_specs = (
        P("dp", None),
        P("dp", None),
        P("dp", None, "tensor", None),
        P(None, "tensor", "dp"),
        P("tensor", None, "dp"),
        P("dp"),
        P("dp"),
        P("dp", None),
        P("dp"),
        P("dp", None, "tensor"),
        P("tensor", "dp"),
        P("dp", None, None, "tensor"),
        P("dp", "tensor", None),
        P(),
    )
    return jax.shard_map(
        on_device, mesh=mesh, in_specs=in_specs, out_specs=out_specs, check_vma=False
    )
```
